32 devices in a mesh: dp: 4 (over x, core), fsdp: 8 (over z, y).
Axes of the slice: x: 2, y: 2, z: 4, core: 2. Of those that a mesh axis runs over, the one named last changes fastest.
Arguments:
- query: bfloat16 [32768, 768], P(('dp', 'fsdp')), may hold values from -6 to 6
- memory: bfloat16 [32768, 768], P(('dp', 'fsdp')), may hold values from -6 to 6
- query_seg: int32 [32768], P(('dp', 'fsdp')), may hold values from 0 to 127, as said below
- memory_seg: int32 [32768], P(('dp', 'fsdp')), may hold values from 0 to 127, as said below
- attn_proj: bfloat16 [6, 768, 768], P(None, ('dp', 'fsdp')), may hold values from -0.21875 to 0.21875
- attn_out: bfloat16 [2, 768, 768], P(None, ('dp', 'fsdp')), may hold values from -3.5 to 3.5
- attn_bias: bfloat16 [6, 768], P(None, ('dp', 'fsdp')), may hold values from -3 to 3
- norm_gain: bfloat16 [3, 768], P(None, ('dp', 'fsdp')), may hold values from 0.25 to 1.75
- norm_bias: bfloat16 [3, 768], P(None, ('dp', 'fsdp')), may hold values from -2 to 2
- ffn_in: bfloat16 [768, 3072], P(('dp', 'fsdp')), may hold values from -0.21875 to 0.21875
- ffn_in_bias: bfloat16 [3072], P(('dp', 'fsdp')), may hold values from -3 to 3
- ffn_out: bfloat16 [3072, 768], P(('dp', 'fsdp')), may hold values from -0.109375 to 0.109375
- ffn_out_bias: bfloat16 [768], P(('dp', 'fsdp')), may hold values from -2 to 2
- cotangent: bfloat16 [32768, 768], P(('dp', 'fsdp')), may hold values from -6 to 6
Outputs:
- mixed: bfloat16 [32768, 768], P(('dp', 'fsdp'))
- query_grad: float32 [32768, 768], P(('dp', 'fsdp'))
- memory_grad: float32 [32768, 768], P(('dp', 'fsdp'))
- attn_proj_grad: float32 [6, 768, 768], P(None, ('dp', 'fsdp'))
- attn_out_grad: float32 [2, 768, 768], P(None, ('dp', 'fsdp'))
- attn_bias_grad: float32 [6, 768], P(None, ('dp', 'fsdp'))
- norm_gain_grad: float32 [3, 768], P(None, ('dp', 'fsdp'))
- norm_bias_grad: float32 [3, 768], P(None, ('dp', 'fsdp'))
- ffn_in_grad: float32 [768, 3072], P(('dp', 'fsdp'))
- ffn_in_bias_grad: float32 [3072], P(('dp', 'fsdp'))
- ffn_out_grad: float32 [3072, 768], P(('dp', 'fsdp'))
- ffn_out_bias_grad: float32 [768], P(('dp', 'fsdp'))
The draws below stay inside these ranges and needn't reach their ends.
Inputs may be any that keep to these rules, and one draw needn't show every extreme that they name: `query_seg`: every aligned block of 512 query rows holds whole sequences, and the memory rows of the same block hold the same sequence numbers: block b carries either the single number b * 2 or the numbers b * 2 to b * 2 + 1 in rising runs, each run nonempty; the first block holds one sequence, the last holds 2. `memory_seg`: laid out as query_seg, block by block, with the same numbers in each block as query_seg and runs of their own lengths.
All inputs are finite; a program needn't handle non-finite values.
Results may differ from the reference program's by a relative error of at most 0.023.
Values may be sent and summed in bfloat16 or wider, within the bound.
No kernel may reach another device: no remote copies, remote signals or barrier semaphores. Data moves between devices by JAX's collectives and lax.ppermute only.
A program may use at most 256 MiB of HBM per device.

```python
import jax
import jax.numpy as jnp
from jax import lax

D = 768
FF = 3072
HEADS = 12
HEAD_DIM = 64
SEQ_MAX = 512
SEQS_BLK = 2
QTOK = 32768
MTOK = 32768


def single_blocks(key, rows):
    blocks = rows // SEQ_MAX
    single = jax.random.randint(jax.random.fold_in(key, 11), (blocks,), 0, 2)
    single = single.at[0].set(1)
    single = single.at[blocks - 1].set(0)
    return single


def block_segments(key, single, rows):
    blocks = rows // SEQ_MAX
    block_keys = jax.random.split(key, blocks)

    def one_block(block_key):
        order = jax.random.permutation(block_key, SEQ_MAX - 1) + 1
        return order[:SEQS_BLK - 1]
    cuts = jax.vmap(one_block)(block_keys)
    position = jnp.arange(SEQ_MAX, dtype=jnp.int32)
    local = jnp.sum((position[None, :, None] >= cuts[:, None, :]).astype(jnp.int32), axis=-1)
    local = local * (1 - single[:, None])
    numbers = jnp.arange(blocks, dtype=jnp.int32)[:, None] * SEQS_BLK + local
    return numbers.reshape(rows).astype(jnp.int32)


def draw_query_seg(key, part):
    single = single_blocks(key, QTOK)
    key = jax.random.fold_in(key, 1)
    return block_segments(key, single, QTOK)


def draw_memory_seg(key, part):
    single = single_blocks(key, MTOK)
    key = jax.random.fold_in(key, 2)
    return block_segments(key, single, MTOK)


def shard_levels(key, dims, shards, smallest, top_value):
    def one(dim, parts):
        heights = jax.random.uniform(jax.random.fold_in(jax.random.fold_in(key, 6), dim), (parts,), jnp.float32, smallest / len(shards), top_value / len(shards))
        return jnp.repeat(jnp.exp(heights), dims[dim] // parts).reshape((-1,) + (1,) * (len(dims) - dim - 1))

    loudness = one(*shards[0])
    for cut in shards[1:]:
        loudness = loudness * one(*cut)
    return loudness


def gaussian(key, dims, deviation, reach, cuts=(), kind=jnp.bfloat16):
    loudness = shard_levels(key, dims, cuts, -0.22, 0.18) if cuts else 1.0
    values = jax.random.normal(key, dims, jnp.float32) * deviation * loudness
    return jnp.minimum(jnp.maximum(values, -reach), reach).astype(kind)


def setup_inputs(seed: int = 0) -> dict:
    key_list = jax.random.split(jax.random.key(seed), 15)
    query = gaussian(key_list[0], (QTOK, D), 1.0, 6.0, ((0, 32),))
    memory = gaussian(key_list[1], (MTOK, D), 1.0, 6.0, ((0, 32),))
    query_seg = draw_query_seg(jax.random.fold_in(key_list[14], 71), 0)
    memory_seg = draw_memory_seg(jax.random.fold_in(key_list[14], 71), 0)
    attn_proj = gaussian(key_list[4], (6, D, D), D ** -0.5, 0.21875, ((1, 32),))
    attn_out = gaussian(key_list[5], (2, D, D), (max(D // 256, 2)) ** -0.5, 3.5, ((1, 32),))
    attn_bias = gaussian(key_list[6], (6, D), 0.5, 3.0, ((1, 32),))
    norm_gain = jnp.clip(1.0 + 0.15 * jax.random.normal(key_list[7], (3, D), jnp.float32), 0.25, 1.75).astype(jnp.bfloat16)
    norm_bias = gaussian(key_list[8], (3, D), 0.3, 2.0, ((1, 32),))
    ffn_in = gaussian(key_list[9], (D, FF), D ** -0.5, 0.21875, ((0, 32),))
    ffn_in_bias = gaussian(key_list[10], (FF,), 0.5, 3.0, ((0, 32),))
    ffn_out = gaussian(key_list[11], (FF, D), FF ** -0.5, 0.109375, ((0, 32),))
    ffn_out_bias = gaussian(key_list[12], (D,), 0.3, 2.0, ((0, 32),))
    cotangent = gaussian(key_list[13], (QTOK, D), 1.0, 6.0, ((0, 32),))
    return {"query": query, "memory": memory, "query_seg": query_seg, "memory_seg": memory_seg, "attn_proj": attn_proj, "attn_out": attn_out, "attn_bias": attn_bias, "norm_gain": norm_gain, "norm_bias": norm_bias, "ffn_in": ffn_in, "ffn_in_bias": ffn_in_bias, "ffn_out": ffn_out, "ffn_out_bias": ffn_out_bias, "cotangent": cotangent}


EPSILON = 1e-05
NEG_FILL = -1e+30
HIGH = lax.Precision.HIGHEST

@jax.custom_vjp
def low(v):
    return lax.optimization_barrier(v.astype(jnp.bfloat16)).astype(jnp.float32)

@jax.custom_vjp
def low_back(v):
    return v

def low_keep(v):
    return (low(v), None)

def low_pass(kept, grad):
    return (grad,)

def back_keep(v):
    return (v, None)

def back_low(kept, grad):
    return (low(grad),)
low.defvjp(low_keep, low_pass)
low_back.defvjp(back_keep, back_low)

def both_ways(value):
    return low_back(low(value))

def layer_norm(resid, gain, shift):
    center = resid - lax.optimization_barrier(jnp.mean(resid, axis=-1, keepdims=True))
    spread = lax.optimization_barrier(jnp.mean(center * center, axis=-1, keepdims=True))
    return center * lax.rsqrt(spread + EPSILON) * gain + shift

def project(left, right):
    return jnp.dot(left, right, precision=HIGH)

def attend(queries, keys, values, query_ids, key_ids):
    blocks = queries.shape[0] // SEQ_MAX
    shape = (blocks, SEQ_MAX, HEADS, HEAD_DIM)
    scores = jnp.einsum('bqhd,bkhd->bhqk', queries.reshape(shape), keys.reshape(shape), precision=HIGH)
    scores = low_back(scores * HEAD_DIM ** (-0.5))
    same = query_ids.reshape(blocks, 1, SEQ_MAX, 1) == key_ids.reshape(blocks, 1, 1, SEQ_MAX)
    scores = jnp.where(same, scores, NEG_FILL)
    peak = lax.optimization_barrier(jnp.max(scores, axis=-1, keepdims=True))
    weights = jnp.exp(scores - peak)
    attention = low(weights / lax.optimization_barrier(jnp.sum(weights, axis=-1, keepdims=True)))
    result = jnp.einsum('bhqk,bkhd->bqhd', attention, values.reshape(shape), precision=HIGH)
    return both_ways(result.reshape(queries.shape))

def layer_group(params, items):
    projections, out_weights, biases, gains, shifts, in_weights, in_bias, out_ffn, out_bias = params
    query, memory, query_ids, memory_ids = items
    self_queries = both_ways(project(query, projections[0]) + biases[0])
    self_keys = both_ways(project(query, projections[1]))
    self_values = both_ways(project(query, projections[2]) + biases[1])
    self_mixed = attend(self_queries, self_keys, self_values, query_ids, query_ids)
    first_sum = query + low_back(project(self_mixed, out_weights[0]) + biases[2])
    first = layer_norm(first_sum, gains[0], shifts[0])
    cross_queries = both_ways(project(low(first), projections[3]) + biases[3])
    cross_keys = both_ways(project(memory, projections[4]))
    cross_values = both_ways(project(memory, projections[5]) + biases[4])
    cross_mixed = attend(cross_queries, cross_keys, cross_values, query_ids, memory_ids)
    second_sum = first + low_back(project(cross_mixed, out_weights[1]) + biases[5])
    second = layer_norm(second_sum, gains[1], shifts[1])
    hidden_pre = low_back(project(low(second), in_weights) + in_bias)
    hidden = low(jax.nn.gelu(hidden_pre, approximate=False))
    third_sum = second + low_back(project(hidden, out_ffn) + out_bias)
    return layer_norm(third_sum, gains[2], shifts[2])

def forward(floats, query_seg, memory_seg):
    query, memory = (floats[0], floats[1])
    params = tuple(floats[2:])
    groups = QTOK // (8 * SEQ_MAX)
    items = (query.reshape(groups, -1, D), memory.reshape(groups, -1, D), query_seg.reshape(groups, -1), memory_seg.reshape(groups, -1))
    checked = jax.checkpoint(layer_group)
    result = lax.map(lambda group_items: checked(params, group_items), items)
    return result.reshape(QTOK, D)

def reference(query, memory, query_seg, memory_seg, attn_proj, attn_out, attn_bias, norm_gain, norm_bias, ffn_in, ffn_in_bias, ffn_out, ffn_out_bias, cotangent):
    floats = tuple((array.astype(jnp.float32) for array in (query, memory, attn_proj, attn_out, attn_bias, norm_gain, norm_bias, ffn_in, ffn_in_bias, ffn_out, ffn_out_bias)))

    def apply(*values):
        return forward(values, query_seg, memory_seg)
    output, pull = jax.vjp(apply, *floats)
    grads = pull(cotangent.astype(jnp.float32))
    return (output.astype(jnp.bfloat16), grads[0], grads[1], grads[2], grads[3], grads[4], grads[5], grads[6], grads[7], grads[8], grads[9], grads[10])
```

```python
import functools

import jax
import jax.numpy as jnp
from jax import lax
from jax.experimental import pallas as pl
from jax.experimental.pallas import tpu as pltpu
from jax.sharding import PartitionSpec as P

HEADS = 12
HEAD_DIM = 64
SEQ_MAX = 512
PAIRS = HEADS // 2
EPSILON = 1e-05
MASKED = 1e30
SCALE = HEAD_DIM ** (-0.5)
BF = jnp.bfloat16
F32 = jnp.float32
VMEM_LIMIT = 60 * 1024 * 1024


def dot(left, right):
    return jnp.dot(left, right, preferred_element_type=F32)


def dot_nt(left, right):
    return lax.dot_general(left, right, (((1,), (1,)), ((), ())), preferred_element_type=F32)


def norm_parts(resid):
    center = resid - jnp.mean(resid, axis=-1, keepdims=True)
    rstd = lax.rsqrt(jnp.mean(center * center, axis=-1, keepdims=True) + EPSILON)
    return center * rstd, rstd


def norm_back(unit, rstd, gain, upstream):
    scaled = upstream * gain
    mean_s = jnp.mean(scaled, axis=-1, keepdims=True)
    mean_su = jnp.mean(scaled * unit, axis=-1, keepdims=True)
    grad = rstd * (scaled - mean_s - unit * mean_su)
    return grad, col_sum(upstream * unit), col_sum(upstream)


def col_sum(rows):
    return jnp.sum(rows, axis=0, keepdims=True)


def place_rows(rows, count):
    parts = list(rows)
    parts.append(jnp.zeros((count - len(parts), parts[0].shape[1]), F32))
    return jnp.concatenate(parts, axis=0)


def gelu_parts(value):
    size = jnp.abs(value) * (0.5**0.5)
    bell = jnp.exp(-0.5 * value * value)
    t = 1.0 / (1.0 + 0.3275911 * size)
    poly = t * (0.254829592 + t * (-0.284496736 + t * (1.421413741 + t * (-1.453152027 + t * 1.061405429))))
    tail = 0.5 * poly * bell
    phi = jnp.where(value >= 0, 1.0 - tail, tail)
    return value * phi, phi + value * (bell * (1.0 / (2.0 * 3.141592653589793) ** 0.5))


def left_half(shape):
    return lax.broadcasted_iota(jnp.int32, shape, 1) < HEAD_DIM


def head_pair(side, pair):
    return pl.ds(pl.multiple_of(pair * 128 + side * HEAD_DIM, HEAD_DIM), HEAD_DIM)


def key_tile(tile, marks, side):
    left = left_half(tile.shape)
    return jnp.where(left, tile, marks) if side == 0 else jnp.where(left, marks, tile)


def query_tile(rows, marks, side):
    return jnp.concatenate([rows, marks] if side == 0 else [marks, rows], axis=0)


def attend_block(k_ref, qt_ref, vt_ref, kmark_ref, qmark_ref, ot_ref, lse_ref):
    kmark = kmark_ref[...]
    qmark = qmark_ref[0]
    ones = jnp.ones((16, SEQ_MAX), BF)

    def one_pair(pair, carry):
        tile = k_ref[:, pl.ds(pl.multiple_of(pair * 128, 128), 128)]
        for side in range(2):
            rows = head_pair(side, pair)
            scores = dot(key_tile(tile, kmark, side), query_tile(qt_ref[rows, :], qmark, side))
            peak = jnp.max(scores, axis=0, keepdims=True)
            weights = jnp.exp(scores - peak).astype(BF)
            result = dot(jnp.concatenate([vt_ref[rows, :], ones], axis=0), weights)
            total = result[HEAD_DIM : HEAD_DIM + 1]
            ot_ref[rows, :] = (result[:HEAD_DIM] * (1.0 / total)).astype(BF)
            lse_ref[0, pl.ds(pair * 2 + side, 1), :] = peak + jnp.log(total)
        return carry

    lax.fori_loop(0, PAIRS, one_pair, 0)


def attend_back_block(
    q_ref, k_ref, v_ref, qt_ref, kt_ref, ot_ref, do_ref, dot_ref, kmark_ref, qmark_ref, lse_ref, dqt_ref, dk_ref, dv_ref
):
    kmark = kmark_ref[...]
    qmark = qmark_ref[0]
    left = left_half((SEQ_MAX, 128))
    blank = jnp.zeros((HEAD_DIM, SEQ_MAX), BF)

    def one_pair(pair, carry):
        cols = pl.ds(pl.multiple_of(pair * 128, 128), 128)
        k_tile, v_tile, q_tile, do_tile = k_ref[:, cols], v_ref[:, cols], q_ref[:, cols], do_ref[:, cols]
        value_grads, key_grads = [], []
        for side in range(2):
            rows = head_pair(side, pair)
            scores = dot(key_tile(k_tile, kmark, side), query_tile(qt_ref[rows, :], qmark, side))
            probs = jnp.exp(scores - lse_ref[0, pl.ds(pair * 2 + side, 1), :])
            value_grads.append(dot(probs.astype(BF), do_tile))
            up = dot_ref[rows, :]
            center = col_sum(up.astype(F32) * ot_ref[rows, :].astype(F32))
            probs_grad = dot(v_tile, query_tile(up, blank, side))
            score_grad = (probs * (probs_grad - center)).astype(BF)
            key_grads.append(dot(score_grad, q_tile))
            dqt_ref[rows, :] = (dot(kt_ref[rows, :], score_grad) * SCALE).astype(BF)
        dv_ref[:, cols] = jnp.where(left, value_grads[0], value_grads[1]).astype(BF)
        dk_ref[:, cols] = jnp.where(left, key_grads[0], key_grads[1]).astype(BF)
        return carry

    lax.fori_loop(0, PAIRS, one_pair, 0)


def self_forward_kernel(
    x_ref, w_ref, bias_ref, kmark_ref, qmark_ref, q_ref, k_ref, v_ref, ot_ref, lse_ref, qt_s, vt_s
):
    x = x_ref[...]
    queries = ((dot(x, w_ref[0]) + bias_ref[0:1]).astype(BF)) * SCALE
    q_ref[...] = queries
    qt_s[...] = queries.T
    k_ref[...] = dot(x, w_ref[1]).astype(BF)
    values = (dot(x, w_ref[2]) + bias_ref[1:2]).astype(BF)
    v_ref[...] = values
    vt_s[...] = values.T
    attend_block(k_ref, qt_s, vt_s, kmark_ref, qmark_ref, ot_ref, lse_ref)


def cross_forward_kernel(
    x_ref, mem_ref, sot_ref, wo_ref, w_ref, bias_ref, gain_ref, shift_ref, kmark_ref, qmark_ref,
    first_sum_ref, low_ref, q_ref, k_ref, v_ref, ot_ref, lse_ref, second_sum_ref, qt_s, vt_s,
):
    mem = mem_ref[...]
    k_ref[...] = dot(mem, w_ref[1]).astype(BF)
    values = (dot(mem, w_ref[2]) + bias_ref[4:5]).astype(BF)
    v_ref[...] = values
    vt_s[...] = values.T
    first_sum = x_ref[...].astype(F32) + (dot(sot_ref[...].T, wo_ref[0]) + bias_ref[2:3])
    first_sum_ref[...] = first_sum
    unit, _ = norm_parts(first_sum)
    first = unit * gain_ref[0:1] + shift_ref[0:1]
    low = first.astype(BF)
    low_ref[...] = low
    queries = ((dot(low, w_ref[0]) + bias_ref[3:4]).astype(BF)) * SCALE
    q_ref[...] = queries
    qt_s[...] = queries.T
    attend_block(k_ref, qt_s, vt_s, kmark_ref, qmark_ref, ot_ref, lse_ref)
    second_sum_ref[...] = first + (dot(ot_ref[...].T, wo_ref[1]) + bias_ref[5:6])


def feed_kernel(
    ss_ref, cot_ref, win_ref, bin_ref, wout_ref, bout_ref, gain_ref, shift_ref,
    mixed_ref, ssg_ref, dwin_ref, dwout_ref, dbin_ref, small_ref,
    low_s, lowt_s, hid_s, slope_s, acc_s, third_s, z_s,
):
    phase, chunk = pl.program_id(0), pl.program_id(1)
    last = pl.num_programs(1) - 1

    @pl.when((phase == 0) & (chunk == 0))
    def _():
        unit, _ = norm_parts(ss_ref[...])
        second = unit * gain_ref[1:2] + shift_ref[1:2]
        low = second.astype(BF)
        low_s[...] = low
        lowt_s[...] = low.T
        acc_s[...] = second + bout_ref[...]

    @pl.when(phase == 0)
    def _():
        pre = dot(low_s[...], win_ref[...]) + bin_ref[...]
        hidden, slope = gelu_parts(pre)
        hidden = hidden.astype(BF)
        hid_s[chunk] = hidden
        slope_s[chunk] = slope
        acc_s[...] += dot(hidden, wout_ref[...])

    @pl.when((phase == 1) & (chunk == 0))
    def _():
        unit, rstd = norm_parts(acc_s[...])
        mixed_ref[...] = (unit * gain_ref[2:3] + shift_ref[2:3]).astype(BF)
        third, dgain, dshift = norm_back(unit, rstd, gain_ref[2:3], cot_ref[...].astype(F32))
        z = third.astype(BF)
        z_s[...] = z
        acc_s[...] = third
        small_ref[...] = place_rows([dgain, dshift, col_sum(z.astype(F32))], 8)

    @pl.when(phase == 1)
    def _():
        z = z_s[...]
        pre_grad = (dot_nt(z, wout_ref[...]) * slope_s[chunk]).astype(BF)
        dbin_ref[...] = col_sum(pre_grad.astype(F32))
        dwout_ref[...] = dot(hid_s[chunk].T, z).astype(BF)
        dwin_ref[...] = dot(lowt_s[...], pre_grad).astype(BF)
        acc_s[...] += dot_nt(pre_grad, win_ref[...])

    @pl.when((phase == 1) & (chunk == last))
    def _():
        unit, rstd = norm_parts(ss_ref[...])
        grad, dgain, dshift = norm_back(unit, rstd, gain_ref[1:2], acc_s[...])
        ssg_ref[...] = grad
        small_ref[3:5] = jnp.concatenate([dgain, dshift], axis=0)


def add_to(ref, index, value, first):
    @pl.when(first)
    def _():
        ref[index] = value

    @pl.when(jnp.logical_not(first))
    def _():
        ref[index] += value


def cross_back_kernel(
    ssg_ref, fs_ref, low_ref, mem_ref, q_ref, k_ref, v_ref, ot_ref, lse_ref, wo_ref, w_ref, gain_ref, kmark_ref, qmark_ref,
    fsg_ref, mg_ref, dw_ref, small_ref,
    qt_s, kt_s, do_s, dot_s, dqt_s, dk_s, dv_s, acc_s, small_s,
):
    block = pl.program_id(0)
    first, last = block == 0, block == pl.num_programs(0) - 1
    upstream = ssg_ref[...]
    branch = upstream.astype(BF)
    out_grad = dot(ot_ref[...], branch)
    mixed_grad = dot_nt(branch, wo_ref[0]).astype(BF)
    do_s[...] = mixed_grad
    dot_s[...] = mixed_grad.T
    qt_s[...] = q_ref[...].T
    kt_s[...] = k_ref[...].T
    attend_back_block(
        q_ref, k_ref, v_ref, qt_s, kt_s, ot_ref, do_s, dot_s, kmark_ref, qmark_ref, lse_ref, dqt_s, dk_s, dv_s
    )
    dq = dqt_s[...].T
    dk, dv = dk_s[...], dv_s[...]
    mg_ref[...] = dot_nt(dk, w_ref[1]) + dot_nt(dv, w_ref[2])
    memt = mem_ref[...].T
    add_to(acc_s, 0, dot(low_ref[...].T, dq), first)
    add_to(acc_s, 1, dot(memt, dk), first)
    add_to(acc_s, 2, dot(memt, dv), first)
    add_to(acc_s, 3, out_grad, first)
    first_grad = upstream + dot_nt(dq, w_ref[0])
    unit, rstd = norm_parts(fs_ref[...])
    grad, dgain, dshift = norm_back(unit, rstd, gain_ref[0:1], first_grad)
    fsg_ref[...] = grad
    sums = [col_sum(dq.astype(F32)), col_sum(dv.astype(F32)), col_sum(branch.astype(F32)), dgain, dshift]
    add_to(small_s, slice(None), place_rows(sums, 8), first)

    @pl.when(last)
    def _():
        dw_ref[...] = acc_s[...].astype(BF)
        small_ref[...] = small_s[...]


def self_back_kernel(
    fsg_ref, x_ref, q_ref, k_ref, v_ref, ot_ref, lse_ref, wo_ref, w_ref, kmark_ref, qmark_ref,
    qg_ref, dw_ref, small_ref,
    qt_s, kt_s, do_s, dot_s, dqt_s, dk_s, dv_s, acc_s, small_s,
):
    block = pl.program_id(0)
    first, last = block == 0, block == pl.num_programs(0) - 1
    upstream = fsg_ref[...]
    branch = upstream.astype(BF)
    out_grad = dot(ot_ref[...], branch)
    mixed_grad = dot_nt(branch, wo_ref[0]).astype(BF)
    do_s[...] = mixed_grad
    dot_s[...] = mixed_grad.T
    qt_s[...] = q_ref[...].T
    kt_s[...] = k_ref[...].T
    attend_back_block(
        q_ref, k_ref, v_ref, qt_s, kt_s, ot_ref, do_s, dot_s, kmark_ref, qmark_ref, lse_ref, dqt_s, dk_s, dv_s
    )
    dq = dqt_s[...].T
    dk, dv = dk_s[...], dv_s[...]
    xt = x_ref[...].T
    add_to(acc_s, 0, dot(xt, dq), first)
    add_to(acc_s, 1, dot(xt, dk), first)
    add_to(acc_s, 2, dot(xt, dv), first)
    add_to(acc_s, 3, out_grad, first)
    qg_ref[...] = upstream + dot_nt(dq, w_ref[0]) + dot_nt(dk, w_ref[1]) + dot_nt(dv, w_ref[2])
    sums = [col_sum(dq.astype(F32)), col_sum(dv.astype(F32)), col_sum(branch.astype(F32))]
    add_to(small_s, slice(None), place_rows(sums, 8), first)

    @pl.when(last)
    def _():
        dw_ref[...] = acc_s[...].astype(BF)
        small_ref[...] = small_s[...]


def row_block(width):
    return pl.BlockSpec((SEQ_MAX, width), lambda b: (b, 0))


def col_block(height):
    return pl.BlockSpec((height, SEQ_MAX), lambda b: (0, b))


def lead_block(rows):
    return pl.BlockSpec((1, rows, SEQ_MAX), lambda b: (b, 0, 0))


def whole(array, **kw):
    zeros = (0,) * array.ndim
    return pl.BlockSpec(array.shape, lambda *_: zeros, pipeline_mode=pl.Buffered(1))


def params(semantics):
    return pltpu.CompilerParams(vmem_limit_bytes=VMEM_LIMIT, dimension_semantics=semantics)


def cost(flops, data, exps=0):
    return pl.CostEstimate(flops=int(flops), bytes_accessed=int(data), transcendentals=int(exps))


def shape(dims, kind):
    return jax.ShapeDtypeStruct(dims, kind)


def self_forward(x, w, bias, kmark, qmark):
    rows, d = x.shape
    blocks = rows // SEQ_MAX
    act = shape((rows, d), BF)
    return pl.pallas_call(
        self_forward_kernel,
        grid=(blocks,),
        in_specs=[row_block(d), whole(w), whole(bias), row_block(128), lead_block(HEAD_DIM)],
        out_specs=[row_block(d), row_block(d), row_block(d), col_block(d), lead_block(16)],
        out_shape=[act, act, act, shape((d, rows), BF), shape((blocks, 16, SEQ_MAX), F32)],
        scratch_shapes=[pltpu.VMEM((d, SEQ_MAX), BF)] * 2,
        compiler_params=params(("arbitrary",)),
        cost_estimate=cost(20e9, 12e6),
        name="self_forward",
    )(x, w, bias, kmark, qmark)


def cross_forward(x, mem, sot, wo, w, bias, gain, shift, kmark, qmark):
    rows, d = x.shape
    blocks = rows // SEQ_MAX
    act, wide = shape((rows, d), BF), shape((rows, d), F32)
    return pl.pallas_call(
        cross_forward_kernel,
        grid=(blocks,),
        in_specs=[
            row_block(d), row_block(d), col_block(d), whole(wo), whole(w), whole(bias), whole(gain), whole(shift),
            row_block(128), lead_block(HEAD_DIM),
        ],
        out_specs=[row_block(d)] * 5 + [col_block(d), lead_block(16), row_block(d)],
        out_shape=[wide, act, act, act, act, shape((d, rows), BF), shape((blocks, 16, SEQ_MAX), F32), wide],
        scratch_shapes=[pltpu.VMEM((d, SEQ_MAX), BF)] * 2,
        compiler_params=params(("arbitrary",)),
        cost_estimate=cost(24e9, 20e6),
        name="cross_forward",
    )(x, mem, sot, wo, w, bias, gain, shift, kmark, qmark)


def feed(second_sum, cot, win, bin_, wout, bout, gain, shift):
    rows, d = second_sum.shape
    ff = win.shape[1]
    width = 512
    chunks = ff // width
    fixed = lambda p, j: (0, 0)
    phase_chunk = lambda p, j: j * p
    return pl.pallas_call(
        feed_kernel,
        grid=(2, chunks),
        in_specs=[
            whole(second_sum), whole(cot),
            pl.BlockSpec((d, width), lambda p, j: (0, j)),
            pl.BlockSpec((1, width), lambda p, j: (0, j)),
            pl.BlockSpec((width, d), lambda p, j: (j, 0)),
            whole(bout), whole(gain), whole(shift),
        ],
        out_specs=[
            pl.BlockSpec((rows, d), fixed),
            pl.BlockSpec((rows, d), fixed),
            pl.BlockSpec((d, width), lambda p, j: (0, j * p)),
            pl.BlockSpec((width, d), lambda p, j: (j * p, 0)),
            pl.BlockSpec((1, width), lambda p, j: (0, j * p)),
            pl.BlockSpec((8, d), fixed),
        ],
        out_shape=[
            shape((rows, d), BF), shape((rows, d), F32), shape((d, ff), BF), shape((ff, d), BF),
            shape((1, ff), F32), shape((8, d), F32),
        ],
        scratch_shapes=[
            pltpu.VMEM((rows, d), BF), pltpu.VMEM((d, rows), BF),
            pltpu.VMEM((chunks, rows, width), BF), pltpu.VMEM((chunks, rows, width), F32),
            pltpu.VMEM((rows, d), F32), pltpu.VMEM((8, 128), F32), pltpu.VMEM((rows, d), BF),
        ],
        compiler_params=params(("arbitrary", "arbitrary")),
        cost_estimate=cost(40e9, 40e6),
        name="feed",
    )(second_sum, cot, win, bin_, wout, bout, gain, shift)


def back_scratch(d):
    return (
        [pltpu.VMEM((d, SEQ_MAX), BF)] * 2 + [pltpu.VMEM((SEQ_MAX, d), BF)] + [pltpu.VMEM((d, SEQ_MAX), BF)] * 2
        + [pltpu.VMEM((SEQ_MAX, d), BF)] * 2 + [pltpu.VMEM((4, d, d), F32), pltpu.VMEM((8, d), F32)]
    )


def cross_back(ssg, first_sum, low, mem, q, k, v, ot, lse, wo, w, gain, kmark, qmark):
    rows, d = low.shape
    blocks = rows // SEQ_MAX
    wide = shape((rows, d), F32)
    return pl.pallas_call(
        cross_back_kernel,
        grid=(blocks,),
        in_specs=[row_block(d)] * 7 + [
            col_block(d), lead_block(16), whole(wo), whole(w), whole(gain), row_block(128), lead_block(HEAD_DIM),
        ],
        out_specs=[
            row_block(d), row_block(d),
            pl.BlockSpec((4, d, d), lambda b: (0, 0, 0), pipeline_mode=pl.Buffered(1)),
            pl.BlockSpec((8, d), lambda b: (0, 0)),
        ],
        out_shape=[wide, wide, shape((4, d, d), BF), shape((8, d), F32)],
        scratch_shapes=back_scratch(d),
        compiler_params=params(("arbitrary",)),
        cost_estimate=cost(50e9, 30e6),
        name="cross_back",
    )(ssg, first_sum, low, mem, q, k, v, ot, lse, wo, w, gain, kmark, qmark)


def self_back(fsg, x, q, k, v, ot, lse, wo, w, kmark, qmark):
    rows, d = x.shape
    blocks = rows // SEQ_MAX
    return pl.pallas_call(
        self_back_kernel,
        grid=(blocks,),
        in_specs=[row_block(d)] * 5 + [
            col_block(d), lead_block(16), whole(wo), whole(w), row_block(128), lead_block(HEAD_DIM),
        ],
        out_specs=[
            row_block(d),
            pl.BlockSpec((4, d, d), lambda b: (0, 0, 0), pipeline_mode=pl.Buffered(1)),
            pl.BlockSpec((8, d), lambda b: (0, 0)),
        ],
        out_shape=[shape((rows, d), F32), shape((4, d, d), BF), shape((8, d), F32)],
        scratch_shapes=back_scratch(d),
        compiler_params=params(("arbitrary",)),
        cost_estimate=cost(50e9, 30e6),
        name="self_back",
    )(fsg, x, q, k, v, ot, lse, wo, w, kmark, qmark)


def key_marks(seg):
    odd = (seg & 1)[:, None]
    lane = lax.broadcasted_iota(jnp.int32, (seg.shape[0], 128), 1) % HEAD_DIM
    return jnp.where(lane == 0, 1 - odd, jnp.where(lane == 1, odd, 0)).astype(BF)


def query_marks(seg):
    odd = (seg & 1).reshape(-1, 1, SEQ_MAX)
    row = lax.broadcasted_iota(jnp.int32, (odd.shape[0], HEAD_DIM, SEQ_MAX), 1)
    return jnp.where(row == 0, odd, jnp.where(row == 1, 1 - odd, 0)).astype(BF) * (-MASKED)


def layer(query, memory, query_seg, memory_seg, params_, cotangent):
    proj, out, bias, gain, shift, win, bin_, wout, bout = params_
    bias, gain, shift = bias.astype(F32), gain.astype(F32), shift.astype(F32)
    bin_, bout = bin_.astype(F32)[None], bout.astype(F32)[None]
    qmark = query_marks(query_seg)
    smark, cmark = key_marks(query_seg), key_marks(memory_seg)
    sq, sk, sv, sot, slse = self_forward(query, proj[0:3], bias, smark, qmark)
    first_sum, low, cq, ck, cv, cot_, clse, second_sum = cross_forward(
        query, memory, sot, out, proj[3:6], bias, gain, shift, cmark, qmark
    )
    mixed, ssg, dwin, dwout, dbin, small3 = feed(second_sum, cotangent, win, bin_, wout, bout, gain, shift)
    fsg, memory_grad, cdw, small2 = cross_back(
        ssg, first_sum, low, memory, cq, ck, cv, cot_, clse, out[1:2], proj[3:6], gain, cmark, qmark
    )
    query_grad, sdw, small1 = self_back(fsg, query, sq, sk, sv, sot, slse, out[0:1], proj[0:3], smark, qmark)
    bias_grad = jnp.stack([small1[0], small1[1], small1[2], small2[0], small2[1], small2[2]])
    gain_grad = jnp.stack([small2[3], small3[3], small3[0]])
    shift_grad = jnp.stack([small2[4], small3[4], small3[1]])
    return mixed, query_grad, memory_grad, sdw, cdw, bias_grad, gain_grad, shift_grad, dwin, dbin[0], dwout, small3[2]


BOTH = ("dp", "fsdp")


def body(
    query, memory, query_seg, memory_seg, attn_proj, attn_out, attn_bias, norm_gain, norm_bias, ffn_in, ffn_in_bias,
    ffn_out, ffn_out_bias, cotangent,
):
    gather = functools.partial(lax.all_gather, axis_name=BOTH, tiled=True)
    scatter = functools.partial(lax.psum_scatter, axis_name=BOTH, tiled=True)
    full = (
        gather(attn_proj, axis=1), gather(attn_out, axis=1), gather(attn_bias, axis=1), gather(norm_gain, axis=1),
        gather(norm_bias, axis=1), gather(ffn_in, axis=0), gather(ffn_in_bias, axis=0), gather(ffn_out, axis=0),
        gather(ffn_out_bias, axis=0),
    )
    mixed, query_grad, memory_grad, sdw, cdw, bias_g, gain_g, shift_g, dwin, dbin, dwout, dbout = layer(
        query, memory, query_seg, memory_seg, full, cotangent
    )
    dwin = scatter(dwin, scatter_dimension=0)
    dwout = scatter(dwout, scatter_dimension=0)
    cdw = scatter(cdw, scatter_dimension=1)
    sdw = scatter(sdw, scatter_dimension=1)
    proj_grad = jnp.concatenate([sdw[:3], cdw[:3]]).astype(F32)
    out_grad = jnp.concatenate([sdw[3:], cdw[3:]]).astype(F32)
    return (
        mixed, query_grad, memory_grad, proj_grad, out_grad,
        scatter(bias_g, scatter_dimension=1), scatter(gain_g, scatter_dimension=1), scatter(shift_g, scatter_dimension=1),
        dwin.astype(F32), scatter(dbin, scatter_dimension=0), dwout.astype(F32), scatter(dbout, scatter_dimension=0),
    )


def solution(mesh):
    rows, mid, flat, row1 = P(BOTH, None), P(None, BOTH, None), P(None, BOTH), P(BOTH)
    return jax.shard_map(
        body,
        mesh=mesh,
        in_specs=(rows, rows, row1, row1, mid, mid, flat, flat, flat, rows, row1, rows, row1, rows),
        out_specs=(rows, rows, rows, mid, mid, flat, flat, flat, rows, row1, rows, row1),
        check_vma=False,
    )
```

```python
import functools

import jax
import jax.numpy as jnp
from jax import lax
from jax.experimental import pallas as pl
from jax.experimental.pallas import tpu as pltpu
from jax.sharding import Mesh
from jax.sharding import PartitionSpec as P

HEADS = 12
HEAD_DIM = 64
SEQ_MAX = 512
PAIRS = HEADS // 2
EPSILON = 1e-05
MASKED = 1e30
SCALE = HEAD_DIM ** (-0.5)
BF = jnp.bfloat16
F32 = jnp.float32
VMEM_LIMIT = 60 * 1024 * 1024


def dot(left, right):
    return jnp.dot(left, right, preferred_element_type=F32)


def dot_nt(left, right):
    return lax.dot_general(left, right, (((1,), (1,)), ((), ())), preferred_element_type=F32)


def norm_parts(resid):
    center = resid - jnp.mean(resid, axis=-1, keepdims=True)
    rstd = lax.rsqrt(jnp.mean(center * center, axis=-1, keepdims=True) + EPSILON)
    return center * rstd, rstd


def norm_back(unit, rstd, gain, upstream):
    scaled = upstream * gain
    mean_s = jnp.mean(scaled, axis=-1, keepdims=True)
    mean_su = jnp.mean(scaled * unit, axis=-1, keepdims=True)
    grad = rstd * (scaled - mean_s - unit * mean_su)
    return grad, col_sum(upstream * unit), col_sum(upstream)


def col_sum(rows):
    return jnp.sum(rows, axis=0, keepdims=True)


def place_rows(rows, count):
    parts = list(rows)
    parts.append(jnp.zeros((count - len(parts), parts[0].shape[1]), F32))
    return jnp.concatenate(parts, axis=0)


def gelu_parts(value):
    size = jnp.abs(value) * (0.5**0.5)
    bell = jnp.exp(-0.5 * value * value)
    t = 1.0 / (1.0 + 0.3275911 * size)
    poly = t * (0.254829592 + t * (-0.284496736 + t * (1.421413741 + t * (-1.453152027 + t * 1.061405429))))
    tail = 0.5 * poly * bell
    phi = jnp.where(value >= 0, 1.0 - tail, tail)
    return value * phi, phi + value * (bell * (1.0 / (2.0 * 3.141592653589793) ** 0.5))


def left_half(shape):
    return lax.broadcasted_iota(jnp.int32, shape, 1) < HEAD_DIM


def head_pair(side, pair):
    return pl.ds(pl.multiple_of(pair * 128 + side * HEAD_DIM, HEAD_DIM), HEAD_DIM)


def key_tile(tile, marks, side):
    left = left_half(tile.shape)
    return jnp.where(left, tile, marks) if side == 0 else jnp.where(left, marks, tile)


def query_tile(rows, marks, side):
    return jnp.concatenate([rows, marks] if side == 0 else [marks, rows], axis=0)


def attend_block(k_ref, qt_ref, vt_ref, kmark_ref, qmark_ref, ot_ref, lse_ref):
    kmark = kmark_ref[...]
    qmark = qmark_ref[0]
    ones = jnp.ones((16, SEQ_MAX), BF)

    def one_pair(pair, carry):
        tile = k_ref[:, pl.ds(pl.multiple_of(pair * 128, 128), 128)]
        for side in range(2):
            rows = head_pair(side, pair)
            scores = dot(key_tile(tile, kmark, side), query_tile(qt_ref[rows, :], qmark, side))
            peak = jnp.max(scores, axis=0, keepdims=True)
            weights = jnp.exp(scores - peak).astype(BF)
            result = dot(jnp.concatenate([vt_ref[rows, :], ones], axis=0), weights)
            total = result[HEAD_DIM : HEAD_DIM + 1]
            ot_ref[rows, :] = (result[:HEAD_DIM] * (1.0 / total)).astype(BF)
            lse_ref[0, pl.ds(pair * 2 + side, 1), :] = peak + jnp.log(total)
        return carry

    lax.fori_loop(0, PAIRS, one_pair, 0)


def attend_back_block(
    q_ref, k_ref, v_ref, qt_ref, kt_ref, ot_ref, do_ref, dot_ref, kmark_ref, qmark_ref, lse_ref, dqt_ref, dk_ref, dv_ref
):
    kmark = kmark_ref[...]
    qmark = qmark_ref[0]
    left = left_half((SEQ_MAX, 128))
    blank = jnp.zeros((HEAD_DIM, SEQ_MAX), BF)

    def one_pair(pair, carry):
        cols = pl.ds(pl.multiple_of(pair * 128, 128), 128)
        k_tile, v_tile, q_tile, do_tile = k_ref[:, cols], v_ref[:, cols], q_ref[:, cols], do_ref[:, cols]
        value_grads, key_grads = [], []
        for side in range(2):
            rows = head_pair(side, pair)
            scores = dot(key_tile(k_tile, kmark, side), query_tile(qt_ref[rows, :], qmark, side))
            probs = jnp.exp(scores - lse_ref[0, pl.ds(pair * 2 + side, 1), :])
            value_grads.append(dot(probs.astype(BF), do_tile))
            up = dot_ref[rows, :]
            center = col_sum(up.astype(F32) * ot_ref[rows, :].astype(F32))
            probs_grad = dot(v_tile, query_tile(up, blank, side))
            score_grad = (probs * (probs_grad - center)).astype(BF)
            key_grads.append(dot(score_grad, q_tile))
            dqt_ref[rows, :] = (dot(kt_ref[rows, :], score_grad) * SCALE).astype(BF)
        dv_ref[:, cols] = jnp.where(left, value_grads[0], value_grads[1]).astype(BF)
        dk_ref[:, cols] = jnp.where(left, key_grads[0], key_grads[1]).astype(BF)
        return carry

    lax.fori_loop(0, PAIRS, one_pair, 0)


def self_forward_kernel(
    x_ref, wqk_ref, wv_ref, bias_ref, kmark_ref, qmark_ref, q_ref, k_ref, v_ref, ot_ref, lse_ref, qt_s, vt_s
):
    x = x_ref[...]
    queries = ((dot(x, wqk_ref[0]) + bias_ref[0:1]).astype(BF)) * SCALE
    q_ref[...] = queries
    qt_s[...] = queries.T
    k_ref[...] = dot(x, wqk_ref[1]).astype(BF)
    values = (dot(x, wv_ref[0]) + bias_ref[1:2]).astype(BF)
    v_ref[...] = values
    vt_s[...] = values.T
    attend_block(k_ref, qt_s, vt_s, kmark_ref, qmark_ref, ot_ref, lse_ref)


def cross_forward_kernel(
    x_ref, mem_ref, sot_ref, wo_ref, w_ref, bias_ref, gain_ref, shift_ref, kmark_ref, qmark_ref,
    first_sum_ref, low_ref, q_ref, k_ref, v_ref, ot_ref, lse_ref, second_sum_ref, qt_s, vt_s,
):
    mem = mem_ref[...]
    k_ref[...] = dot(mem, w_ref[1]).astype(BF)
    values = (dot(mem, w_ref[2]) + bias_ref[4:5]).astype(BF)
    v_ref[...] = values
    vt_s[...] = values.T
    first_sum = x_ref[...].astype(F32) + (dot(sot_ref[...].T, wo_ref[0]) + bias_ref[2:3])
    first_sum_ref[...] = first_sum
    unit, _ = norm_parts(first_sum)
    first = unit * gain_ref[0:1] + shift_ref[0:1]
    low = first.astype(BF)
    low_ref[...] = low
    queries = ((dot(low, w_ref[0]) + bias_ref[3:4]).astype(BF)) * SCALE
    q_ref[...] = queries
    qt_s[...] = queries.T
    attend_block(k_ref, qt_s, vt_s, kmark_ref, qmark_ref, ot_ref, lse_ref)
    second_sum_ref[...] = first + (dot(ot_ref[...].T, wo_ref[1]) + bias_ref[5:6])


def feed_kernel(
    ss_ref, cot_ref, win_ref, bin_ref, wout_ref, bout_ref, gain_ref, shift_ref,
    mixed_ref, ssg_ref, dwin_ref, dwout_ref, dbin_ref, small_ref,
    low_s, lowt_s, hid_s, slope_s, acc_s, third_s, z_s,
):
    phase, chunk = pl.program_id(0), pl.program_id(1)
    last = pl.num_programs(1) - 1

    @pl.when((phase == 0) & (chunk == 0))
    def _():
        unit, _ = norm_parts(ss_ref[...])
        second = unit * gain_ref[1:2] + shift_ref[1:2]
        low = second.astype(BF)
        low_s[...] = low
        lowt_s[...] = low.T
        acc_s[...] = second + bout_ref[...]

    @pl.when(phase == 0)
    def _():
        pre = dot(low_s[...], win_ref[0]) + bin_ref[...]
        hidden, slope = gelu_parts(pre)
        hidden = hidden.astype(BF)
        hid_s[chunk] = hidden
        slope_s[chunk] = slope
        acc_s[...] += dot(hidden, wout_ref[...])

    @pl.when((phase == 1) & (chunk == 0))
    def _():
        unit, rstd = norm_parts(acc_s[...])
        mixed_ref[...] = (unit * gain_ref[2:3] + shift_ref[2:3]).astype(BF)
        third, dgain, dshift = norm_back(unit, rstd, gain_ref[2:3], cot_ref[...].astype(F32))
        z = third.astype(BF)
        z_s[...] = z
        acc_s[...] = third
        small_ref[...] = place_rows([dgain, dshift, col_sum(z.astype(F32))], 8)

    @pl.when(phase == 1)
    def _():
        z = z_s[...]
        pre_grad = (dot_nt(z, wout_ref[...]) * slope_s[chunk]).astype(BF)
        dbin_ref[...] = col_sum(pre_grad.astype(F32))
        dwout_ref[...] = dot(hid_s[chunk].T, z).astype(BF)
        dwin_ref[0] = dot(lowt_s[...], pre_grad).astype(BF)
        acc_s[...] += dot_nt(pre_grad, win_ref[0])

    @pl.when((phase == 1) & (chunk == last))
    def _():
        unit, rstd = norm_parts(ss_ref[...])
        grad, dgain, dshift = norm_back(unit, rstd, gain_ref[1:2], acc_s[...])
        ssg_ref[...] = grad
        small_ref[3:5] = jnp.concatenate([dgain, dshift], axis=0)


def cross_back_kernel(
    ssg_ref, fs_ref, q_ref, k_ref, v_ref, ot_ref, lse_ref, wo_ref, w_ref, gain_ref, kmark_ref, qmark_ref, *refs
):
    fsg_ref, dq_ref, dk_ref, dv_ref, small_ref, qt_s, kt_s, do_s, dot_s, dqt_s = refs[-10:]
    upstream = ssg_ref[...]
    branch = upstream.astype(BF)
    mixed_grad = dot_nt(branch, wo_ref[0]).astype(BF)
    do_s[...] = mixed_grad
    dot_s[...] = mixed_grad.T
    qt_s[...] = q_ref[...].T
    kt_s[...] = k_ref[...].T
    attend_back_block(
        q_ref, k_ref, v_ref, qt_s, kt_s, ot_ref, do_s, dot_s, kmark_ref, qmark_ref, lse_ref, dqt_s, dk_ref, dv_ref
    )
    dq = dqt_s[...].T
    dq_ref[...] = dq
    first_grad = upstream + dot_nt(dq, w_ref[0])
    unit, rstd = norm_parts(fs_ref[...])
    grad, dgain, dshift = norm_back(unit, rstd, gain_ref[0:1], first_grad)
    fsg_ref[...] = grad
    sums = [col_sum(dq.astype(F32)), col_sum(dv_ref[...].astype(F32)), col_sum(branch.astype(F32)), dgain, dshift]
    small_ref[...] = place_rows(sums, 8)


def self_back_kernel(fsg_ref, q_ref, k_ref, v_ref, ot_ref, lse_ref, wo_ref, kmark_ref, qmark_ref, *refs):
    dq_ref, dk_ref, dv_ref, small_ref, qt_s, kt_s, do_s, dot_s, dqt_s = refs[-9:]
    branch = fsg_ref[...].astype(BF)
    mixed_grad = dot_nt(branch, wo_ref[0]).astype(BF)
    do_s[...] = mixed_grad
    dot_s[...] = mixed_grad.T
    qt_s[...] = q_ref[...].T
    kt_s[...] = k_ref[...].T
    attend_back_block(
        q_ref, k_ref, v_ref, qt_s, kt_s, ot_ref, do_s, dot_s, kmark_ref, qmark_ref, lse_ref, dqt_s, dk_ref, dv_ref
    )
    dq = dqt_s[...].T
    dq_ref[...] = dq
    sums = [col_sum(dq.astype(F32)), col_sum(dv_ref[...].astype(F32)), col_sum(branch.astype(F32))]
    small_ref[...] = place_rows(sums, 8)


def cross_weight_kernel(
    dq_ref, dk_ref, dv_ref, low_ref, mem_ref, ot_ref, ssg_ref, sot_ref, fsg_ref, w_ref, dw_ref, mg_ref
):
    dk, dv = dk_ref[...], dv_ref[...]
    memt = mem_ref[...].T
    dw_ref[0] = dot(low_ref[...].T, dq_ref[...]).astype(BF)
    dw_ref[1] = dot(memt, dk).astype(BF)
    dw_ref[2] = dot(memt, dv).astype(BF)
    dw_ref[3] = dot(ot_ref[...], ssg_ref[...].astype(BF)).astype(BF)
    dw_ref[4] = dot(sot_ref[...], fsg_ref[...].astype(BF)).astype(BF)
    mg_ref[...] = dot_nt(dk, w_ref[1]) + dot_nt(dv, w_ref[2])


def self_weight_kernel(dq_ref, dk_ref, dv_ref, x_ref, dw_ref):
    xt = x_ref[...].T
    dw_ref[0] = dot(xt, dq_ref[...]).astype(BF)
    dw_ref[1] = dot(xt, dk_ref[...]).astype(BF)
    dw_ref[2] = dot(xt, dv_ref[...]).astype(BF)


def self_input_kernel(fsg_ref, dq_ref, dk_ref, dv_ref, wqk_ref, wv_ref, qg_ref):
    qg_ref[...] = (
        fsg_ref[...]
        + dot_nt(dq_ref[...], wqk_ref[0]) + dot_nt(dk_ref[...], wqk_ref[1]) + dot_nt(dv_ref[...], wv_ref[0])
    )


def row_block(width):
    return pl.BlockSpec((SEQ_MAX, width), lambda b: (b, 0))


def col_block(height):
    return pl.BlockSpec((height, SEQ_MAX), lambda b: (0, b))


def lead_block(rows):
    return pl.BlockSpec((1, rows, SEQ_MAX), lambda b: (b, 0, 0))


def whole(array, **kw):
    zeros = (0,) * array.ndim
    return pl.BlockSpec(array.shape, lambda *_: zeros, pipeline_mode=pl.Buffered(1))


def params(semantics):
    return pltpu.CompilerParams(vmem_limit_bytes=VMEM_LIMIT, dimension_semantics=semantics)


def cost(flops, data, exps=0):
    return pl.CostEstimate(flops=int(flops), bytes_accessed=int(data), transcendentals=int(exps))


def shape(dims, kind):
    return jax.ShapeDtypeStruct(dims, kind)


def self_forward(x, wqk, wv, bias, kmark, qmark):
    rows, d = x.shape
    blocks = rows // SEQ_MAX
    act = shape((rows, d), BF)
    return pl.pallas_call(
        self_forward_kernel,
        grid=(blocks,),
        in_specs=[row_block(d), whole(wqk), whole(wv), whole(bias), row_block(128), lead_block(HEAD_DIM)],
        out_specs=[row_block(d), row_block(d), row_block(d), col_block(d), lead_block(16)],
        out_shape=[act, act, act, shape((d, rows), BF), shape((blocks, 16, SEQ_MAX), F32)],
        scratch_shapes=[pltpu.VMEM((d, SEQ_MAX), BF)] * 2,
        compiler_params=params(("arbitrary",)),
        cost_estimate=cost(20e9, 12e6),
        name="self_forward",
    )(x, wqk, wv, bias, kmark, qmark)


def cross_forward(x, mem, sot, wo, w, bias, gain, shift, kmark, qmark):
    rows, d = x.shape
    blocks = rows // SEQ_MAX
    act, wide = shape((rows, d), BF), shape((rows, d), F32)
    return pl.pallas_call(
        cross_forward_kernel,
        grid=(blocks,),
        in_specs=[
            row_block(d), row_block(d), col_block(d), whole(wo), whole(w), whole(bias), whole(gain), whole(shift),
            row_block(128), lead_block(HEAD_DIM),
        ],
        out_specs=[row_block(d)] * 5 + [col_block(d), lead_block(16), row_block(d)],
        out_shape=[wide, act, act, act, act, shape((d, rows), BF), shape((blocks, 16, SEQ_MAX), F32), wide],
        scratch_shapes=[pltpu.VMEM((d, SEQ_MAX), BF)] * 2,
        compiler_params=params(("arbitrary",)),
        cost_estimate=cost(24e9, 20e6),
        name="cross_forward",
    )(x, mem, sot, wo, w, bias, gain, shift, kmark, qmark)


def feed(second_sum, cot, win, bin_, wout, bout, gain, shift):
    rows, d = second_sum.shape
    chunks, _, width = win.shape
    ff = chunks * width
    fixed = lambda p, j: (0, 0)
    return pl.pallas_call(
        feed_kernel,
        grid=(2, chunks),
        in_specs=[
            whole(second_sum), whole(cot),
            pl.BlockSpec((1, d, width), lambda p, j: (j, 0, 0)),
            pl.BlockSpec((1, width), lambda p, j: (0, j)),
            pl.BlockSpec((width, d), lambda p, j: (j, 0)),
            whole(bout), whole(gain), whole(shift),
        ],
        out_specs=[
            pl.BlockSpec((rows, d), fixed),
            pl.BlockSpec((rows, d), fixed),
            pl.BlockSpec((1, d, width), lambda p, j: (j * p, 0, 0)),
            pl.BlockSpec((width, d), lambda p, j: (j * p, 0)),
            pl.BlockSpec((1, width), lambda p, j: (0, j * p)),
            pl.BlockSpec((8, d), fixed),
        ],
        out_shape=[
            shape((rows, d), BF), shape((rows, d), F32), shape((chunks, d, width), BF), shape((ff, d), BF),
            shape((1, ff), F32), shape((8, d), F32),
        ],
        scratch_shapes=[
            pltpu.VMEM((rows, d), BF), pltpu.VMEM((d, rows), BF),
            pltpu.VMEM((chunks, rows, width), BF), pltpu.VMEM((chunks, rows, width), F32),
            pltpu.VMEM((rows, d), F32), pltpu.VMEM((8, 128), F32), pltpu.VMEM((rows, d), BF),
        ],
        compiler_params=params(("arbitrary", "arbitrary")),
        cost_estimate=cost(40e9, 40e6),
        name="feed",
    )(second_sum, cot, win, bin_, wout, bout, gain, shift)


def back_scratch(d):
    return (
        [pltpu.VMEM((d, SEQ_MAX), BF)] * 2 + [pltpu.VMEM((SEQ_MAX, d), BF)] + [pltpu.VMEM((d, SEQ_MAX), BF)] * 2
    )


def at_row(block, width):
    return pl.BlockSpec((SEQ_MAX, width), lambda b: (block, 0))


def at_col(block, height):
    return pl.BlockSpec((height, SEQ_MAX), lambda b: (0, block))


def at_lead(block, rows):
    return pl.BlockSpec((1, rows, SEQ_MAX), lambda b: (block, 0, 0))


def one_back(kernel, block, before, args, specs, outs, name):
    d = outs[0].shape[1]
    kept = [pl.BlockSpec(memory_space=pl.ANY)] * len(before)
    return pl.pallas_call(
        kernel,
        grid=(1,),
        in_specs=specs + kept,
        out_specs=[at_row(block, d)] * len(outs) + [pl.BlockSpec((8, d), lambda b: (0, 0))],
        out_shape=outs + [shape((8, d), F32)],
        scratch_shapes=back_scratch(d),
        input_output_aliases={len(args) + i: i for i in range(len(before))},
        compiler_params=params(("arbitrary",)),
        cost_estimate=cost(25e9, 15e6),
        name=name,
    )(*args, *before)


def cross_back(block, before, ssg, first_sum, q, k, v, ot, lse, wo, w, gain, kmark, qmark):
    rows, d = first_sum.shape
    act = shape((rows, d), BF)
    specs = [at_row(block, d)] * 5 + [
        at_col(block, d), at_lead(block, 16), whole(wo), whole(w), whole(gain), at_row(block, 128), at_lead(block, HEAD_DIM),
    ]
    args = (ssg, first_sum, q, k, v, ot, lse, wo, w, gain, kmark, qmark)
    return one_back(
        cross_back_kernel, block, before, args, specs, [shape((rows, d), F32), act, act, act], f"cross_back_{block}"
    )


def self_back(block, before, fsg, q, k, v, ot, lse, wo, kmark, qmark):
    rows, d = fsg.shape
    act = shape((rows, d), BF)
    specs = [at_row(block, d)] * 4 + [
        at_col(block, d), at_lead(block, 16), whole(wo), at_row(block, 128), at_lead(block, HEAD_DIM),
    ]
    args = (fsg, q, k, v, ot, lse, wo, kmark, qmark)
    return one_back(self_back_kernel, block, before, args, specs, [act, act, act], f"self_back_{block}")


def cross_weight(dq, dk, dv, low, mem, ot, ssg, sot, fsg, w):
    rows, d = dq.shape
    args = (dq, dk, dv, low, mem, ot, ssg, sot, fsg, w)
    return pl.pallas_call(
        cross_weight_kernel,
        grid=(1,),
        in_specs=[whole(a) for a in args],
        out_specs=[pl.BlockSpec((5, d, d), lambda b: (0, 0, 0)), pl.BlockSpec((rows, d), lambda b: (0, 0))],
        out_shape=[shape((5, d, d), BF), shape((rows, d), F32)],
        compiler_params=params(("arbitrary",)),
        cost_estimate=cost(9e9, 20e6),
        name="cross_weight",
    )(*args)


def self_weight(dq, dk, dv, x):
    rows, d = dq.shape
    args = (dq, dk, dv, x)
    return pl.pallas_call(
        self_weight_kernel,
        grid=(1,),
        in_specs=[whole(a) for a in args],
        out_specs=pl.BlockSpec((3, d, d), lambda b: (0, 0, 0)),
        out_shape=shape((3, d, d), BF),
        compiler_params=params(("arbitrary",)),
        cost_estimate=cost(4e9, 10e6),
        name="self_weight",
    )(*args)


def self_input(fsg, dq, dk, dv, wqk, wv):
    rows, d = fsg.shape
    return pl.pallas_call(
        self_input_kernel,
        grid=(rows // SEQ_MAX,),
        in_specs=[row_block(d)] * 4 + [whole(wqk), whole(wv)],
        out_specs=row_block(d),
        out_shape=shape((rows, d), F32),
        compiler_params=params(("arbitrary",)),
        cost_estimate=cost(4e9, 14e6),
        name="self_input",
    )(fsg, dq, dk, dv, wqk, wv)


def key_marks(seg):
    odd = (seg & 1)[:, None]
    lane = lax.broadcasted_iota(jnp.int32, (seg.shape[0], 128), 1) % HEAD_DIM
    return jnp.where(lane == 0, 1 - odd, jnp.where(lane == 1, odd, 0)).astype(BF)


def query_marks(seg):
    odd = (seg & 1).reshape(-1, 1, SEQ_MAX)
    row = lax.broadcasted_iota(jnp.int32, (odd.shape[0], HEAD_DIM, SEQ_MAX), 1)
    return jnp.where(row == 0, odd, jnp.where(row == 1, 1 - odd, 0)).astype(BF) * (-MASKED)


def pack_small(small1, small2, small3, dbin, devices):
    d = small1.shape[1]
    rows = [
        small1[0], small1[1], small1[2], small2[0], small2[1], small2[2], small2[3], small3[3], small3[0], small2[4],
        small3[4], small3[1], small3[2],
    ]
    part = jnp.stack(rows).reshape(len(rows), devices, d // devices).swapaxes(0, 1).reshape(devices, -1)
    part = jnp.concatenate([part, dbin.reshape(devices, -1)], axis=1)
    return part


def unpack_small(part, own):
    rows = part[: 13 * own].reshape(13, own)
    return rows[0:6], rows[6:9], rows[9:12], part[13 * own :], rows[12]


def take_side(value, axis, index):
    return lax.dynamic_index_in_dim(value, index, axis, keepdims=False)


def add_low(left, right):
    return (left.astype(F32) + right.astype(F32)).astype(BF)


def halve(value, name, axis):
    me = lax.axis_index(name)
    got = lax.ppermute(take_side(value, axis, 1 - me), name, [(0, 1), (1, 0)])
    return add_low(take_side(value, axis, me), got)


class Halving:
    def __init__(self, left, right):
        self.left, self.right = (
            a.reshape(a.shape[0], 2, 2, 4, 2, a.shape[1] // 32, a.shape[2]) for a in (left, right)
        )

    def core(self):
        self.left, self.right = halve(self.left, "c", 2), halve(self.right, "c", 2)

    def first(self):
        self.left, self.right = halve(self.left, "x", 1), halve(self.right, "y", 3)

    def second(self):
        self.left, self.right = halve(self.left, "y", 2), halve(self.right, "x", 1)

    def last(self):
        me = lax.axis_index("z")

        def part(step):
            index = (me + step) % 4
            left, right = take_side(self.left, 1, index), take_side(self.right, 1, index)
            return jnp.stack([left, right.reshape(left.shape)])

        total = part(0).astype(F32)
        for step in range(1, 4):
            got = lax.ppermute(part(step), "z", [(i, (i + step) % 4) for i in range(4)])
            total = total + got.astype(F32)
        shape_r = self.right.shape
        return total[0], total[1].reshape(shape_r[0], *shape_r[2:])


class Whole:
    def __init__(self, left, right):
        self.left, self.right = left, right

    def core(self):
        pass

    first = second = core

    def last(self):
        return [lax.psum_scatter(a, ("dp", "fsdp"), scatter_dimension=1, tiled=True).astype(F32) for a in (self.left, self.right)]


def take_turns(value):
    me = lax.axis_index("z")
    parts = [value]
    for step in range(3, 0, -1):
        parts.append(lax.ppermute(value, "z", [(i, (i + step) % 4) for i in range(4)]))
    return jnp.stack([lax.select_n((j - me) % 4, *parts) for j in range(4)], axis=1)


def take_pair(value, name, axis):
    me = lax.axis_index(name)
    got = lax.ppermute(value, name, [(0, 1), (1, 0)])
    return jnp.stack([jnp.where(me == 0, value, got), jnp.where(me == 0, got, value)], axis=axis)


class Doubling:
    def __init__(self, left, right):
        self.left, self.right = left, right

    def line(self):
        cut = self.left.shape[0]
        if self.left.shape[1:] == self.right.shape[1:]:
            both = take_turns(jnp.concatenate([self.left, self.right]))
            self.left, self.right = both[:cut], both[cut:]
        else:
            rows = self.left.shape[0] * self.left.shape[1]
            flat = jnp.concatenate([a.reshape(1, -1, a.shape[2]) for a in (self.left, self.right)], axis=1)
            both = take_turns(flat)
            r, d = self.left.shape[1:]
            self.left = both[0, :, :rows].reshape(4, cut, r, d).swapaxes(0, 1)
            self.right = both[:, :, rows:]

    def first(self):
        self.left, self.right = take_pair(self.left, "y", 2), take_pair(self.right, "x", 1)

    def second(self):
        self.left, self.right = take_pair(self.left, "x", 1), take_pair(self.right, "y", 3)

    def core(self):
        return take_pair(self.left, "c", 2), take_pair(self.right, "c", 2)


def local_small(bias, gain, shift, bin_, bout):
    return jnp.concatenate([a.reshape(-1) for a in (bias, gain, shift, bout, bin_)])


def spread_small(parts, own):
    parts = parts.astype(F32)
    devices = parts.shape[0]
    rows = parts[:, : 13 * own].reshape(devices, 13, own).swapaxes(0, 1).reshape(13, -1)
    bin_ = parts[:, 13 * own :].reshape(1, -1)
    return {"bias": rows[0:6], "gain": rows[6:9], "shift": rows[9:12], "bout": rows[12:13], "bin": bin_}


def gather_stages(proj, out, small, win, wout):
    _, own, d = proj.shape
    chunks = win.shape[1] // d
    feed_local = jnp.concatenate([win.reshape(own, chunks, d).swapaxes(0, 1), wout.reshape(chunks, own, d)])
    feed_all = lax.all_gather(feed_local, ("x", "c", "z", "y"), axis=1)
    full = {}
    full["win"] = feed_all[:chunks].reshape(chunks, -1, d)
    full["wout"] = feed_all[chunks:].swapaxes(0, 1).reshape(-1, d)
    extra = jnp.pad(small[None, None], ((0, 0), (0, 7), (0, d - small.shape[0])))
    one = Doubling(proj[:2], jnp.concatenate([proj[2:3], extra], axis=1))
    two = Doubling(proj[3:6], out)
    one.line()
    one.first()
    two.line()
    one.second()
    two.first()
    left, right = one.core()
    full["qk"] = left.reshape(2, -1, d)
    full["v"] = right[..., :own, :].reshape(1, -1, d)
    full.update(spread_small(right[..., own, : small.shape[0]].reshape(-1, small.shape[0]), own))
    two.second()
    left, right = two.core()
    full["cross_proj"] = left.reshape(3, -1, d)
    full["out"] = right.reshape(2, -1, d)
    return full


def gather_whole(proj, out, small, win, wout):
    take = functools.partial(lax.all_gather, axis_name=("dp", "fsdp"), tiled=True)
    _, own, d = proj.shape
    proj = take(proj, axis=1)
    win = take(win, axis=0)
    full = {
        "qk": proj[:2], "v": proj[2:3], "cross_proj": proj[3:], "out": take(out, axis=1),
        "win": win.reshape(d, -1, d).swapaxes(0, 1), "wout": take(wout, axis=0),
    }
    full.update(spread_small(take(small[None], axis=0), own))
    return full


def columns(array):
    half = array.shape[2] // 2
    return array[..., :half], array[..., half:]


def after(value, *sums):
    held = lax.optimization_barrier((value, [(s.left, s.right) for s in sums]))
    for s, (s.left, s.right) in zip(sums, held[1]):
        pass
    return held[0]


def body(
    gather, scatter, devices, query, memory, query_seg, memory_seg, attn_proj, attn_out, attn_bias, norm_gain, norm_bias,
    ffn_in, ffn_in_bias, ffn_out, ffn_out_bias, cotangent,
):
    blocks = query.shape[0] // SEQ_MAX
    own = attn_proj.shape[1]
    d = query.shape[1]
    small = local_small(attn_bias, norm_gain, norm_bias, ffn_in_bias, ffn_out_bias)
    full = gather(attn_proj, attn_out, small, ffn_in, ffn_out)
    bias, gain, shift, out, cross_proj = (full[k] for k in ("bias", "gain", "shift", "out", "cross_proj"))
    qmark = query_marks(query_seg)
    smark, cmark = key_marks(query_seg), key_marks(memory_seg)
    sq, sk, sv, sot, slse = self_forward(query, full["qk"], full["v"], bias, smark, qmark)
    first_sum, low, cq, ck, cv, cot_, clse, second_sum = cross_forward(
        query, memory, sot, out, cross_proj, bias, gain, shift, cmark, qmark
    )
    mixed, ssg, dwin, dwout, dbin, small3 = feed(
        second_sum, cotangent, full["win"], full["bin"], full["wout"], full["bout"], gain, shift
    )
    feed_sum = scatter(dwin, dwout[None])
    feed_sum.core()
    grads, small2, upstream = [], 0, ssg
    for block in range(blocks):
        *grads, part = cross_back(
            block, grads, upstream, first_sum, cq, ck, cv, cot_, clse, out[1:2], cross_proj, gain, cmark, qmark
        )
        small2 = small2 + part
        if block == 0:
            upstream = after(upstream, feed_sum)
            feed_sum.first()
    fsg, dq, dk, dv = grads
    cdw, memory_grad = cross_weight(dq, dk, dv, low, memory, cot_, ssg, sot, fsg, cross_proj)
    cross_sum = scatter(*columns(cdw))
    upstream = after(fsg, feed_sum, cross_sum)
    feed_sum.second()
    cross_sum.core()
    grads, small1 = [], 0
    for block in range(blocks):
        *grads, part = self_back(block, grads, upstream, sq, sk, sv, sot, slse, out[0:1], smark, qmark)
        small1 = small1 + part
        if block == 0:
            upstream = after(upstream, feed_sum, cross_sum)
            cross_sum.first()
            dwin, dwout = feed_sum.last()
    dq, dk, dv = grads
    dq = after(dq, cross_sum)
    cross_sum.second()
    sdw = self_weight(dq, dk, dv, query)
    small = pack_small(small1, small2, small3, dbin, devices)
    rows = sdw.reshape(3, devices, own, d).swapaxes(0, 1).reshape(devices, 3 * own, d)
    extra = jnp.pad(small[:, None, :], ((0, 0), (0, 7), (0, d - small.shape[1]))).astype(BF)
    rows = jnp.concatenate([rows, extra], axis=1).reshape(1, -1, d)
    self_sum = scatter(*columns(rows))
    self_sum.core()
    query_grad = self_input(fsg, dq, dk, dv, full["qk"], full["v"])
    self_sum.first()
    cdw = jnp.concatenate(cross_sum.last(), axis=2)
    self_sum.second()
    rows = jnp.concatenate(self_sum.last(), axis=2)[0]
    sdw = rows[: 3 * own].reshape(3, own, d)
    bias_g, gain_g, shift_g, dbin, dbout = unpack_small(rows[3 * own, : small.shape[1]], own)
    return (
        mixed, query_grad, memory_grad, jnp.concatenate([sdw, cdw[:3]]), cdw[4:2:-1], bias_g, gain_g, shift_g,
        dwin.swapaxes(0, 1).reshape(own, -1), dbin, dwout[0], dbout,
    )


def solution(mesh):
    devices = mesh.size
    if dict(mesh.shape) == {"dp": 4, "fsdp": 8}:
        axes = ("x", "c", "z", "y")
        mesh = Mesh(mesh.devices.reshape(2, 2, 4, 2), axes)
        gather, scatter = gather_stages, Halving
    else:
        axes = ("dp", "fsdp")
        gather, scatter = gather_whole, Whole
    rows, mid, flat, row1 = P(axes, None), P(None, axes, None), P(None, axes), P(axes)
    return jax.shard_map(
        functools.partial(body, gather, scatter, devices),
        mesh=mesh,
        in_specs=(rows, rows, row1, row1, mid, mid, flat, flat, flat, rows, row1, rows, row1, rows),
        out_specs=(rows, rows, rows, mid, mid, flat, flat, flat, rows, row1, rows, row1),
        check_vma=False,
    )
```

```python
import functools

import jax
import jax.numpy as jnp
from jax import lax
from jax.experimental import pallas as pl
from jax.experimental.pallas import tpu as pltpu
from jax.sharding import Mesh
from jax.sharding import PartitionSpec as P

HEADS = 12
HEAD_DIM = 64
SEQ_MAX = 512
PAIRS = HEADS // 2
EPSILON = 1e-05
MASKED = 1e30
SCALE = HEAD_DIM ** (-0.5)
BF = jnp.bfloat16
F32 = jnp.float32
VMEM_LIMIT = 60 * 1024 * 1024


def dot(left, right):
    return jnp.dot(left, right, preferred_element_type=F32)


def dot_nt(left, right):
    return lax.dot_general(left, right, (((1,), (1,)), ((), ())), preferred_element_type=F32)


def norm_parts(resid):
    center = resid - jnp.mean(resid, axis=-1, keepdims=True)
    rstd = lax.rsqrt(jnp.mean(center * center, axis=-1, keepdims=True) + EPSILON)
    return center * rstd, rstd


def norm_back(unit, rstd, gain, upstream):
    scaled = upstream * gain
    mean_s = jnp.mean(scaled, axis=-1, keepdims=True)
    mean_su = jnp.mean(scaled * unit, axis=-1, keepdims=True)
    grad = rstd * (scaled - mean_s - unit * mean_su)
    return grad, col_sum(upstream * unit), col_sum(upstream)


def col_sum(rows):
    return jnp.sum(rows, axis=0, keepdims=True)


def place_rows(rows, count):
    parts = list(rows)
    parts.append(jnp.zeros((count - len(parts), parts[0].shape[1]), F32))
    return jnp.concatenate(parts, axis=0)


def gelu_parts(value):
    size = jnp.abs(value) * (0.5**0.5)
    bell = jnp.exp(-0.5 * value * value)
    t = 1.0 / (1.0 + 0.3275911 * size)
    poly = t * (0.254829592 + t * (-0.284496736 + t * (1.421413741 + t * (-1.453152027 + t * 1.061405429))))
    tail = 0.5 * poly * bell
    phi = jnp.where(value >= 0, 1.0 - tail, tail)
    return value * phi, phi + value * (bell * (1.0 / (2.0 * 3.141592653589793) ** 0.5))


def left_half(shape):
    return lax.broadcasted_iota(jnp.int32, shape, 1) < HEAD_DIM


def head_pair(side, pair):
    return pl.ds(pl.multiple_of(pair * 128 + side * HEAD_DIM, HEAD_DIM), HEAD_DIM)


def key_tile(tile, marks, side):
    left = left_half(tile.shape)
    return jnp.where(left, tile, marks) if side == 0 else jnp.where(left, marks, tile)


def query_tile(rows, marks, side):
    return jnp.concatenate([rows, marks] if side == 0 else [marks, rows], axis=0)


def attend_block(k_ref, qt_ref, vt_ref, kmark_ref, qmark_ref, ot_ref, lse_ref):
    kmark = kmark_ref[...]
    qmark = qmark_ref[0]
    ones = jnp.ones((16, SEQ_MAX), BF)

    def one_pair(pair, carry):
        tile = k_ref[:, pl.ds(pl.multiple_of(pair * 128, 128), 128)]
        for side in range(2):
            rows = head_pair(side, pair)
            scores = dot(key_tile(tile, kmark, side), query_tile(qt_ref[rows, :], qmark, side))
            peak = jnp.max(scores, axis=0, keepdims=True)
            weights = jnp.exp(scores - peak).astype(BF)
            result = dot(jnp.concatenate([vt_ref[rows, :], ones], axis=0), weights)
            total = result[HEAD_DIM : HEAD_DIM + 1]
            ot_ref[rows, :] = (result[:HEAD_DIM] * (1.0 / total)).astype(BF)
            lse_ref[0, pl.ds(pair * 2 + side, 1), :] = peak + jnp.log(total)
        return carry

    lax.fori_loop(0, PAIRS, one_pair, 0)


def attend_back_block(
    q_ref, k_ref, v_ref, qt_ref, kt_ref, ot_ref, do_ref, dot_ref, kmark_ref, qmark_ref, lse_ref, dqt_ref, dk_ref, dv_ref
):
    kmark = kmark_ref[...]
    qmark = qmark_ref[0]
    left = left_half((SEQ_MAX, 128))
    blank = jnp.zeros((HEAD_DIM, SEQ_MAX), BF)

    def one_pair(pair, carry):
        cols = pl.ds(pl.multiple_of(pair * 128, 128), 128)
        k_tile, v_tile, q_tile, do_tile = k_ref[:, cols], v_ref[:, cols], q_ref[:, cols], do_ref[:, cols]
        value_grads, key_grads = [], []
        for side in range(2):
            rows = head_pair(side, pair)
            scores = dot(key_tile(k_tile, kmark, side), query_tile(qt_ref[rows, :], qmark, side))
            probs = jnp.exp(scores - lse_ref[0, pl.ds(pair * 2 + side, 1), :])
            value_grads.append(dot(probs.astype(BF), do_tile))
            up = dot_ref[rows, :]
            center = col_sum(up.astype(F32) * ot_ref[rows, :].astype(F32))
            probs_grad = dot(v_tile, query_tile(up, blank, side))
            score_grad = (probs * (probs_grad - center)).astype(BF)
            key_grads.append(dot(score_grad, q_tile))
            dqt_ref[rows, :] = (dot(kt_ref[rows, :], score_grad) * SCALE).astype(BF)
        dv_ref[:, cols] = jnp.where(left, value_grads[0], value_grads[1]).astype(BF)
        dk_ref[:, cols] = jnp.where(left, key_grads[0], key_grads[1]).astype(BF)
        return carry

    lax.fori_loop(0, PAIRS, one_pair, 0)


def self_forward_kernel(
    x_ref, wqk_ref, wv_ref, bias_ref, kmark_ref, qmark_ref, q_ref, k_ref, v_ref, ot_ref, lse_ref, qt_s, vt_s
):
    x = x_ref[...]
    queries = ((dot(x, wqk_ref[0]) + bias_ref[0:1]).astype(BF)) * SCALE
    q_ref[...] = queries
    qt_s[...] = queries.T
    k_ref[...] = dot(x, wqk_ref[1]).astype(BF)
    values = (dot(x, wv_ref[0]) + bias_ref[1:2]).astype(BF)
    v_ref[...] = values
    vt_s[...] = values.T
    attend_block(k_ref, qt_s, vt_s, kmark_ref, qmark_ref, ot_ref, lse_ref)


def cross_forward_kernel(
    x_ref, mem_ref, sot_ref, wo_ref, w_ref, bias_ref, gain_ref, shift_ref, kmark_ref, qmark_ref,
    first_sum_ref, low_ref, q_ref, k_ref, v_ref, ot_ref, lse_ref, second_sum_ref, qt_s, vt_s,
):
    mem = mem_ref[...]
    k_ref[...] = dot(mem, w_ref[1]).astype(BF)
    values = (dot(mem, w_ref[2]) + bias_ref[4:5]).astype(BF)
    v_ref[...] = values
    vt_s[...] = values.T
    first_sum = x_ref[...].astype(F32) + (dot(sot_ref[...].T, wo_ref[0]) + bias_ref[2:3])
    first_sum_ref[...] = first_sum
    unit, _ = norm_parts(first_sum)
    first = unit * gain_ref[0:1] + shift_ref[0:1]
    low = first.astype(BF)
    low_ref[...] = low
    queries = ((dot(low, w_ref[0]) + bias_ref[3:4]).astype(BF)) * SCALE
    q_ref[...] = queries
    qt_s[...] = queries.T
    attend_block(k_ref, qt_s, vt_s, kmark_ref, qmark_ref, ot_ref, lse_ref)
    second_sum_ref[...] = first + (dot(ot_ref[...].T, wo_ref[1]) + bias_ref[5:6])


def feed_kernel(
    own, ss_ref, cot_ref, win_ref, bin_ref, wout_ref, bout_ref, gain_ref, shift_ref,
    mixed_ref, ssg_ref, dw_ref, dbin_ref, small_ref,
    low_s, lowt_s, hid_s, slope_s, acc_s, z_s, din_s, dout_s, sems,
):
    phase, chunk = pl.program_id(0), pl.program_id(1)
    chunks = pl.num_programs(1)
    last = chunks - 1
    slot = chunk % 2
    width, d = dout_s.shape[1] * dout_s.shape[2], dout_s.shape[3]
    parts = dout_s.shape[1]

    def wout():
        if not own:
            return wout_ref[...]
        groups = wout_ref[...].astype(F32)
        return jnp.concatenate([groups[:, i] for i in range(groups.shape[1])], axis=0).reshape(width, d).astype(BF)

    def sends(slot, chunk):
        if own:
            group = width // parts
            rows = pl.ds(pl.multiple_of(chunk * group, group), group)
            outs = [
                pltpu.make_async_copy(
                    dout_s.at[slot, part], dw_ref.at[rows, pl.ds((chunks + part) * width, width)], sems.at[1 + part, slot]
                )
                for part in range(parts)
            ]
        else:
            cols = pl.ds(pl.multiple_of((chunks + chunk) * width, width), width)
            outs = [pltpu.make_async_copy(dout_s.at[slot, 0], dw_ref.at[:, cols], sems.at[1, slot])]
        cols = pl.ds(pl.multiple_of(chunk * width, width), width)
        return [pltpu.make_async_copy(din_s.at[slot], dw_ref.at[:, cols], sems.at[0, slot])] + outs

    @pl.when((phase == 0) & (chunk == 0))
    def _():
        unit, _ = norm_parts(ss_ref[...])
        second = unit * gain_ref[1:2] + shift_ref[1:2]
        low = second.astype(BF)
        low_s[...] = low
        lowt_s[...] = low.T
        acc_s[...] = second + bout_ref[...]

    @pl.when(phase == 0)
    def _():
        pre = dot(low_s[...], win_ref[0]) + bin_ref[...]
        hidden, slope = gelu_parts(pre)
        hidden = hidden.astype(BF)
        hid_s[chunk] = hidden
        slope_s[chunk] = slope
        acc_s[...] += dot(hidden, wout())

    @pl.when((phase == 1) & (chunk == 0))
    def _():
        unit, rstd = norm_parts(acc_s[...])
        mixed_ref[...] = (unit * gain_ref[2:3] + shift_ref[2:3]).astype(BF)
        third, dgain, dshift = norm_back(unit, rstd, gain_ref[2:3], cot_ref[...].astype(F32))
        z = third.astype(BF)
        z_s[...] = z
        acc_s[...] = third
        small_ref[...] = place_rows([dgain, dshift, col_sum(z.astype(F32))], 8)

    @pl.when((phase == 1) & (chunk >= 2))
    def _():
        for copy in sends(slot, chunk - 2):
            copy.wait()

    @pl.when(phase == 1)
    def _():
        z = z_s[...]
        pre_grad = (dot_nt(z, wout()) * slope_s[chunk]).astype(BF)
        dbin_ref[...] = col_sum(pre_grad.astype(F32))
        dout = dot(hid_s[chunk].T, z)
        if own:
            groups = dout.reshape(width // (parts * own), parts, own, d)
            for part in range(parts):
                dout_s[slot, part] = groups[:, part].reshape(width // parts, d).astype(BF)
        else:
            dout_s[slot] = dout.reshape(dout_s.shape[1:]).astype(BF)
        din_s[slot] = dot(lowt_s[...], pre_grad).astype(BF)
        for copy in sends(slot, chunk):
            copy.start()
        acc_s[...] += dot_nt(pre_grad, win_ref[0])

    @pl.when((phase == 1) & (chunk == last))
    def _():
        unit, rstd = norm_parts(ss_ref[...])
        grad, dgain, dshift = norm_back(unit, rstd, gain_ref[1:2], acc_s[...])
        ssg_ref[...] = grad
        small_ref[3:5] = jnp.concatenate([dgain, dshift], axis=0)
        for copy in sends(1 - slot, chunk - 1) + sends(slot, chunk):
            copy.wait()


def cross_back_kernel(
    ssg_ref, fs_ref, q_ref, k_ref, v_ref, ot_ref, lse_ref, wo_ref, w_ref, gain_ref, kmark_ref, qmark_ref, *refs
):
    fsg_ref, dq_ref, dk_ref, dv_ref, small_ref, qt_s, kt_s, do_s, dot_s, dqt_s = refs[-10:]
    upstream = ssg_ref[...]
    branch = upstream.astype(BF)
    mixed_grad = dot_nt(branch, wo_ref[0]).astype(BF)
    do_s[...] = mixed_grad
    dot_s[...] = mixed_grad.T
    qt_s[...] = q_ref[...].T
    kt_s[...] = k_ref[...].T
    attend_back_block(
        q_ref, k_ref, v_ref, qt_s, kt_s, ot_ref, do_s, dot_s, kmark_ref, qmark_ref, lse_ref, dqt_s, dk_ref, dv_ref
    )
    dq = dqt_s[...].T
    dq_ref[...] = dq
    first_grad = upstream + dot_nt(dq, w_ref[0])
    unit, rstd = norm_parts(fs_ref[...])
    grad, dgain, dshift = norm_back(unit, rstd, gain_ref[0:1], first_grad)
    fsg_ref[...] = grad
    sums = [col_sum(dq.astype(F32)), col_sum(dv_ref[...].astype(F32)), col_sum(branch.astype(F32)), dgain, dshift]
    small_ref[...] = place_rows(sums, 8)


def self_back_kernel(fsg_ref, q_ref, k_ref, v_ref, ot_ref, lse_ref, wo_ref, kmark_ref, qmark_ref, *refs):
    dq_ref, dk_ref, dv_ref, small_ref, qt_s, kt_s, do_s, dot_s, dqt_s = refs[-9:]
    branch = fsg_ref[...].astype(BF)
    mixed_grad = dot_nt(branch, wo_ref[0]).astype(BF)
    do_s[...] = mixed_grad
    dot_s[...] = mixed_grad.T
    qt_s[...] = q_ref[...].T
    kt_s[...] = k_ref[...].T
    attend_back_block(
        q_ref, k_ref, v_ref, qt_s, kt_s, ot_ref, do_s, dot_s, kmark_ref, qmark_ref, lse_ref, dqt_s, dk_ref, dv_ref
    )
    dq = dqt_s[...].T
    dq_ref[...] = dq
    sums = [col_sum(dq.astype(F32)), col_sum(dv_ref[...].astype(F32)), col_sum(branch.astype(F32))]
    small_ref[...] = place_rows(sums, 8)


def bring(sources, slots, sems):
    copies = [pltpu.make_async_copy(s, v, sems.at[i]) for i, (s, v) in enumerate(zip(sources, slots))]
    for copy in copies:
        copy.start()

    def get(i):
        copies[i].wait()
        return slots[i][...]

    return get


def split_out(grads, me, keep_ref, send_ref, small=None):
    places = keep_ref.shape[1] * keep_ref.shape[2]
    own = grads[0].shape[0] // (4 * places)
    for x in range(2):
        cores = []
        for core in range(2):
            rows = pl.ds((2 * x + core) * places * own, places * own)
            parts = [g[rows, :].reshape(places, own, g.shape[1]) for g in grads]
            if small is not None:
                parts.append(small(x, core))
            cores.append(jnp.concatenate(parts, axis=1))
        mine = me == 0
        block = keep_ref.shape[1:]
        keep_ref[x] = jnp.where(mine, cores[0], cores[1]).astype(BF).reshape(block)
        send_ref[x] = jnp.where(mine, cores[1], cores[0]).astype(BF).reshape(block)


def cross_weight_kernel(staged, me_ref, *refs):
    sources, (keep_ref, send_ref, mg_ref), slots = refs[:10], refs[10:13], refs[13:23]
    dw_s, mg_s, sems, out_sem = refs[23:]
    get = bring(sources, slots, sems)
    memt = get(0).T
    dk = get(1)
    dw_s[3] = dot(memt, dk)
    dv = get(2)
    dw_s[4] = dot(memt, dv)
    get(3)
    w_s = slots[3]
    mg_s[...] = dot_nt(dk, w_s[1]) + dot_nt(dv, w_s[2])
    move = pltpu.make_async_copy(mg_s, mg_ref, out_sem)
    move.start()
    dw_s[0] = dot(get(4), get(5).astype(BF))
    dw_s[1] = dot(get(6), get(7).astype(BF))
    dw_s[2] = dot(get(8).T, get(9))
    if staged:
        split_out([dw_s.at[i] for i in range(5)], me_ref[0], keep_ref, send_ref)
    else:
        keep_ref[...] = dw_s[...].astype(BF)
        send_ref[...] = jnp.zeros(send_ref.shape, BF)
    move.wait()


def self_weight_kernel(staged, me_ref, small_ref, dbin_ref, x_ref, dq_ref, dk_ref, dv_ref, keep_ref, send_ref, *scratch):
    dw_s, sems = scratch[4:]
    get = bring((x_ref, dq_ref, dk_ref, dv_ref), scratch[:4], sems)
    xt = get(0).T
    for i in range(3):
        dw_s[i] = dot(xt, get(i + 1))
    if not staged:
        keep_ref[...] = dw_s[...].astype(BF)
        send_ref[...] = jnp.zeros(send_ref.shape, BF)
        return
    d = small_ref.shape[1]
    places = keep_ref.shape[1] * keep_ref.shape[2]
    own = d // (4 * places)
    wide = dbin_ref.shape[1]

    lines = jnp.broadcast_to(dbin_ref[...], (8, wide))

    def small(x, core):
        out = []
        for place in range(places):
            device = (2 * x + core) * places + place
            rows, line = small_ref[...], lines
            if device:
                rows = pltpu.roll(rows, d - own * device, 1)
                line = pltpu.roll(lines, wide - wide // (4 * places) * device, 1)
            out.append(jnp.concatenate([rows, line[:, :d]], axis=0))
        return jnp.stack(out)

    split_out([dw_s.at[i] for i in range(3)], me_ref[0], keep_ref, send_ref, small)


def self_input_kernel(fsg_ref, dq_ref, dk_ref, dv_ref, wqk_ref, wv_ref, qg_ref):
    qg_ref[...] = (
        fsg_ref[...]
        + dot_nt(dq_ref[...], wqk_ref[0]) + dot_nt(dk_ref[...], wqk_ref[1]) + dot_nt(dv_ref[...], wv_ref[0])
    )


def pick(first, second, other):
    return jnp.where(other == 0, first, second)


def first_stage_kernel(me_ref, keep_ref, got_ref, sl_ref, kl_ref, sr_ref, kr_ref):
    total = keep_ref[...].astype(F32) + got_ref[...].astype(F32)
    half = total.shape[4] // 2
    left, right = total[..., :half], total[..., half:]
    sl_ref[...] = pick(left[1], left[0], me_ref[0]).astype(BF)
    kl_ref[...] = pick(left[0], left[1], me_ref[0]).astype(BF)
    sr_ref[...] = pick(right[:, :, 1], right[:, :, 0], me_ref[1]).astype(BF)
    kr_ref[...] = pick(right[:, :, 0], right[:, :, 1], me_ref[1]).astype(BF)


def second_stage_kernel(me_ref, kl_ref, gl_ref, kr_ref, gr_ref, sl_ref, ml_ref, sr_ref, mr_ref):
    left = kl_ref[...].astype(F32) + gl_ref[...].astype(F32)
    right = kr_ref[...].astype(F32) + gr_ref[...].astype(F32)
    sl_ref[...] = pick(left[:, 1], left[:, 0], me_ref[1]).astype(BF)
    ml_ref[...] = pick(left[:, 0], left[:, 1], me_ref[1]).astype(BF)
    sr_ref[...] = pick(right[1], right[0], me_ref[0]).astype(BF)
    mr_ref[...] = pick(right[0], right[1], me_ref[0]).astype(BF)


def third_stage_kernel(me_ref, kl_ref, gl_ref, kr_ref, gr_ref, own_ref, *outs):
    total = jnp.concatenate(
        [kl_ref[...].astype(F32) + gl_ref[...].astype(F32), kr_ref[...].astype(F32) + gr_ref[...].astype(F32)], axis=2
    )
    me = me_ref[2]
    for step, ref in enumerate((own_ref, *outs)):
        index = (me + step) % 4
        value = jnp.where(
            index < 2, jnp.where(index == 0, total[0], total[1]), jnp.where(index == 2, total[2], total[3])
        )
        ref[...] = value.astype(ref.dtype)


def stage_call(kernel, me, args, outs, name):
    data = sum(a.size * a.dtype.itemsize for a in args)
    return pl.pallas_call(
        kernel,
        in_specs=[pl.BlockSpec(memory_space=pltpu.SMEM)] + [pl.BlockSpec(memory_space=pltpu.VMEM)] * len(args),
        out_specs=[pl.BlockSpec(memory_space=pltpu.VMEM)] * len(outs),
        out_shape=outs,
        compiler_params=pltpu.CompilerParams(vmem_limit_bytes=VMEM_LIMIT),
        cost_estimate=cost(data, 2 * data),
        name=name,
    )(me, *args)


def first_stage(me, keep, got):
    x, z, y, rows, d = keep.shape
    line = lambda *lead: pl.BlockSpec((*lead, rows, d // 2), lambda i: (i, 0, 0, 0))
    both = pl.BlockSpec((x, 1, y, rows, d), lambda i: (0, i, 0, 0, 0))
    side = pl.BlockSpec((x, 1, rows, d // 2), lambda i: (0, i, 0, 0))
    left, right = shape((z, y, rows, d // 2), BF), shape((x, z, rows, d // 2), BF)
    return pl.pallas_call(
        first_stage_kernel,
        grid=(z,),
        in_specs=[pl.BlockSpec(memory_space=pltpu.SMEM), both, both],
        out_specs=[line(1, y), line(1, y), side, side],
        out_shape=[left, left, right, right],
        compiler_params=params(("arbitrary",)),
        cost_estimate=cost(keep.size, 6 * keep.size),
        name="first_stage",
    )(me, keep, got)


def row_block(width):
    return pl.BlockSpec((SEQ_MAX, width), lambda b: (b, 0))


def col_block(height):
    return pl.BlockSpec((height, SEQ_MAX), lambda b: (0, b))


def lead_block(rows):
    return pl.BlockSpec((1, rows, SEQ_MAX), lambda b: (b, 0, 0))


def whole(array, **kw):
    zeros = (0,) * array.ndim
    return pl.BlockSpec(array.shape, lambda *_: zeros, pipeline_mode=pl.Buffered(1))


def plane(array, index):
    return pl.BlockSpec((1, *array.shape[1:]), lambda *_: (index, 0, 0), pipeline_mode=pl.Buffered(1))


def params(semantics):
    return pltpu.CompilerParams(vmem_limit_bytes=VMEM_LIMIT, dimension_semantics=semantics)


def cost(flops, data, exps=0):
    return pl.CostEstimate(flops=int(flops), bytes_accessed=int(data), transcendentals=int(exps))


def shape(dims, kind):
    return jax.ShapeDtypeStruct(dims, kind)


def self_forward(x, wqk, wv, bias, kmark, qmark):
    rows, d = x.shape
    blocks = rows // SEQ_MAX
    act = shape((rows, d), BF)
    return pl.pallas_call(
        self_forward_kernel,
        grid=(blocks,),
        in_specs=[row_block(d), whole(wqk), whole(wv), whole(bias), row_block(128), lead_block(HEAD_DIM)],
        out_specs=[row_block(d), row_block(d), row_block(d), col_block(d), lead_block(16)],
        out_shape=[act, act, act, shape((d, rows), BF), shape((blocks, 16, SEQ_MAX), F32)],
        scratch_shapes=[pltpu.VMEM((d, SEQ_MAX), BF)] * 2,
        compiler_params=params(("arbitrary",)),
        cost_estimate=cost(20e9, 12e6),
        name="self_forward",
    )(x, wqk, wv, bias, kmark, qmark)


def cross_forward(x, mem, sot, wo, w, bias, gain, shift, kmark, qmark):
    rows, d = x.shape
    blocks = rows // SEQ_MAX
    act, wide = shape((rows, d), BF), shape((rows, d), F32)
    return pl.pallas_call(
        cross_forward_kernel,
        grid=(blocks,),
        in_specs=[
            row_block(d), row_block(d), col_block(d), whole(wo), whole(w), whole(bias), whole(gain), whole(shift),
            row_block(128), lead_block(HEAD_DIM),
        ],
        out_specs=[row_block(d)] * 5 + [col_block(d), lead_block(16), row_block(d)],
        out_shape=[wide, act, act, act, act, shape((d, rows), BF), shape((blocks, 16, SEQ_MAX), F32), wide],
        scratch_shapes=[pltpu.VMEM((d, SEQ_MAX), BF)] * 2,
        compiler_params=params(("arbitrary",)),
        cost_estimate=cost(24e9, 20e6),
        name="cross_forward",
    )(x, mem, sot, wo, w, bias, gain, shift, kmark, qmark)


def feed(second_sum, cot, win, bin_, wout, bout, gain, shift):
    rows, d = second_sum.shape
    width = win.shape[2]
    ff = bin_.shape[1]
    chunks = ff // width
    own = wout.shape[2] if wout.ndim == 4 else 0
    fixed = lambda p, j: (0, 0)
    parts = chunks if own else 1
    if own:
        wout_spec = pl.BlockSpec((parts, width // (parts * own), own, d), lambda p, j: (1, j, 0, 0))
    else:
        wout_spec = pl.BlockSpec((width, d), lambda p, j: (j, 0))
    return pl.pallas_call(
        functools.partial(feed_kernel, own),
        grid=(2, chunks),
        in_specs=[
            whole(second_sum), whole(cot),
            pl.BlockSpec((1, d, width), lambda p, j: (j, 0, 0)),
            pl.BlockSpec((1, width), lambda p, j: (0, j)),
            wout_spec, whole(bout), whole(gain), whole(shift),
        ],
        out_specs=[
            pl.BlockSpec((rows, d), fixed),
            pl.BlockSpec((rows, d), fixed),
            pl.BlockSpec(memory_space=pl.ANY),
            pl.BlockSpec((1, width), lambda p, j: (0, j * p)),
            pl.BlockSpec((8, d), fixed),
        ],
        out_shape=[
            shape((rows, d), BF), shape((rows, d), F32), shape((d, 2 * ff), BF),
            shape((1, ff), F32), shape((8, d), F32),
        ],
        scratch_shapes=[
            pltpu.VMEM((rows, d), BF), pltpu.VMEM((d, rows), BF),
            pltpu.VMEM((chunks, rows, width), BF), pltpu.VMEM((chunks, rows, width), F32),
            pltpu.VMEM((rows, d), F32), pltpu.VMEM((rows, d), BF),
            pltpu.VMEM((2, d, width), BF), pltpu.VMEM((2, parts, width // parts, d), BF),
            pltpu.SemaphoreType.DMA((1 + parts, 2)),
        ],
        compiler_params=params(("arbitrary", "arbitrary")),
        cost_estimate=cost(40e9, 40e6),
        name="feed",
    )(second_sum, cot, win, bin_, wout, bout, gain, shift)


def back_scratch(d):
    return (
        [pltpu.VMEM((d, SEQ_MAX), BF)] * 2 + [pltpu.VMEM((SEQ_MAX, d), BF)] + [pltpu.VMEM((d, SEQ_MAX), BF)] * 2
    )


def at_row(block, width):
    return pl.BlockSpec((SEQ_MAX, width), lambda b: (block, 0))


def at_col(block, height):
    return pl.BlockSpec((height, SEQ_MAX), lambda b: (0, block))


def at_lead(block, rows):
    return pl.BlockSpec((1, rows, SEQ_MAX), lambda b: (block, 0, 0))


def one_back(kernel, block, before, args, specs, outs, name):
    d = outs[0].shape[1]
    kept = [pl.BlockSpec(memory_space=pl.ANY)] * len(before)
    return pl.pallas_call(
        kernel,
        grid=(1,),
        in_specs=specs + kept,
        out_specs=[at_row(block, d)] * len(outs) + [pl.BlockSpec((8, d), lambda b: (0, 0))],
        out_shape=outs + [shape((8, d), F32)],
        scratch_shapes=back_scratch(d),
        input_output_aliases={len(args) + i: i for i in range(len(before))},
        compiler_params=params(("arbitrary",)),
        cost_estimate=cost(25e9, 15e6),
        name=name,
    )(*args, *before)


def cross_back(block, before, ssg, first_sum, q, k, v, ot, lse, wo, w, gain, kmark, qmark):
    rows, d = first_sum.shape
    act = shape((rows, d), BF)
    specs = [at_row(block, d)] * 5 + [
        at_col(block, d), at_lead(block, 16), plane(wo, 1), plane(w, 0), whole(gain), at_row(block, 128), at_lead(block, HEAD_DIM),
    ]
    args = (ssg, first_sum, q, k, v, ot, lse, wo, w, gain, kmark, qmark)
    return one_back(
        cross_back_kernel, block, before, args, specs, [shape((rows, d), F32), act, act, act], f"cross_back_{block}"
    )


def self_back(block, before, fsg, q, k, v, ot, lse, wo, kmark, qmark):
    rows, d = fsg.shape
    act = shape((rows, d), BF)
    specs = [at_row(block, d)] * 4 + [
        at_col(block, d), at_lead(block, 16), plane(wo, 0), at_row(block, 128), at_lead(block, HEAD_DIM),
    ]
    args = (fsg, q, k, v, ot, lse, wo, kmark, qmark)
    return one_back(self_back_kernel, block, before, args, specs, [act, act, act], f"self_back_{block}")


def weight_outs(staged, count, extra, devices, d):
    if not staged:
        return [shape((count, d, d), BF), shape((8, 128), BF)]
    half = shape((2, 4, 2, count * d // devices + extra, d), BF)
    return [half, half]


def cross_weight(staged, me, devices, dq, dk, dv, low, mem, ot, ssg, sot, fsg, w):
    rows, d = dq.shape
    args = (mem, dk, dv, w, ot, ssg, sot, fsg, low, dq)
    anywhere, here = pl.BlockSpec(memory_space=pl.ANY), pl.BlockSpec(memory_space=pltpu.VMEM)
    return pl.pallas_call(
        functools.partial(cross_weight_kernel, staged),
        in_specs=[pl.BlockSpec(memory_space=pltpu.SMEM)] + [anywhere] * 10,
        out_specs=[here, here, anywhere],
        out_shape=weight_outs(staged, 5, 0, devices, d) + [shape((rows, d), F32)],
        scratch_shapes=[pltpu.VMEM(a.shape, a.dtype) for a in args] + [
            pltpu.VMEM((5, d, d), F32), pltpu.VMEM((rows, d), F32), pltpu.SemaphoreType.DMA((10,)),
            pltpu.SemaphoreType.DMA,
        ],
        compiler_params=pltpu.CompilerParams(vmem_limit_bytes=VMEM_LIMIT),
        cost_estimate=cost(9e9, 20e6),
        name="cross_weight",
    )(me, *args)


def self_weight(staged, me, devices, small, dbin, dq, dk, dv, x):
    rows, d = dq.shape
    args = (x, dq, dk, dv)
    anywhere, here = pl.BlockSpec(memory_space=pl.ANY), pl.BlockSpec(memory_space=pltpu.VMEM)
    return pl.pallas_call(
        functools.partial(self_weight_kernel, staged),
        in_specs=[pl.BlockSpec(memory_space=pltpu.SMEM), here, here] + [anywhere] * 4,
        out_specs=[here, here],
        out_shape=weight_outs(staged, 3, 32, devices, d),
        scratch_shapes=[pltpu.VMEM(a.shape, a.dtype) for a in args] + [
            pltpu.VMEM((3, d, d), F32), pltpu.SemaphoreType.DMA((4,)),
        ],
        compiler_params=pltpu.CompilerParams(vmem_limit_bytes=VMEM_LIMIT),
        cost_estimate=cost(4e9, 10e6),
        name="self_weight",
    )(me, small, dbin, *args)


def self_input(fsg, dq, dk, dv, wqk, wv):
    rows, d = fsg.shape
    return pl.pallas_call(
        self_input_kernel,
        grid=(rows // SEQ_MAX,),
        in_specs=[row_block(d)] * 4 + [whole(wqk), whole(wv)],
        out_specs=row_block(d),
        out_shape=shape((rows, d), F32),
        compiler_params=params(("arbitrary",)),
        cost_estimate=cost(4e9, 14e6),
        name="self_input",
    )(fsg, dq, dk, dv, wqk, wv)


def key_marks(seg):
    odd = (seg & 1)[:, None]
    lane = lax.broadcasted_iota(jnp.int32, (seg.shape[0], 128), 1) % HEAD_DIM
    return jnp.where(lane == 0, 1 - odd, jnp.where(lane == 1, odd, 0)).astype(BF)


def query_marks(seg):
    odd = (seg & 1).reshape(-1, 1, SEQ_MAX)
    row = lax.broadcasted_iota(jnp.int32, (odd.shape[0], HEAD_DIM, SEQ_MAX), 1)
    return jnp.where(row == 0, odd, jnp.where(row == 1, 1 - odd, 0)).astype(BF) * (-MASKED)


def swap(value, name):
    return lax.ppermute(value, name, [(0, 1), (1, 0)])


class Halving:
    def __init__(self, me, keep, send):
        self.me, self.keep, self.out = me, [keep], [send]

    def core(self):
        got = swap(self.out[0], "c")
        sl, kl, sr, kr = first_stage(self.me, self.keep[0], got)
        self.keep, self.out = [kl, kr], [sl, sr]

    def first(self):
        (kl, kr), (sl, sr) = self.keep, self.out
        gl, gr = swap(sl, "x"), swap(sr, "y")
        z, _, rows, half = kl.shape
        piece = shape((z, rows, half), BF)
        sl, ml, sr, mr = stage_call(second_stage_kernel, self.me, (kl, gl, kr, gr), [piece] * 4, "second_stage")
        self.keep, self.out = [ml, mr], [sl, sr]

    def second(self):
        (kl, kr), (sl, sr) = self.keep, self.out
        gl, gr = swap(sl, "y"), swap(sr, "x")
        _, rows, half = kl.shape
        piece = (rows, 2 * half)
        outs = [shape(piece, F32)] + [shape(piece, BF)] * 3
        own, *self.out = stage_call(third_stage_kernel, self.me, (kl, gl, kr, gr), outs, "third_stage")
        self.keep = [own]

    def last(self):
        total = self.keep[0]
        for step, out in zip(range(1, 4), self.out):
            total = total + lax.ppermute(out, "z", [(i, (i + step) % 4) for i in range(4)]).astype(F32)
        return total

    @staticmethod
    def feed(grads, own):
        sums = lax.psum_scatter(grads, ("x", "c", "z", "y"), scatter_dimension=0, tiled=True).astype(F32)
        half = sums.shape[1] // 2
        d = grads.shape[0]
        return sums[:, :half], sums[:, half:].reshape(own, -1, d).swapaxes(0, 1).reshape(-1, d)


class Whole:
    def __init__(self, me, grads, _):
        self.grads, self.out = grads, ()

    def core(self):
        pass

    first = second = core

    def last(self):
        sums = lax.psum_scatter(self.grads, ("dp", "fsdp"), scatter_dimension=1, tiled=True).astype(F32)
        return sums.reshape(-1, sums.shape[2])

    @staticmethod
    def feed(grads, own):
        sum_up = functools.partial(lax.psum_scatter, axis_name=("dp", "fsdp"), scatter_dimension=0, tiled=True)
        half, d = grads.shape[1] // 2, grads.shape[0]
        dwin = sum_up(grads[:, :half]).astype(F32)
        return dwin, sum_up(grads[:, half:].reshape(d, -1, d).swapaxes(0, 1).reshape(-1, d)).astype(F32)


def after(value, *sums):
    value, outs = lax.optimization_barrier((value, [s.out for s in sums]))
    for s, s.out in zip(sums, outs):
        pass
    return value


def take_turns(value):
    me = lax.axis_index("z")
    parts = [value]
    for step in range(3, 0, -1):
        parts.append(lax.ppermute(value, "z", [(i, (i + step) % 4) for i in range(4)]))
    return jnp.stack([lax.select_n((j - me) % 4, *parts) for j in range(4)], axis=1)


def take_pair(value, name, axis):
    me = lax.axis_index(name)
    got = lax.ppermute(value, name, [(0, 1), (1, 0)])
    return jnp.stack([jnp.where(me == 0, value, got), jnp.where(me == 0, got, value)], axis=axis)


class Doubling:
    def __init__(self, left, right):
        self.cut, self.rows = left.shape[0], left.shape[1]
        self.flat = left.shape[1:] != right.shape[1:]
        if self.flat:
            left, right = (a.reshape(1, -1, a.shape[2]) for a in (left, right))
            self.out = [jnp.concatenate([left, right], axis=1)]
            self.split = left.shape[1]
        else:
            self.out = [jnp.concatenate([left, right])]

    def line(self):
        both = take_turns(self.out[0])
        if self.flat:
            d = both.shape[3]
            left = both[0, :, : self.split].reshape(4, self.cut, self.rows, d).swapaxes(0, 1)
            self.out = [left, both[:, :, self.split :]]
        else:
            self.out = [both[: self.cut], both[self.cut :]]

    def first(self):
        self.out = [take_pair(self.out[0], "y", 2), take_pair(self.out[1], "x", 1)]

    def second(self):
        self.out = [take_pair(self.out[0], "x", 1), take_pair(self.out[1], "y", 3)]

    def core(self):
        self.out = [take_pair(self.out[0], "c", 2), take_pair(self.out[1], "c", 2)]
        return self.out


def local_small(bias, gain, shift, bin_, bout):
    return jnp.concatenate([a.reshape(-1) for a in (bias, gain, shift, bout, bin_)])


def spread_small(parts, own):
    parts = parts.astype(F32)
    devices = parts.shape[0]
    rows = parts[:, : 13 * own].reshape(devices, 13, own).swapaxes(0, 1).reshape(13, -1)
    bin_ = parts[:, 13 * own :].reshape(1, -1)
    return {"bias": rows[0:6], "gain": rows[6:9], "shift": rows[9:12], "bout": rows[12:13], "bin": bin_}


def behind(later, earlier):
    later.out = lax.optimization_barrier((later.out, earlier.out))[0]


class Stages:
    def __init__(self, proj, out, small, win, wout):
        _, own, d = proj.shape
        self.chunks = win.shape[1] // d
        feed_local = jnp.concatenate([win.reshape(own, self.chunks, d).swapaxes(0, 1), wout.reshape(self.chunks, own, d)])
        self.feed_all = lax.all_gather(feed_local, ("x", "c", "z", "y"), axis=1)
        extra = jnp.pad(small[None, None], ((0, 0), (0, 7), (0, d - small.shape[0])))
        self.one = Doubling(proj[:2], jnp.concatenate([proj[2:3], extra], axis=1))
        self.two = Doubling(proj[3:6], out)
        self.own, self.cut, self.d = own, small.shape[0], d

    def begin(self, value):
        one, two, own, d = self.one, self.two, self.own, self.d
        one.line()
        behind(two, one)
        one.first()
        two.line()
        one.second()
        behind(two, one)
        two.first()
        left, right = one.core()
        full = {"qk": left.reshape(2, -1, d), "v": right[..., :own, :].reshape(1, -1, d)}
        full.update(spread_small(right[..., own, : self.cut].reshape(-1, self.cut), own))
        value = after(value, two)
        two.second()
        return full, value

    def finish(self, value):
        two, d = self.two, self.d
        value = after(value, two)
        left, right = two.core()
        shape_f = (2 * self.chunks, -1, d)
        return {
            "cross_proj": left.reshape(3, -1, d), "out": right.reshape(2, -1, d),
            "win": self.feed_all.reshape(shape_f), "wout": self.feed_all,
        }, value


class Plain:
    def __init__(self, proj, out, small, win, wout):
        take = functools.partial(lax.all_gather, axis_name=("dp", "fsdp"), tiled=True)
        _, own, d = proj.shape
        proj = take(proj, axis=1)
        self.full = {"qk": proj[:2], "v": proj[2:3]}
        self.full.update(spread_small(take(small[None], axis=0), own))
        win = take(win, axis=0).reshape(d, -1, d).swapaxes(0, 1)
        self.rest = {"cross_proj": proj[3:], "out": take(out, axis=1), "win": win, "wout": take(wout, axis=0)}

    def begin(self, value):
        return self.full, value

    def finish(self, value):
        return self.rest, value


def body(
    gather, scatter, devices, query, memory, query_seg, memory_seg, attn_proj, attn_out, attn_bias, norm_gain, norm_bias,
    ffn_in, ffn_in_bias, ffn_out, ffn_out_bias, cotangent,
):
    blocks = range(query.shape[0] // SEQ_MAX)
    own = attn_proj.shape[1]
    d = query.shape[1]
    staged = scatter is Halving
    me, pair = jnp.zeros((3,), jnp.int32), jnp.zeros((1,), jnp.int32)
    if staged:
        me = jnp.stack([lax.axis_index(name) for name in ("x", "y", "z")])
        pair = lax.axis_index("c").reshape(1)
    small = local_small(attn_bias, norm_gain, norm_bias, ffn_in_bias, ffn_out_bias)
    weights = gather(attn_proj, attn_out, small, ffn_in, ffn_out)
    full, rows_in = weights.begin(query)
    bias, gain, shift = full["bias"], full["gain"], full["shift"]
    qmark = query_marks(query_seg)
    smark, cmark = key_marks(query_seg), key_marks(memory_seg)
    sq, sk, sv, sot, slse = self_forward(rows_in, full["qk"], full["v"], bias, smark, qmark)
    rest, sot = weights.finish(sot)
    out, cross_proj = rest["out"], rest["cross_proj"]
    first_sum, low, cq, ck, cv, cot_, clse, second_sum = cross_forward(
        query, memory, sot, out, cross_proj, bias, gain, shift, cmark, qmark
    )
    mixed, ssg, fdw, dbin, small3 = feed(
        second_sum, cotangent, rest["win"], full["bin"], rest["wout"], full["bout"], gain, shift
    )
    dwin, dwout = scatter.feed(fdw, own)
    grads, small2 = [], 0
    for block in blocks:
        *grads, part = cross_back(
            block, grads, ssg, first_sum, cq, ck, cv, cot_, clse, out, cross_proj, gain, cmark, qmark
        )
        small2 = small2 + part
    fsg, dq, dk, dv = grads
    keep, send, memory_grad = cross_weight(
        staged, pair, devices, dq, dk, dv, low, memory, cot_, ssg, sot, fsg, cross_proj
    )
    cross_sum = scatter(me, keep, send)
    upstream = after(fsg, cross_sum)
    grads, small1 = [], 0
    for block in blocks:
        *grads, part = self_back(block, grads, upstream, sq, sk, sv, sot, slse, out, smark, qmark)
        small1 = small1 + part
        if block == 0:
            cross_sum.core()
            upstream = after(upstream, cross_sum)
    dq, dk, dv = grads
    cross_sum.first()
    dq = after(dq, cross_sum)
    sums = jnp.concatenate([small1, small2, small3])
    keep, send = self_weight(staged, pair, devices, sums, dbin, dq, dk, dv, query)
    self_sum = scatter(me, keep, send)
    cross_sum.second()
    self_sum.core()
    upstream = after(fsg, self_sum, cross_sum)
    query_grad = self_input(upstream, dq, dk, dv, full["qk"], full["v"])
    self_sum.first()
    cross = cross_sum.last()
    self_sum.second()
    rows = self_sum.last()
    cross = cross.reshape(5, own, d)
    proj_grad = jnp.concatenate([rows[: 3 * own].reshape(3, own, d), cross[2:]])
    if staged:
        sums = rows[3 * own : 3 * own + 24, :own]
        dbin = rows[3 * own + 24, : dbin.shape[1] // devices]
    else:
        sum_up = functools.partial(lax.psum_scatter, axis_name=("dp", "fsdp"), scatter_dimension=1, tiled=True)
        sums, dbin = sum_up(sums), sum_up(dbin)[0]
    bias_g = jnp.concatenate([sums[0:3], sums[8:11]])
    gain_g = jnp.stack([sums[11], sums[19], sums[16]])
    shift_g = jnp.stack([sums[12], sums[20], sums[17]])
    return (
        mixed, query_grad, memory_grad, proj_grad, cross[1::-1], bias_g, gain_g, shift_g, dwin, dbin, dwout, sums[18],
    )


def solution(mesh):
    devices = mesh.size
    if dict(mesh.shape) == {"dp": 4, "fsdp": 8}:
        axes = ("x", "c", "z", "y")
        mesh = Mesh(mesh.devices.reshape(2, 2, 4, 2), axes)
        gather, scatter = Stages, Halving
    else:
        axes = ("dp", "fsdp")
        gather, scatter = Plain, Whole
    rows, mid, flat, row1 = P(axes, None), P(None, axes, None), P(None, axes), P(axes)
    return jax.shard_map(
        functools.partial(body, gather, scatter, devices),
        mesh=mesh,
        in_specs=(rows, rows, row1, row1, mid, mid, flat, flat, flat, rows, row1, rows, row1, rows),
        out_specs=(rows, rows, rows, mid, mid, flat, flat, flat, rows, row1, rows, row1),
        check_vma=False,
    )
```

```python
import functools

import jax
import jax.numpy as jnp
from jax import lax
from jax.experimental import pallas as pl
from jax.experimental.pallas import tpu as pltpu
from jax.sharding import Mesh
from jax.sharding import PartitionSpec as P

HEADS = 12
HEAD_DIM = 64
SEQ_MAX = 512
PAIRS = HEADS // 2
EPSILON = 1e-05
MASKED = 1e30
SCALE = HEAD_DIM ** (-0.5)
BF = jnp.bfloat16
F32 = jnp.float32
VMEM_LIMIT = 60 * 1024 * 1024


def dot(left, right):
    return jnp.dot(left, right, preferred_element_type=F32)


def dot_nt(left, right):
    return lax.dot_general(left, right, (((1,), (1,)), ((), ())), preferred_element_type=F32)


def norm_parts(resid):
    center = resid - jnp.mean(resid, axis=-1, keepdims=True)
    rstd = lax.rsqrt(jnp.mean(center * center, axis=-1, keepdims=True) + EPSILON)
    return center * rstd, rstd


def norm_back(unit, rstd, gain, upstream):
    scaled = upstream * gain
    mean_s = jnp.mean(scaled, axis=-1, keepdims=True)
    mean_su = jnp.mean(scaled * unit, axis=-1, keepdims=True)
    grad = rstd * (scaled - mean_s - unit * mean_su)
    return grad, col_sum(upstream * unit), col_sum(upstream)


def col_sum(rows):
    return jnp.sum(rows, axis=0, keepdims=True)


def place_rows(rows, count):
    parts = list(rows)
    parts.append(jnp.zeros((count - len(parts), parts[0].shape[1]), F32))
    return jnp.concatenate(parts, axis=0)


def gelu_parts(value):
    size = jnp.abs(value) * (0.5**0.5)
    bell = jnp.exp(-0.5 * value * value)
    t = 1.0 / (1.0 + 0.3275911 * size)
    poly = t * (0.254829592 + t * (-0.284496736 + t * (1.421413741 + t * (-1.453152027 + t * 1.061405429))))
    tail = 0.5 * poly * bell
    phi = jnp.where(value >= 0, 1.0 - tail, tail)
    return value * phi, phi + value * (bell * (1.0 / (2.0 * 3.141592653589793) ** 0.5))


def left_half(shape):
    return lax.broadcasted_iota(jnp.int32, shape, 1) < HEAD_DIM


def head_pair(side, pair):
    return pl.ds(pl.multiple_of(pair * 128 + side * HEAD_DIM, HEAD_DIM), HEAD_DIM)


def key_tile(tile, marks, side):
    left = left_half(tile.shape)
    return jnp.where(left, tile, marks) if side == 0 else jnp.where(left, marks, tile)


def query_tile(rows, marks, side):
    return jnp.concatenate([rows, marks] if side == 0 else [marks, rows], axis=0)


def attend_block(k_ref, qt_ref, vt_ref, kmark_ref, qmark_ref, ot_ref, lse_ref):
    kmark = kmark_ref[...]
    qmark = qmark_ref[0]
    ones = jnp.ones((16, SEQ_MAX), BF)

    def score(head):
        pair, side = head // 2, head % 2
        rows = slice(head * HEAD_DIM, (head + 1) * HEAD_DIM)
        tile = k_ref[:, pair * 128 : (pair + 1) * 128]
        return dot(key_tile(tile, kmark, side), query_tile(qt_ref[rows, :], qmark, side))

    def finish(head, peak, weights):
        rows = slice(head * HEAD_DIM, (head + 1) * HEAD_DIM)
        result = dot(jnp.concatenate([vt_ref[rows, :], ones], axis=0), weights)
        total = result[HEAD_DIM : HEAD_DIM + 1]
        ot_ref[rows, :] = (result[:HEAD_DIM] * (1.0 / total)).astype(BF)
        lse_ref[0, head : head + 1, :] = peak + jnp.log(total)

    for start in range(0, HEADS, 6):
        heads = range(start, start + 6)
        scores = [score(head) for head in heads]
        peaks = [jnp.max(s, axis=0, keepdims=True) for s in scores]
        weights = [jnp.exp(s - peak).astype(BF) for s, peak in zip(scores, peaks)]
        for head, peak, weight in zip(heads, peaks, weights):
            finish(head, peak, weight)


def attend_back_block(
    q_ref, k_ref, v_ref, qt_ref, kt_ref, ot_ref, do_ref, dot_ref, kmark_ref, qmark_ref, lse_ref, dqt_ref, dk_ref, dv_ref
):
    kmark = kmark_ref[...]
    qmark = qmark_ref[0]
    left = left_half((SEQ_MAX, 128))
    blank = jnp.zeros((HEAD_DIM, SEQ_MAX), BF)

    def begin(head):
        pair, side = head // 2, head % 2
        rows = slice(head * HEAD_DIM, (head + 1) * HEAD_DIM)
        cols = slice(pair * 128, (pair + 1) * 128)
        scores = dot(key_tile(k_ref[:, cols], kmark, side), query_tile(qt_ref[rows, :], qmark, side))
        up = dot_ref[rows, :]
        probs_grad = dot(v_ref[:, cols], query_tile(up, blank, side))
        return scores, probs_grad, col_sum(up.astype(F32) * ot_ref[rows, :].astype(F32))

    def middle(head, scores, probs_grad, center):
        probs = jnp.exp(scores - lse_ref[0, head : head + 1, :])
        return probs.astype(BF), (probs * (probs_grad - center)).astype(BF)

    def finish(head, probs, score_grad):
        rows = slice(head * HEAD_DIM, (head + 1) * HEAD_DIM)
        cols = slice(head // 2 * 128, (head // 2 + 1) * 128)
        dqt_ref[rows, :] = (dot(kt_ref[rows, :], score_grad) * SCALE).astype(BF)
        return dot(probs, do_ref[:, cols]), dot(score_grad, q_ref[:, cols])

    for start in range(0, HEADS, 4):
        heads = range(start, start + 4)
        begun = [begin(head) for head in heads]
        mid = [middle(head, *b) for head, b in zip(heads, begun)]
        done = [finish(head, *m) for head, m in zip(heads, mid)]
        for i in range(0, 4, 2):
            cols = slice((start + i) // 2 * 128, ((start + i) // 2 + 1) * 128)
            dv_ref[:, cols] = jnp.where(left, done[i][0], done[i + 1][0]).astype(BF)
            dk_ref[:, cols] = jnp.where(left, done[i][1], done[i + 1][1]).astype(BF)


def self_forward_kernel(
    x_ref, wqk_ref, wv_ref, bias_ref, kmark_ref, qmark_ref, q_ref, k_ref, v_ref, ot_ref, lse_ref, qt_s, vt_s
):
    x = x_ref[...]
    queries = ((dot(x, wqk_ref[0]) + bias_ref[0:1]).astype(BF)) * SCALE
    q_ref[...] = queries
    qt_s[...] = queries.T
    k_ref[...] = dot(x, wqk_ref[1]).astype(BF)
    values = (dot(x, wv_ref[0]) + bias_ref[1:2]).astype(BF)
    v_ref[...] = values
    vt_s[...] = values.T
    attend_block(k_ref, qt_s, vt_s, kmark_ref, qmark_ref, ot_ref, lse_ref)


def cross_forward_kernel(
    x_ref, mem_ref, sot_ref, wo_ref, w_ref, bias_ref, gain_ref, shift_ref, kmark_ref, qmark_ref,
    first_sum_ref, low_ref, q_ref, k_ref, v_ref, ot_ref, lse_ref, second_sum_ref, qt_s, vt_s,
):
    mem = mem_ref[...]
    k_ref[...] = dot(mem, w_ref[1]).astype(BF)
    values = (dot(mem, w_ref[2]) + bias_ref[4:5]).astype(BF)
    v_ref[...] = values
    vt_s[...] = values.T
    first_sum = x_ref[...].astype(F32) + (dot(sot_ref[...].T, wo_ref[0]) + bias_ref[2:3])
    first_sum_ref[...] = first_sum
    unit, _ = norm_parts(first_sum)
    first = unit * gain_ref[0:1] + shift_ref[0:1]
    low = first.astype(BF)
    low_ref[...] = low
    queries = ((dot(low, w_ref[0]) + bias_ref[3:4]).astype(BF)) * SCALE
    q_ref[...] = queries
    qt_s[...] = queries.T
    attend_block(k_ref, qt_s, vt_s, kmark_ref, qmark_ref, ot_ref, lse_ref)
    second_sum_ref[...] = first + (dot(ot_ref[...].T, wo_ref[1]) + bias_ref[5:6])


def feed_kernel(
    own, ss_ref, cot_ref, win_ref, bin_ref, wout_ref, bout_ref, gain_ref, shift_ref,
    mixed_ref, ssg_ref, dw_ref, dbin_ref, small_ref,
    low_s, lowt_s, hid_s, slope_s, acc_s, z_s, din_s, dout_s, sems,
):
    phase, chunk = pl.program_id(0), pl.program_id(1)
    chunks = pl.num_programs(1)
    last = chunks - 1
    slot = chunk % 2
    width, d = dout_s.shape[1] * dout_s.shape[2], dout_s.shape[3]
    parts = dout_s.shape[1]

    def wout():
        if not own:
            return wout_ref[...]
        groups = wout_ref[...].astype(F32)
        return jnp.concatenate([groups[:, i] for i in range(groups.shape[1])], axis=0).reshape(width, d).astype(BF)

    def sends(slot, chunk):
        if own:
            group = width // parts
            rows = pl.ds(pl.multiple_of(chunk * group, group), group)
            outs = [
                pltpu.make_async_copy(
                    dout_s.at[slot, part], dw_ref.at[rows, pl.ds((chunks + part) * width, width)], sems.at[1 + part, slot]
                )
                for part in range(parts)
            ]
        else:
            cols = pl.ds(pl.multiple_of((chunks + chunk) * width, width), width)
            outs = [pltpu.make_async_copy(dout_s.at[slot, 0], dw_ref.at[:, cols], sems.at[1, slot])]
        cols = pl.ds(pl.multiple_of(chunk * width, width), width)
        return [pltpu.make_async_copy(din_s.at[slot], dw_ref.at[:, cols], sems.at[0, slot])] + outs

    @pl.when((phase == 0) & (chunk == 0))
    def _():
        unit, _ = norm_parts(ss_ref[...])
        second = unit * gain_ref[1:2] + shift_ref[1:2]
        low = second.astype(BF)
        low_s[...] = low
        lowt_s[...] = low.T
        acc_s[...] = second + bout_ref[...]

    @pl.when(phase == 0)
    def _():
        weights_in, weights_out, count = win_ref[0], wout(), low_s.shape[0] // 4
        blocks = [slice(i * count, (i + 1) * count) for i in range(4)]
        pres = [dot(low_s[block, :], weights_in) + bin_ref[...] for block in blocks]
        both = [gelu_parts(pre) for pre in pres]
        for block, (hidden, slope) in zip(blocks, both):
            hidden = hidden.astype(BF)
            hid_s[chunk, block] = hidden
            slope_s[chunk, block] = slope
            acc_s[block, :] += dot(hidden, weights_out)

    @pl.when((phase == 1) & (chunk == 0))
    def _():
        unit, rstd = norm_parts(acc_s[...])
        mixed_ref[...] = (unit * gain_ref[2:3] + shift_ref[2:3]).astype(BF)
        third, dgain, dshift = norm_back(unit, rstd, gain_ref[2:3], cot_ref[...].astype(F32))
        z = third.astype(BF)
        z_s[...] = z
        acc_s[...] = third
        small_ref[...] = place_rows([dgain, dshift, col_sum(z.astype(F32))], 8)

    @pl.when((phase == 1) & (chunk >= 2))
    def _():
        for copy in sends(slot, chunk - 2):
            copy.wait()

    @pl.when(phase == 1)
    def _():
        z = z_s[...]
        pre_grad = (dot_nt(z, wout()) * slope_s[chunk]).astype(BF)
        dbin_ref[...] = col_sum(pre_grad.astype(F32))
        dout = dot(hid_s[chunk].T, z)
        if own:
            groups = dout.reshape(width // (parts * own), parts, own, d)
            for part in range(parts):
                dout_s[slot, part] = groups[:, part].reshape(width // parts, d).astype(BF)
        else:
            dout_s[slot] = dout.reshape(dout_s.shape[1:]).astype(BF)
        din_s[slot] = dot(lowt_s[...], pre_grad).astype(BF)
        for copy in sends(slot, chunk):
            copy.start()
        acc_s[...] += dot_nt(pre_grad, win_ref[0])

    @pl.when((phase == 1) & (chunk == last))
    def _():
        unit, rstd = norm_parts(ss_ref[...])
        grad, dgain, dshift = norm_back(unit, rstd, gain_ref[1:2], acc_s[...])
        ssg_ref[...] = grad
        small_ref[3:5] = jnp.concatenate([dgain, dshift], axis=0)
        for copy in sends(1 - slot, chunk - 1) + sends(slot, chunk):
            copy.wait()


def cross_back_kernel(
    ssg_ref, fs_ref, q_ref, k_ref, v_ref, ot_ref, lse_ref, wo_ref, w_ref, gain_ref, kmark_ref, qmark_ref, *refs
):
    fsg_ref, dq_ref, dk_ref, dv_ref, small_ref, qt_s, kt_s, do_s, dot_s, dqt_s = refs[-10:]
    upstream = ssg_ref[...]
    branch = upstream.astype(BF)
    mixed_grad = dot_nt(branch, wo_ref[0]).astype(BF)
    do_s[...] = mixed_grad
    dot_s[...] = mixed_grad.T
    qt_s[...] = q_ref[...].T
    kt_s[...] = k_ref[...].T
    attend_back_block(
        q_ref, k_ref, v_ref, qt_s, kt_s, ot_ref, do_s, dot_s, kmark_ref, qmark_ref, lse_ref, dqt_s, dk_ref, dv_ref
    )
    dq = dqt_s[...].T
    dq_ref[...] = dq
    first_grad = upstream + dot_nt(dq, w_ref[0])
    unit, rstd = norm_parts(fs_ref[...])
    grad, dgain, dshift = norm_back(unit, rstd, gain_ref[0:1], first_grad)
    fsg_ref[...] = grad
    sums = [col_sum(dq.astype(F32)), col_sum(dv_ref[...].astype(F32)), col_sum(branch.astype(F32)), dgain, dshift]
    small_ref[...] = place_rows(sums, 8)


def self_back_kernel(fsg_ref, q_ref, k_ref, v_ref, ot_ref, lse_ref, wo_ref, kmark_ref, qmark_ref, *refs):
    dq_ref, dk_ref, dv_ref, small_ref, qt_s, kt_s, do_s, dot_s, dqt_s = refs[-9:]
    branch = fsg_ref[...].astype(BF)
    mixed_grad = dot_nt(branch, wo_ref[0]).astype(BF)
    do_s[...] = mixed_grad
    dot_s[...] = mixed_grad.T
    qt_s[...] = q_ref[...].T
    kt_s[...] = k_ref[...].T
    attend_back_block(
        q_ref, k_ref, v_ref, qt_s, kt_s, ot_ref, do_s, dot_s, kmark_ref, qmark_ref, lse_ref, dqt_s, dk_ref, dv_ref
    )
    dq = dqt_s[...].T
    dq_ref[...] = dq
    sums = [col_sum(dq.astype(F32)), col_sum(dv_ref[...].astype(F32)), col_sum(branch.astype(F32))]
    small_ref[...] = place_rows(sums, 8)


def bring(sources, slots, sems):
    copies = [pltpu.make_async_copy(s, v, sems.at[i]) for i, (s, v) in enumerate(zip(sources, slots))]
    for copy in copies:
        copy.start()

    def get(i):
        copies[i].wait()
        return slots[i][...]

    return get


def split_out(grads, me, keep_ref, send_ref, small=None):
    places = keep_ref.shape[1] * keep_ref.shape[2]
    own = grads[0].shape[0] // (4 * places)
    for x in range(2):
        cores = []
        for core in range(2):
            rows = pl.ds((2 * x + core) * places * own, places * own)
            parts = [g[rows, :].reshape(places, own, g.shape[1]) for g in grads]
            if small is not None:
                parts.append(small(x, core))
            cores.append(jnp.concatenate(parts, axis=1))
        mine = me == 0
        block = keep_ref.shape[1:]
        keep_ref[x] = jnp.where(mine, cores[0], cores[1]).astype(BF).reshape(block)
        send_ref[x] = jnp.where(mine, cores[1], cores[0]).astype(BF).reshape(block)


def cross_weight_kernel(staged, me_ref, *refs):
    sources, (keep_ref, send_ref, mg_ref), slots = list(refs[:10]), refs[10:13], refs[13:23]
    sources[3] = sources[3].at[pl.ds(0, 3)]
    dw_s, mg_s, sems, out_sem = refs[23:]
    get = bring(sources, slots, sems)
    memt = get(0).T
    dk = get(1)
    dw_s[3] = dot(memt, dk)
    dv = get(2)
    dw_s[4] = dot(memt, dv)
    get(3)
    w_s = slots[3]
    mg_s[...] = dot_nt(dk, w_s[1]) + dot_nt(dv, w_s[2])
    move = pltpu.make_async_copy(mg_s, mg_ref, out_sem)
    move.start()
    dw_s[0] = dot(get(4), get(5).astype(BF))
    dw_s[1] = dot(get(6), get(7).astype(BF))
    dw_s[2] = dot(get(8).T, get(9))
    if staged:
        split_out([dw_s.at[i] for i in range(5)], me_ref[0], keep_ref, send_ref)
    else:
        keep_ref[...] = dw_s[...].astype(BF)
        send_ref[...] = jnp.zeros(send_ref.shape, BF)
    move.wait()


def self_weight_kernel(staged, me_ref, small_ref, dbin_ref, x_ref, dq_ref, dk_ref, dv_ref, keep_ref, send_ref, *scratch):
    dw_s, sems = scratch[4:]
    get = bring((x_ref, dq_ref, dk_ref, dv_ref), scratch[:4], sems)
    xt = get(0).T
    for i in range(3):
        dw_s[i] = dot(xt, get(i + 1))
    if not staged:
        keep_ref[...] = dw_s[...].astype(BF)
        send_ref[...] = jnp.zeros(send_ref.shape, BF)
        return
    d = small_ref.shape[1]
    places = keep_ref.shape[1] * keep_ref.shape[2]
    own = d // (4 * places)
    wide = dbin_ref.shape[1]

    lines = jnp.broadcast_to(dbin_ref[...], (8, wide))

    def small(x, core):
        out = []
        for place in range(places):
            device = (2 * x + core) * places + place
            rows, line = small_ref[...], lines
            if device:
                rows = pltpu.roll(rows, d - own * device, 1)
                line = pltpu.roll(lines, wide - wide // (4 * places) * device, 1)
            out.append(jnp.concatenate([rows, line[:, :d]], axis=0))
        return jnp.stack(out)

    split_out([dw_s.at[i] for i in range(3)], me_ref[0], keep_ref, send_ref, small)


def self_input_kernel(fsg_ref, dq_ref, dk_ref, dv_ref, wqk_ref, wv_ref, qg_ref):
    qg_ref[...] = (
        fsg_ref[...]
        + dot_nt(dq_ref[...], wqk_ref[0]) + dot_nt(dk_ref[...], wqk_ref[1]) + dot_nt(dv_ref[...], wv_ref[0])
    )


def pick(first, second, other):
    return jnp.where(other == 0, first, second)


def first_stage_kernel(me_ref, keep_ref, got_ref, sl_ref, kl_ref, sr_ref, kr_ref):
    total = keep_ref[...].astype(F32) + got_ref[...].astype(F32)
    half = total.shape[4] // 2
    left, right = total[..., :half], total[..., half:]
    sl_ref[...] = pick(left[1], left[0], me_ref[0]).astype(BF)
    kl_ref[...] = pick(left[0], left[1], me_ref[0]).astype(BF)
    sr_ref[...] = pick(right[:, :, 1], right[:, :, 0], me_ref[1]).astype(BF)
    kr_ref[...] = pick(right[:, :, 0], right[:, :, 1], me_ref[1]).astype(BF)


def second_stage_kernel(me_ref, kl_ref, gl_ref, kr_ref, gr_ref, sl_ref, ml_ref, sr_ref, mr_ref):
    left = kl_ref[...].astype(F32) + gl_ref[...].astype(F32)
    right = kr_ref[...].astype(F32) + gr_ref[...].astype(F32)
    sl_ref[...] = pick(left[:, 1], left[:, 0], me_ref[1]).astype(BF)
    ml_ref[...] = pick(left[:, 0], left[:, 1], me_ref[1]).astype(BF)
    sr_ref[...] = pick(right[1], right[0], me_ref[0]).astype(BF)
    mr_ref[...] = pick(right[0], right[1], me_ref[0]).astype(BF)


def third_stage_kernel(me_ref, kl_ref, gl_ref, kr_ref, gr_ref, own_ref, *outs):
    total = jnp.concatenate(
        [kl_ref[...].astype(F32) + gl_ref[...].astype(F32), kr_ref[...].astype(F32) + gr_ref[...].astype(F32)], axis=2
    )
    me = me_ref[2]
    for step, ref in enumerate((own_ref, *outs)):
        index = (me + step) % 4
        value = jnp.where(
            index < 2, jnp.where(index == 0, total[0], total[1]), jnp.where(index == 2, total[2], total[3])
        )
        ref[...] = value.astype(ref.dtype)


def stage_call(kernel, me, args, outs, name):
    data = sum(a.size * a.dtype.itemsize for a in args)
    return pl.pallas_call(
        kernel,
        in_specs=[pl.BlockSpec(memory_space=pltpu.SMEM)] + [pl.BlockSpec(memory_space=pltpu.VMEM)] * len(args),
        out_specs=[pl.BlockSpec(memory_space=pltpu.VMEM)] * len(outs),
        out_shape=outs,
        compiler_params=pltpu.CompilerParams(vmem_limit_bytes=VMEM_LIMIT),
        cost_estimate=cost(data, 2 * data),
        name=name,
    )(me, *args)


def first_stage(me, keep, got):
    x, z, y, rows, d = keep.shape
    line = lambda *lead: pl.BlockSpec((*lead, rows, d // 2), lambda i: (i, 0, 0, 0))
    both = pl.BlockSpec((x, 1, y, rows, d), lambda i: (0, i, 0, 0, 0))
    side = pl.BlockSpec((x, 1, rows, d // 2), lambda i: (0, i, 0, 0))
    left, right = shape((z, y, rows, d // 2), BF), shape((x, z, rows, d // 2), BF)
    return pl.pallas_call(
        first_stage_kernel,
        grid=(z,),
        in_specs=[pl.BlockSpec(memory_space=pltpu.SMEM), both, both],
        out_specs=[line(1, y), line(1, y), side, side],
        out_shape=[left, left, right, right],
        compiler_params=params(("arbitrary",)),
        cost_estimate=cost(keep.size, 6 * keep.size),
        name="first_stage",
    )(me, keep, got)


def row_block(width):
    return pl.BlockSpec((SEQ_MAX, width), lambda b: (b, 0))


def col_block(height):
    return pl.BlockSpec((height, SEQ_MAX), lambda b: (0, b))


def lead_block(rows):
    return pl.BlockSpec((1, rows, SEQ_MAX), lambda b: (b, 0, 0))


def whole(array, **kw):
    zeros = (0,) * array.ndim
    return pl.BlockSpec(array.shape, lambda *_: zeros, pipeline_mode=pl.Buffered(1))


def planes(array, start, count):
    return pl.BlockSpec(
        (count, *array.shape[1:]), lambda *_: (start // count, 0, 0), pipeline_mode=pl.Buffered(1)
    )


def params(semantics):
    return pltpu.CompilerParams(vmem_limit_bytes=VMEM_LIMIT, dimension_semantics=semantics)


def cost(flops, data, exps=0):
    return pl.CostEstimate(flops=int(flops), bytes_accessed=int(data), transcendentals=int(exps))


def shape(dims, kind):
    return jax.ShapeDtypeStruct(dims, kind)


def self_forward(x, wqk, wv, bias, kmark, qmark):
    rows, d = x.shape
    blocks = rows // SEQ_MAX
    act = shape((rows, d), BF)
    return pl.pallas_call(
        self_forward_kernel,
        grid=(blocks,),
        in_specs=[row_block(d), whole(wqk), whole(wv), whole(bias), row_block(128), lead_block(HEAD_DIM)],
        out_specs=[row_block(d), row_block(d), row_block(d), col_block(d), lead_block(16)],
        out_shape=[act, act, act, shape((d, rows), BF), shape((blocks, 16, SEQ_MAX), F32)],
        scratch_shapes=[pltpu.VMEM((d, SEQ_MAX), BF)] * 2,
        compiler_params=params(("arbitrary",)),
        cost_estimate=cost(20e9, 12e6),
        name="self_forward",
    )(x, wqk, wv, bias, kmark, qmark)


def cross_forward(x, mem, sot, wo, wo_at, w, bias, gain, shift, kmark, qmark):
    rows, d = x.shape
    blocks = rows // SEQ_MAX
    act, wide = shape((rows, d), BF), shape((rows, d), F32)
    return pl.pallas_call(
        cross_forward_kernel,
        grid=(blocks,),
        in_specs=[
            row_block(d), row_block(d), col_block(d), planes(wo, wo_at, 2), planes(w, 0, 3), whole(bias), whole(gain),
            whole(shift),
            row_block(128), lead_block(HEAD_DIM),
        ],
        out_specs=[row_block(d)] * 5 + [col_block(d), lead_block(16), row_block(d)],
        out_shape=[wide, act, act, act, act, shape((d, rows), BF), shape((blocks, 16, SEQ_MAX), F32), wide],
        scratch_shapes=[pltpu.VMEM((d, SEQ_MAX), BF)] * 2,
        compiler_params=params(("arbitrary",)),
        cost_estimate=cost(24e9, 20e6),
        name="cross_forward",
    )(x, mem, sot, wo, w, bias, gain, shift, kmark, qmark)


def feed(second_sum, cot, win, bin_, wout, bout, gain, shift):
    rows, d = second_sum.shape
    width = win.shape[2]
    ff = bin_.shape[1]
    chunks = ff // width
    own = wout.shape[2] if wout.ndim == 4 else 0
    fixed = lambda p, j: (0, 0)
    parts = chunks if own else 1
    if own:
        wout_spec = pl.BlockSpec((parts, width // (parts * own), own, d), lambda p, j: (1, j, 0, 0))
    else:
        wout_spec = pl.BlockSpec((width, d), lambda p, j: (j, 0))
    return pl.pallas_call(
        functools.partial(feed_kernel, own),
        grid=(2, chunks),
        in_specs=[
            whole(second_sum), whole(cot),
            pl.BlockSpec((1, d, width), lambda p, j: (jnp.where(j == 0, 3, 9 + j) if own else j, 0, 0)),
            pl.BlockSpec((1, width), lambda p, j: (0, j)),
            wout_spec, whole(bout), whole(gain), whole(shift),
        ],
        out_specs=[
            pl.BlockSpec((rows, d), fixed),
            pl.BlockSpec((rows, d), fixed),
            pl.BlockSpec(memory_space=pl.ANY),
            pl.BlockSpec((1, width), lambda p, j: (0, j * p)),
            pl.BlockSpec((8, d), fixed),
        ],
        out_shape=[
            shape((rows, d), BF), shape((rows, d), F32), shape((d, 2 * ff), BF),
            shape((1, ff), F32), shape((8, d), F32),
        ],
        scratch_shapes=[
            pltpu.VMEM((rows, d), BF), pltpu.VMEM((d, rows), BF),
            pltpu.VMEM((chunks, rows, width), BF), pltpu.VMEM((chunks, rows, width), F32),
            pltpu.VMEM((rows, d), F32), pltpu.VMEM((rows, d), BF),
            pltpu.VMEM((2, d, width), BF), pltpu.VMEM((2, parts, width // parts, d), BF),
            pltpu.SemaphoreType.DMA((1 + parts, 2)),
        ],
        compiler_params=params(("arbitrary", "arbitrary")),
        cost_estimate=cost(40e9, 40e6),
        name="feed",
    )(second_sum, cot, win, bin_, wout, bout, gain, shift)


def back_scratch(d):
    return (
        [pltpu.VMEM((d, SEQ_MAX), BF)] * 2 + [pltpu.VMEM((SEQ_MAX, d), BF)] + [pltpu.VMEM((d, SEQ_MAX), BF)] * 2
    )


def at_row(block, width):
    return pl.BlockSpec((SEQ_MAX, width), lambda b: (block, 0))


def at_col(block, height):
    return pl.BlockSpec((height, SEQ_MAX), lambda b: (0, block))


def at_lead(block, rows):
    return pl.BlockSpec((1, rows, SEQ_MAX), lambda b: (block, 0, 0))


def one_back(kernel, block, before, args, specs, outs, name):
    d = outs[0].shape[1]
    kept = [pl.BlockSpec(memory_space=pl.ANY)] * len(before)
    return pl.pallas_call(
        kernel,
        grid=(1,),
        in_specs=specs + kept,
        out_specs=[at_row(block, d)] * len(outs) + [pl.BlockSpec((8, d), lambda b: (0, 0))],
        out_shape=outs + [shape((8, d), F32)],
        scratch_shapes=back_scratch(d),
        input_output_aliases={len(args) + i: i for i in range(len(before))},
        compiler_params=params(("arbitrary",)),
        cost_estimate=cost(25e9, 15e6),
        name=name,
    )(*args, *before)


def cross_back(block, before, wo_at, ssg, first_sum, q, k, v, ot, lse, wo, w, gain, kmark, qmark):
    rows, d = first_sum.shape
    act = shape((rows, d), BF)
    specs = [at_row(block, d)] * 5 + [
        at_col(block, d), at_lead(block, 16), planes(wo, wo_at + 1, 1), planes(w, 0, 1), whole(gain), at_row(block, 128), at_lead(block, HEAD_DIM),
    ]
    args = (ssg, first_sum, q, k, v, ot, lse, wo, w, gain, kmark, qmark)
    return one_back(
        cross_back_kernel, block, before, args, specs, [shape((rows, d), F32), act, act, act], f"cross_back_{block}"
    )


def self_back(block, before, wo_at, fsg, q, k, v, ot, lse, wo, kmark, qmark):
    rows, d = fsg.shape
    act = shape((rows, d), BF)
    specs = [at_row(block, d)] * 4 + [
        at_col(block, d), at_lead(block, 16), planes(wo, wo_at, 1), at_row(block, 128), at_lead(block, HEAD_DIM),
    ]
    args = (fsg, q, k, v, ot, lse, wo, kmark, qmark)
    return one_back(self_back_kernel, block, before, args, specs, [act, act, act], f"self_back_{block}")


def weight_outs(staged, count, extra, devices, d):
    if not staged:
        return [shape((count, d, d), BF), shape((8, 128), BF)]
    half = shape((2, 4, 2, count * d // devices + extra, d), BF)
    return [half, half]


def cross_weight(staged, me, devices, dq, dk, dv, low, mem, ot, ssg, sot, fsg, w):
    rows, d = dq.shape
    args = (mem, dk, dv, w, ot, ssg, sot, fsg, low, dq)
    anywhere, here = pl.BlockSpec(memory_space=pl.ANY), pl.BlockSpec(memory_space=pltpu.VMEM)
    return pl.pallas_call(
        functools.partial(cross_weight_kernel, staged),
        in_specs=[pl.BlockSpec(memory_space=pltpu.SMEM)] + [anywhere] * 10,
        out_specs=[here, here, anywhere],
        out_shape=weight_outs(staged, 5, 0, devices, d) + [shape((rows, d), F32)],
        scratch_shapes=[pltpu.VMEM((min(a.shape[0], 3), *a.shape[1:]) if a is w else a.shape, a.dtype) for a in args] + [
            pltpu.VMEM((5, d, d), F32), pltpu.VMEM((rows, d), F32), pltpu.SemaphoreType.DMA((10,)),
            pltpu.SemaphoreType.DMA,
        ],
        compiler_params=pltpu.CompilerParams(vmem_limit_bytes=VMEM_LIMIT),
        cost_estimate=cost(9e9, 20e6),
        name="cross_weight",
    )(me, *args)


def self_weight(staged, me, devices, small, dbin, dq, dk, dv, x):
    rows, d = dq.shape
    args = (x, dq, dk, dv)
    anywhere, here = pl.BlockSpec(memory_space=pl.ANY), pl.BlockSpec(memory_space=pltpu.VMEM)
    return pl.pallas_call(
        functools.partial(self_weight_kernel, staged),
        in_specs=[pl.BlockSpec(memory_space=pltpu.SMEM), here, here] + [anywhere] * 4,
        out_specs=[here, here],
        out_shape=weight_outs(staged, 3, 32, devices, d),
        scratch_shapes=[pltpu.VMEM(a.shape, a.dtype) for a in args] + [
            pltpu.VMEM((3, d, d), F32), pltpu.SemaphoreType.DMA((4,)),
        ],
        compiler_params=pltpu.CompilerParams(vmem_limit_bytes=VMEM_LIMIT),
        cost_estimate=cost(4e9, 10e6),
        name="self_weight",
    )(me, small, dbin, *args)


def self_input(fsg, dq, dk, dv, wqk, wv):
    rows, d = fsg.shape
    return pl.pallas_call(
        self_input_kernel,
        grid=(rows // SEQ_MAX,),
        in_specs=[row_block(d)] * 4 + [whole(wqk), whole(wv)],
        out_specs=row_block(d),
        out_shape=shape((rows, d), F32),
        compiler_params=params(("arbitrary",)),
        cost_estimate=cost(4e9, 14e6),
        name="self_input",
    )(fsg, dq, dk, dv, wqk, wv)


def key_marks(seg):
    odd = (seg & 1)[:, None]
    lane = lax.broadcasted_iota(jnp.int32, (seg.shape[0], 128), 1) % HEAD_DIM
    return jnp.where(lane == 0, 1 - odd, jnp.where(lane == 1, odd, 0)).astype(BF)


def query_marks(seg):
    odd = (seg & 1).reshape(-1, 1, SEQ_MAX)
    row = lax.broadcasted_iota(jnp.int32, (odd.shape[0], HEAD_DIM, SEQ_MAX), 1)
    return jnp.where(row == 0, odd, jnp.where(row == 1, 1 - odd, 0)).astype(BF) * (-MASKED)


def swap(value, name):
    return lax.ppermute(value, name, [(0, 1), (1, 0)])


class Halving:
    def __init__(self, me, keep, send):
        self.me, self.keep, self.out = me, [keep], [send]

    def core(self):
        got = swap(self.out[0], "c")
        sl, kl, sr, kr = first_stage(self.me, self.keep[0], got)
        self.keep, self.out = [kl, kr], [sl, sr]

    def first(self):
        (kl, kr), (sl, sr) = self.keep, self.out
        gl, gr = swap(sl, "x"), swap(sr, "y")
        z, _, rows, half = kl.shape
        piece = shape((z, rows, half), BF)
        sl, ml, sr, mr = stage_call(second_stage_kernel, self.me, (kl, gl, kr, gr), [piece] * 4, "second_stage")
        self.keep, self.out = [ml, mr], [sl, sr]

    def second(self):
        (kl, kr), (sl, sr) = self.keep, self.out
        gl, gr = swap(sl, "y"), swap(sr, "x")
        _, rows, half = kl.shape
        piece = (rows, 2 * half)
        outs = [shape(piece, F32)] + [shape(piece, BF)] * 3
        own, *self.out = stage_call(third_stage_kernel, self.me, (kl, gl, kr, gr), outs, "third_stage")
        self.keep = [own]

    def last(self):
        total = self.keep[0]
        for step, out in zip(range(1, 4), self.out):
            total = total + lax.ppermute(out, "z", [(i, (i + step) % 4) for i in range(4)]).astype(F32)
        return total

    @staticmethod
    def feed(grads, own):
        sums = lax.psum_scatter(grads, ("x", "c", "z", "y"), scatter_dimension=0, tiled=True).astype(F32)
        half = sums.shape[1] // 2
        d = grads.shape[0]
        return sums[:, :half], sums[:, half:].reshape(own, -1, d).swapaxes(0, 1).reshape(-1, d)


class Whole:
    def __init__(self, me, grads, _):
        self.grads, self.out = grads, ()

    def core(self):
        pass

    first = second = core

    def last(self):
        sums = lax.psum_scatter(self.grads, ("dp", "fsdp"), scatter_dimension=1, tiled=True).astype(F32)
        return sums.reshape(-1, sums.shape[2])

    @staticmethod
    def feed(grads, own):
        sum_up = functools.partial(lax.psum_scatter, axis_name=("dp", "fsdp"), scatter_dimension=0, tiled=True)
        half, d = grads.shape[1] // 2, grads.shape[0]
        dwin = sum_up(grads[:, :half]).astype(F32)
        return dwin, sum_up(grads[:, half:].reshape(d, -1, d).swapaxes(0, 1).reshape(-1, d)).astype(F32)


def after(value, *sums):
    value, outs = lax.optimization_barrier((value, [s.out for s in sums]))
    for s, s.out in zip(sums, outs):
        pass
    return value


def take_turns(value):
    me = lax.axis_index("z")
    parts = [value]
    for step in range(3, 0, -1):
        parts.append(lax.ppermute(value, "z", [(i, (i + step) % 4) for i in range(4)]))
    return jnp.stack([lax.select_n((j - me) % 4, *parts) for j in range(4)], axis=1)


def take_pair(value, name, axis):
    me = lax.axis_index(name)
    got = lax.ppermute(value, name, [(0, 1), (1, 0)])
    return jnp.stack([jnp.where(me == 0, value, got), jnp.where(me == 0, got, value)], axis=axis)


class Doubling:
    def __init__(self, left, right):
        self.cut, self.rows = left.shape[0], left.shape[1]
        self.flat = left.shape[1:] != right.shape[1:]
        if self.flat:
            left, right = (a.reshape(1, -1, a.shape[2]) for a in (left, right))
            self.out = [jnp.concatenate([left, right], axis=1)]
            self.split = left.shape[1]
        else:
            self.out = [jnp.concatenate([left, right])]

    def line(self):
        both = take_turns(self.out[0])
        if self.flat:
            d = both.shape[3]
            left = both[0, :, : self.split].reshape(4, self.cut, self.rows, d).swapaxes(0, 1)
            self.out = [left, both[:, :, self.split :]]
        else:
            self.out = [both[: self.cut], both[self.cut :]]

    def first(self):
        self.out = [take_pair(self.out[0], "y", 2), take_pair(self.out[1], "x", 1)]

    def second(self):
        self.out = [take_pair(self.out[0], "x", 1), take_pair(self.out[1], "y", 3)]

    def core(self):
        self.out = [take_pair(self.out[0], "c", 2), take_pair(self.out[1], "c", 2)]
        return self.out


def local_small(bias, gain, shift, bin_, bout):
    return jnp.concatenate([a.reshape(-1) for a in (bias, gain, shift, bout, bin_)])


def spread_small(parts, own):
    parts = parts.astype(F32)
    devices = parts.shape[0]
    rows = parts[:, : 13 * own].reshape(devices, 13, own).swapaxes(0, 1).reshape(13, -1)
    bin_ = parts[:, 13 * own :].reshape(1, -1)
    return {"bias": rows[0:6], "gain": rows[6:9], "shift": rows[9:12], "bout": rows[12:13], "bin": bin_}


class Stages:
    out_at = 8

    def __init__(self, proj, out, small, win, wout):
        _, own, d = proj.shape
        panels = win.reshape(own, -1, d).swapaxes(0, 1)
        rest = jnp.concatenate([proj[3:6], panels[:1], wout.reshape(-1, own, d), out, panels[1:]])
        self.rest = lax.all_gather(rest, ("x", "c", "z", "y"), axis=1)
        extra = jnp.pad(small[None, None], ((0, 0), (0, 7), (0, d - small.shape[0])))
        self.one = Doubling(proj[:2], jnp.concatenate([proj[2:3], extra], axis=1))
        self.own, self.cut, self.d = own, small.shape[0], d

    def begin(self):
        one, own, d = self.one, self.own, self.d
        one.line()
        one.first()
        one.second()
        left, right = one.core()
        full = {"qk": left.reshape(2, -1, d), "v": right[..., :own, :].reshape(1, -1, d)}
        full.update(spread_small(right[..., own, : self.cut].reshape(-1, self.cut), own))
        return full

    def finish(self):
        planes = self.rest.reshape(self.rest.shape[0], -1, self.d)
        return {"cross_proj": planes, "out": planes, "win": planes, "wout": self.rest}


class Plain:
    out_at = 0

    def __init__(self, proj, out, small, win, wout):
        take = functools.partial(lax.all_gather, axis_name=("dp", "fsdp"), tiled=True)
        _, own, d = proj.shape
        proj = take(proj, axis=1)
        self.full = {"qk": proj[:2], "v": proj[2:3]}
        self.full.update(spread_small(take(small[None], axis=0), own))
        win = take(win, axis=0).reshape(d, -1, d).swapaxes(0, 1)
        self.rest = {"cross_proj": proj[3:], "out": take(out, axis=1), "win": win, "wout": take(wout, axis=0)}

    def begin(self):
        return self.full

    def finish(self):
        return self.rest


def body(
    gather, scatter, devices, query, memory, query_seg, memory_seg, attn_proj, attn_out, attn_bias, norm_gain, norm_bias,
    ffn_in, ffn_in_bias, ffn_out, ffn_out_bias, cotangent,
):
    blocks = range(query.shape[0] // SEQ_MAX)
    own = attn_proj.shape[1]
    d = query.shape[1]
    staged = scatter is Halving
    me, pair = jnp.zeros((3,), jnp.int32), jnp.zeros((1,), jnp.int32)
    if staged:
        me = jnp.stack([lax.axis_index(name) for name in ("x", "y", "z")])
        pair = lax.axis_index("c").reshape(1)
    small = local_small(attn_bias, norm_gain, norm_bias, ffn_in_bias, ffn_out_bias)
    weights = gather(attn_proj, attn_out, small, ffn_in, ffn_out)
    full = weights.begin()
    bias, gain, shift = full["bias"], full["gain"], full["shift"]
    qmark = query_marks(query_seg)
    smark, cmark = key_marks(query_seg), key_marks(memory_seg)
    sq, sk, sv, sot, slse = self_forward(query, full["qk"], full["v"], bias, smark, qmark)
    rest, out_at = weights.finish(), weights.out_at
    out, cross_proj = rest["out"], rest["cross_proj"]
    first_sum, low, cq, ck, cv, cot_, clse, second_sum = cross_forward(
        query, memory, sot, out, out_at, cross_proj, bias, gain, shift, cmark, qmark
    )
    mixed, ssg, fdw, dbin, small3 = feed(
        second_sum, cotangent, rest["win"], full["bin"], rest["wout"], full["bout"], gain, shift
    )
    dwin, dwout = scatter.feed(fdw, own)
    grads, small2 = [], 0
    for block in blocks:
        *grads, part = cross_back(
            block, grads, out_at, ssg, first_sum, cq, ck, cv, cot_, clse, out, cross_proj, gain, cmark, qmark
        )
        small2 = small2 + part
    fsg, dq, dk, dv = grads
    keep, send, memory_grad = cross_weight(
        staged, pair, devices, dq, dk, dv, low, memory, cot_, ssg, sot, fsg, cross_proj
    )
    cross_sum = scatter(me, keep, send)
    upstream = after(fsg, cross_sum)
    grads, small1 = [], 0
    for block in blocks:
        *grads, part = self_back(block, grads, out_at, upstream, sq, sk, sv, sot, slse, out, smark, qmark)
        small1 = small1 + part
        if block == 0:
            cross_sum.core()
            upstream = after(upstream, cross_sum)
    dq, dk, dv = grads
    cross_sum.first()
    dq = after(dq, cross_sum)
    sums = jnp.concatenate([small1, small2, small3])
    keep, send = self_weight(staged, pair, devices, sums, dbin, dq, dk, dv, query)
    self_sum = scatter(me, keep, send)
    cross_sum.second()
    self_sum.core()
    upstream = after(fsg, self_sum, cross_sum)
    query_grad = self_input(upstream, dq, dk, dv, full["qk"], full["v"])
    self_sum.first()
    cross = cross_sum.last()
    self_sum.second()
    rows = self_sum.last()
    cross = cross.reshape(5, own, d)
    proj_grad = jnp.concatenate([rows[: 3 * own].reshape(3, own, d), cross[2:]])
    if staged:
        sums = rows[3 * own : 3 * own + 24, :own]
        dbin = rows[3 * own + 24, : dbin.shape[1] // devices]
    else:
        sum_up = functools.partial(lax.psum_scatter, axis_name=("dp", "fsdp"), scatter_dimension=1, tiled=True)
        sums, dbin = sum_up(sums), sum_up(dbin)[0]
    bias_g = jnp.concatenate([sums[0:3], sums[8:11]])
    gain_g = jnp.stack([sums[11], sums[19], sums[16]])
    shift_g = jnp.stack([sums[12], sums[20], sums[17]])
    return (
        mixed, query_grad, memory_grad, proj_grad, cross[1::-1], bias_g, gain_g, shift_g, dwin, dbin, dwout, sums[18],
    )


def solution(mesh):
    devices = mesh.size
    if dict(mesh.shape) == {"dp": 4, "fsdp": 8}:
        axes = ("x", "c", "z", "y")
        mesh = Mesh(mesh.devices.reshape(2, 2, 4, 2), axes)
        gather, scatter = Stages, Halving
    else:
        axes = ("dp", "fsdp")
        gather, scatter = Plain, Whole
    rows, mid, flat, row1 = P(axes, None), P(None, axes, None), P(None, axes), P(axes)
    return jax.shard_map(
        functools.partial(body, gather, scatter, devices),
        mesh=mesh,
        in_specs=(rows, rows, row1, row1, mid, mid, flat, flat, flat, rows, row1, rows, row1, rows),
        out_specs=(rows, rows, rows, mid, mid, flat, flat, flat, rows, row1, rows, row1),
        check_vma=False,
    )
```

```python
import functools

import jax
import jax.numpy as jnp
from jax import lax
from jax.experimental import pallas as pl
from jax.experimental.pallas import tpu as pltpu
from jax.sharding import Mesh
from jax.sharding import PartitionSpec as P

HEADS = 12
HEAD_DIM = 64
SEQ_MAX = 512
PAIRS = HEADS // 2
EPSILON = 1e-05
MASKED = 1e30
SCALE = HEAD_DIM ** (-0.5)
BF = jnp.bfloat16
F32 = jnp.float32
VMEM_LIMIT = 60 * 1024 * 1024


def dot(left, right):
    return jnp.dot(left, right, preferred_element_type=F32)


def dot_nt(left, right):
    return lax.dot_general(left, right, (((1,), (1,)), ((), ())), preferred_element_type=F32)


def norm_parts(resid):
    center = resid - jnp.mean(resid, axis=-1, keepdims=True)
    rstd = lax.rsqrt(jnp.mean(center * center, axis=-1, keepdims=True) + EPSILON)
    return center * rstd, rstd


def norm_back(unit, rstd, gain, upstream):
    scaled = upstream * gain
    mean_s = jnp.mean(scaled, axis=-1, keepdims=True)
    mean_su = jnp.mean(scaled * unit, axis=-1, keepdims=True)
    grad = rstd * (scaled - mean_s - unit * mean_su)
    return grad, col_sum(upstream * unit), col_sum(upstream)


def col_sum(rows):
    return jnp.sum(rows, axis=0, keepdims=True)


def place_rows(rows, count):
    parts = list(rows)
    parts.append(jnp.zeros((count - len(parts), parts[0].shape[1]), F32))
    return jnp.concatenate(parts, axis=0)


def gelu_parts(value):
    size = jnp.abs(value) * (0.5**0.5)
    bell = jnp.exp(-0.5 * value * value)
    t = 1.0 / (1.0 + 0.3275911 * size)
    poly = t * (0.254829592 + t * (-0.284496736 + t * (1.421413741 + t * (-1.453152027 + t * 1.061405429))))
    tail = 0.5 * poly * bell
    phi = jnp.where(value >= 0, 1.0 - tail, tail)
    return value * phi, phi + value * (bell * (1.0 / (2.0 * 3.141592653589793) ** 0.5))


def left_half(shape):
    return lax.broadcasted_iota(jnp.int32, shape, 1) < HEAD_DIM


def head_pair(side, pair):
    return pl.ds(pl.multiple_of(pair * 128 + side * HEAD_DIM, HEAD_DIM), HEAD_DIM)


def key_tile(tile, marks, side):
    left = left_half(tile.shape)
    return jnp.where(left, tile, marks) if side == 0 else jnp.where(left, marks, tile)


def query_tile(rows, marks, side):
    return jnp.concatenate([rows, marks] if side == 0 else [marks, rows], axis=0)


def attend_block(k_ref, qt_ref, vt_ref, kmark_ref, qmark_ref, ot_ref, lse_ref):
    kmark = kmark_ref[...]
    qmark = qmark_ref[0]
    ones = jnp.ones((16, SEQ_MAX), BF)

    def score(head):
        pair, side = head // 2, head % 2
        rows = slice(head * HEAD_DIM, (head + 1) * HEAD_DIM)
        tile = k_ref[:, pair * 128 : (pair + 1) * 128]
        return dot(key_tile(tile, kmark, side), query_tile(qt_ref[rows, :], qmark, side))

    def finish(head, peak, weights):
        rows = slice(head * HEAD_DIM, (head + 1) * HEAD_DIM)
        result = dot(jnp.concatenate([vt_ref[rows, :], ones], axis=0), weights)
        total = result[HEAD_DIM : HEAD_DIM + 1]
        ot_ref[rows, :] = (result[:HEAD_DIM] * (1.0 / total)).astype(BF)
        lse_ref[0, head : head + 1, :] = peak + jnp.log(total)

    for start in range(0, HEADS, 6):
        heads = range(start, start + 6)
        scores = [score(head) for head in heads]
        peaks = [jnp.max(s, axis=0, keepdims=True) for s in scores]
        weights = [jnp.exp(s - peak).astype(BF) for s, peak in zip(scores, peaks)]
        for head, peak, weight in zip(heads, peaks, weights):
            finish(head, peak, weight)


def attend_back_block(
    q_ref, k_ref, v_ref, qt_ref, kt_ref, ot_ref, do_ref, dot_ref, kmark_ref, qmark_ref, lse_ref, dqt_ref, dk_ref, dv_ref
):
    kmark = kmark_ref[...]
    qmark = qmark_ref[0]
    left = left_half((SEQ_MAX, 128))
    blank = jnp.zeros((HEAD_DIM, SEQ_MAX), BF)

    def begin(head):
        pair, side = head // 2, head % 2
        rows = slice(head * HEAD_DIM, (head + 1) * HEAD_DIM)
        cols = slice(pair * 128, (pair + 1) * 128)
        scores = dot(key_tile(k_ref[:, cols], kmark, side), query_tile(qt_ref[rows, :], qmark, side))
        up = dot_ref[rows, :]
        probs_grad = dot(v_ref[:, cols], query_tile(up, blank, side))
        return scores, probs_grad, col_sum(up.astype(F32) * ot_ref[rows, :].astype(F32))

    def middle(head, scores, probs_grad, center):
        probs = jnp.exp(scores - lse_ref[0, head : head + 1, :])
        return probs.astype(BF), (probs * (probs_grad - center)).astype(BF)

    def finish(head, probs, score_grad):
        rows = slice(head * HEAD_DIM, (head + 1) * HEAD_DIM)
        cols = slice(head // 2 * 128, (head // 2 + 1) * 128)
        dqt_ref[rows, :] = (dot(kt_ref[rows, :], score_grad) * SCALE).astype(BF)
        return dot(probs, do_ref[:, cols]), dot(score_grad, q_ref[:, cols])

    for start in range(0, HEADS, 4):
        heads = range(start, start + 4)
        begun = [begin(head) for head in heads]
        mid = [middle(head, *b) for head, b in zip(heads, begun)]
        done = [finish(head, *m) for head, m in zip(heads, mid)]
        for i in range(0, 4, 2):
            cols = slice((start + i) // 2 * 128, ((start + i) // 2 + 1) * 128)
            dv_ref[:, cols] = jnp.where(left, done[i][0], done[i + 1][0]).astype(BF)
            dk_ref[:, cols] = jnp.where(left, done[i][1], done[i + 1][1]).astype(BF)


def self_forward_kernel(
    x_ref, wqk_ref, wv_ref, bias_ref, kmark_ref, qmark_ref, q_ref, k_ref, v_ref, ot_ref, lse_ref, qt_s, vt_s
):
    x = x_ref[...]
    queries = ((dot(x, wqk_ref[0]) + bias_ref[0:1]).astype(BF)) * SCALE
    q_ref[...] = queries
    qt_s[...] = queries.T
    k_ref[...] = dot(x, wqk_ref[1]).astype(BF)
    values = (dot(x, wv_ref[0]) + bias_ref[1:2]).astype(BF)
    v_ref[...] = values
    vt_s[...] = values.T
    attend_block(k_ref, qt_s, vt_s, kmark_ref, qmark_ref, ot_ref, lse_ref)


def cross_forward_kernel(
    x_ref, mem_ref, sot_ref, wo_ref, w_ref, bias_ref, gain_ref, shift_ref, kmark_ref, qmark_ref,
    first_sum_ref, low_ref, q_ref, k_ref, v_ref, ot_ref, lse_ref, second_sum_ref, qt_s, vt_s,
):
    mem = mem_ref[...]
    k_ref[...] = dot(mem, w_ref[1]).astype(BF)
    values = (dot(mem, w_ref[2]) + bias_ref[4:5]).astype(BF)
    v_ref[...] = values
    vt_s[...] = values.T
    first_sum = x_ref[...].astype(F32) + (dot(sot_ref[...].T, wo_ref[0]) + bias_ref[2:3])
    first_sum_ref[...] = first_sum
    unit, _ = norm_parts(first_sum)
    first = unit * gain_ref[0:1] + shift_ref[0:1]
    low = first.astype(BF)
    low_ref[...] = low
    queries = ((dot(low, w_ref[0]) + bias_ref[3:4]).astype(BF)) * SCALE
    q_ref[...] = queries
    qt_s[...] = queries.T
    attend_block(k_ref, qt_s, vt_s, kmark_ref, qmark_ref, ot_ref, lse_ref)
    second_sum_ref[...] = first + (dot(ot_ref[...].T, wo_ref[1]) + bias_ref[5:6])


def feed_kernel(
    own, ss_ref, cot_ref, win_ref, bin_ref, wout_ref, bout_ref, gain_ref, shift_ref,
    mixed_ref, ssg_ref, dw_ref, dbin_ref, small_ref,
    low_s, lowt_s, hid_s, slope_s, acc_s, z_s, din_s, dout_s, sems,
):
    phase, chunk = pl.program_id(0), pl.program_id(1)
    chunks = pl.num_programs(1)
    last = chunks - 1
    slot = chunk % 2
    width, d = dout_s.shape[1] * dout_s.shape[2], dout_s.shape[3]
    parts = dout_s.shape[1]

    def wout():
        if not own:
            return wout_ref[...]
        groups = wout_ref[...].astype(F32)
        return jnp.concatenate([groups[:, i] for i in range(groups.shape[1])], axis=0).reshape(width, d).astype(BF)

    def sends(slot, chunk):
        if own:
            group = width // parts
            rows = pl.ds(pl.multiple_of(chunk * group, group), group)
            outs = [
                pltpu.make_async_copy(
                    dout_s.at[slot, part], dw_ref.at[rows, pl.ds((chunks + part) * width, width)], sems.at[1 + part, slot]
                )
                for part in range(parts)
            ]
        else:
            cols = pl.ds(pl.multiple_of((chunks + chunk) * width, width), width)
            outs = [pltpu.make_async_copy(dout_s.at[slot, 0], dw_ref.at[:, cols], sems.at[1, slot])]
        cols = pl.ds(pl.multiple_of(chunk * width, width), width)
        return [pltpu.make_async_copy(din_s.at[slot], dw_ref.at[:, cols], sems.at[0, slot])] + outs

    @pl.when((phase == 0) & (chunk == 0))
    def _():
        unit, _ = norm_parts(ss_ref[...])
        second = unit * gain_ref[1:2] + shift_ref[1:2]
        low = second.astype(BF)
        low_s[...] = low
        lowt_s[...] = low.T
        acc_s[...] = second + bout_ref[...]

    @pl.when(phase == 0)
    def _():
        weights_in, weights_out, count = win_ref[0], wout(), low_s.shape[0] // 4
        blocks = [slice(i * count, (i + 1) * count) for i in range(4)]
        pres = [dot(low_s[block, :], weights_in) + bin_ref[...] for block in blocks]
        both = [gelu_parts(pre) for pre in pres]
        for block, (hidden, slope) in zip(blocks, both):
            hidden = hidden.astype(BF)
            hid_s[chunk, block] = hidden
            slope_s[chunk, block] = slope
            acc_s[block, :] += dot(hidden, weights_out)

    @pl.when((phase == 1) & (chunk == 0))
    def _():
        unit, rstd = norm_parts(acc_s[...])
        mixed_ref[...] = (unit * gain_ref[2:3] + shift_ref[2:3]).astype(BF)
        third, dgain, dshift = norm_back(unit, rstd, gain_ref[2:3], cot_ref[...].astype(F32))
        z = third.astype(BF)
        z_s[...] = z
        acc_s[...] = third
        small_ref[...] = place_rows([dgain, dshift, col_sum(z.astype(F32))], 8)

    @pl.when((phase == 1) & (chunk >= 2))
    def _():
        for copy in sends(slot, chunk - 2):
            copy.wait()

    @pl.when(phase == 1)
    def _():
        z = z_s[...]
        pre_grad = (dot_nt(z, wout()) * slope_s[chunk]).astype(BF)
        dbin_ref[...] = col_sum(pre_grad.astype(F32))
        dout = dot(hid_s[chunk].T, z)
        if own:
            groups = dout.reshape(width // (parts * own), parts, own, d)
            for part in range(parts):
                dout_s[slot, part] = groups[:, part].reshape(width // parts, d).astype(BF)
        else:
            dout_s[slot] = dout.reshape(dout_s.shape[1:]).astype(BF)
        din_s[slot] = dot(lowt_s[...], pre_grad).astype(BF)
        for copy in sends(slot, chunk):
            copy.start()
        acc_s[...] += dot_nt(pre_grad, win_ref[0])

    @pl.when((phase == 1) & (chunk == last))
    def _():
        unit, rstd = norm_parts(ss_ref[...])
        grad, dgain, dshift = norm_back(unit, rstd, gain_ref[1:2], acc_s[...])
        ssg_ref[...] = grad
        small_ref[3:5] = jnp.concatenate([dgain, dshift], axis=0)
        for copy in sends(1 - slot, chunk - 1) + sends(slot, chunk):
            copy.wait()


def cross_back_kernel(
    ssg_ref, fs_ref, q_ref, k_ref, v_ref, ot_ref, lse_ref, wo_ref, w_ref, gain_ref, kmark_ref, qmark_ref, *refs
):
    fsg_ref, dq_ref, dk_ref, dv_ref, small_ref, qt_s, kt_s, do_s, dot_s, dqt_s = refs[-10:]
    upstream = ssg_ref[...]
    branch = upstream.astype(BF)
    mixed_grad = dot_nt(branch, wo_ref[0]).astype(BF)
    do_s[...] = mixed_grad
    dot_s[...] = mixed_grad.T
    qt_s[...] = q_ref[...].T
    kt_s[...] = k_ref[...].T
    attend_back_block(
        q_ref, k_ref, v_ref, qt_s, kt_s, ot_ref, do_s, dot_s, kmark_ref, qmark_ref, lse_ref, dqt_s, dk_ref, dv_ref
    )
    dq = dqt_s[...].T
    dq_ref[...] = dq
    first_grad = upstream + dot_nt(dq, w_ref[0])
    unit, rstd = norm_parts(fs_ref[...])
    grad, dgain, dshift = norm_back(unit, rstd, gain_ref[0:1], first_grad)
    fsg_ref[...] = grad
    sums = [col_sum(dq.astype(F32)), col_sum(dv_ref[...].astype(F32)), col_sum(branch.astype(F32)), dgain, dshift]
    small_ref[...] = place_rows(sums, 8)


def self_back_kernel(fsg_ref, q_ref, k_ref, v_ref, ot_ref, lse_ref, wo_ref, kmark_ref, qmark_ref, *refs):
    dq_ref, dk_ref, dv_ref, small_ref, qt_s, kt_s, do_s, dot_s, dqt_s = refs[-9:]
    branch = fsg_ref[...].astype(BF)
    mixed_grad = dot_nt(branch, wo_ref[0]).astype(BF)
    do_s[...] = mixed_grad
    dot_s[...] = mixed_grad.T
    qt_s[...] = q_ref[...].T
    kt_s[...] = k_ref[...].T
    attend_back_block(
        q_ref, k_ref, v_ref, qt_s, kt_s, ot_ref, do_s, dot_s, kmark_ref, qmark_ref, lse_ref, dqt_s, dk_ref, dv_ref
    )
    dq = dqt_s[...].T
    dq_ref[...] = dq
    sums = [col_sum(dq.astype(F32)), col_sum(dv_ref[...].astype(F32)), col_sum(branch.astype(F32))]
    small_ref[...] = place_rows(sums, 8)


def bring(sources, slots, sems):
    copies = [pltpu.make_async_copy(s, v, sems.at[i]) for i, (s, v) in enumerate(zip(sources, slots))]
    for copy in copies:
        copy.start()

    def get(i):
        copies[i].wait()
        return slots[i][...]

    return get


def lay_out(out_s, at, grads, more=None):
    places = out_s.shape[2] * out_s.shape[3]
    d = out_s.shape[5]
    own = d // (4 * places)
    for quarter in range(4):
        first = quarter * places
        parts = [g[first * own : (first + places) * own].reshape(places, own, d) for g in grads]
        if more is not None:
            parts.append(jnp.stack([more(first + i) for i in range(places)]))
        rows = jnp.concatenate(parts, axis=1).astype(BF)
        count = rows.shape[1]
        out_s[quarter // 2, quarter % 2, :, :, at : at + count] = rows.reshape(*out_s.shape[2:4], count, d)


def hand_out(out_s, me, keep_ref, send_ref, sems):
    moves = []
    for x in range(2):
        moves.append(pltpu.make_async_copy(out_s.at[x, me], keep_ref.at[x], sems.at[2 * x]))
        moves.append(pltpu.make_async_copy(out_s.at[x, 1 - me], send_ref.at[x], sems.at[2 * x + 1]))
    for move in moves:
        move.start()
    return moves


def cross_weight_kernel(staged, me_ref, *refs):
    sources, (keep_ref, send_ref), slots = refs[:9], refs[9:11], refs[11:20]
    out_s, sems, out_sems = refs[20:]
    get = bring(sources, slots, sems)
    memt = get(0).T
    dk = get(1)
    keys = dot(memt, dk)
    dv = get(2)
    values = dot(memt, dv)
    if staged:
        lay_out(out_s, 0, [keys, values])
    else:
        out_s[0], out_s[1] = keys.astype(BF), values.astype(BF)
    outs = [dot(get(3), get(4).astype(BF)), dot(get(5), get(6).astype(BF))]
    if staged:
        lay_out(out_s, 2 * outs[0].shape[0] // 32, outs)
    else:
        out_s[2], out_s[3] = outs[0].astype(BF), outs[1].astype(BF)
    queries = dot(get(7).T, get(8))
    if staged:
        lay_out(out_s, 4 * outs[0].shape[0] // 32, [queries])
        moves = hand_out(out_s, me_ref[0], keep_ref, send_ref, out_sems)
    else:
        out_s[4] = queries.astype(BF)
        send_ref[0] = 0
        moves = [pltpu.make_async_copy(out_s, keep_ref, out_sems.at[0])]
        moves[0].start()
    for move in moves:
        move.wait()


def self_last_kernel(
    staged, me_ref, fsg_ref, q_ref, k_ref, v_ref, ot_ref, lse_ref, wo_ref, kmark_ref, qmark_ref, sums_ref, dbin_ref, x_ref,
    *refs,
):
    (keep_ref, send_ref), outs = refs[3:5], refs[5:8]
    qt_s, kt_s, do_s, dot_s, dqt_s, dq_s, dk_s, dv_s, x_s, out_s, sems, out_sems = refs[8:]
    grads = (dq_s, dk_s, dv_s)
    before = x_s.shape[0] - SEQ_MAX
    mine = pl.ds(before, SEQ_MAX)
    loads = [pltpu.make_async_copy(x_ref, x_s, sems.at[0])]
    if before:
        early = pl.ds(0, before)
        loads += [
            pltpu.make_async_copy(o.at[early], g.at[early], sems.at[1 + i]) for i, (o, g) in enumerate(zip(outs, grads))
        ]
    for load in loads:
        load.start()
    branch = fsg_ref[...].astype(BF)
    mixed_grad = dot_nt(branch, wo_ref[0]).astype(BF)
    do_s[...] = mixed_grad
    dot_s[...] = mixed_grad.T
    qt_s[...] = q_ref[...].T
    kt_s[...] = k_ref[...].T
    attend_back_block(
        q_ref, k_ref, v_ref, qt_s, kt_s, ot_ref, do_s, dot_s, kmark_ref, qmark_ref, lse_ref, dqt_s,
        dk_s.at[mine], dv_s.at[mine],
    )
    dq_s[mine] = dqt_s[...].T
    moves = [
        pltpu.make_async_copy(g.at[mine], o.at[mine], sems.at[4 + i]) for i, (g, o) in enumerate(zip(grads, outs))
    ]
    for load in loads:
        load.wait()
    for move in moves:
        move.start()
    last = [col_sum(dq_s[mine].astype(F32)), col_sum(dv_s[mine].astype(F32)), col_sum(branch.astype(F32))]
    sums = sums_ref[...] + place_rows(last, 16)
    xt = x_s[...].T
    if not staged:
        for i in range(3):
            out_s[i] = dot(xt, grads[i][...]).astype(BF)
        send_ref[...] = sums
        moves.append(pltpu.make_async_copy(out_s, keep_ref, out_sems.at[0]))
        moves[-1].start()
    else:
        d, wide = sums_ref.shape[1], dbin_ref.shape[1]
        lines = jnp.broadcast_to(dbin_ref[...], (8, wide))
        last_row = lax.broadcasted_iota(jnp.int32, (16, d), 0) == 15

        def small(device):
            rows, line = sums, lines
            if device:
                rows = pltpu.roll(rows, d - d // 32 * device, 1)
                line = pltpu.roll(lines, wide - wide // 32 * device, 1)
            line = line[:, :d]
            return jnp.where(last_row, jnp.concatenate([line, line], axis=0), rows)

        lay_out(out_s, 0, [dot(xt, dq_s[...]), dot(xt, dk_s[...])])
        lay_out(out_s, 2 * d // 32, [dot(xt, dv_s[...])], small)
        moves += hand_out(out_s, me_ref[0], keep_ref, send_ref, out_sems)
    for move in moves:
        move.wait()


def memory_input_kernel(dk_ref, dv_ref, wk_ref, wv_ref, mg_ref):
    mg_ref[...] = dot_nt(dk_ref[...], wk_ref[0]) + dot_nt(dv_ref[...], wv_ref[0])


def self_input_kernel(fsg_ref, dq_ref, dk_ref, dv_ref, wqk_ref, wv_ref, qg_ref):
    qg_ref[...] = (
        fsg_ref[...]
        + dot_nt(dq_ref[...], wqk_ref[0]) + dot_nt(dk_ref[...], wqk_ref[1]) + dot_nt(dv_ref[...], wv_ref[0])
    )


def pick(first, second, other):
    return jnp.where(other == 0, first, second)


def first_stage_kernel(me_ref, keep_ref, got_ref, sl_ref, kl_ref, sr_ref, kr_ref):
    total = keep_ref[...].astype(F32) + got_ref[...].astype(F32)
    half = total.shape[4] // 2
    left, right = total[..., :half], total[..., half:]
    sl_ref[...] = pick(left[1], left[0], me_ref[0]).astype(BF)
    kl_ref[...] = pick(left[0], left[1], me_ref[0]).astype(BF)
    sr_ref[...] = pick(right[:, :, 1], right[:, :, 0], me_ref[1]).astype(BF)
    kr_ref[...] = pick(right[:, :, 0], right[:, :, 1], me_ref[1]).astype(BF)


def second_stage_kernel(me_ref, kl_ref, gl_ref, kr_ref, gr_ref, sl_ref, ml_ref, sr_ref, mr_ref):
    left = kl_ref[...].astype(F32) + gl_ref[...].astype(F32)
    right = kr_ref[...].astype(F32) + gr_ref[...].astype(F32)
    sl_ref[...] = pick(left[:, 1], left[:, 0], me_ref[1]).astype(BF)
    ml_ref[...] = pick(left[:, 0], left[:, 1], me_ref[1]).astype(BF)
    sr_ref[...] = pick(right[1], right[0], me_ref[0]).astype(BF)
    mr_ref[...] = pick(right[0], right[1], me_ref[0]).astype(BF)


def third_stage_kernel(me_ref, kl_ref, gl_ref, kr_ref, gr_ref, own_ref, *outs):
    total = jnp.concatenate(
        [kl_ref[...].astype(F32) + gl_ref[...].astype(F32), kr_ref[...].astype(F32) + gr_ref[...].astype(F32)], axis=2
    )
    me = me_ref[2]
    for step, ref in enumerate((own_ref, *outs)):
        index = (me + step) % 4
        value = jnp.where(
            index < 2, jnp.where(index == 0, total[0], total[1]), jnp.where(index == 2, total[2], total[3])
        )
        ref[...] = value.astype(ref.dtype)


def final_stage_kernel(own, *refs):
    cross_refs, self_refs, outs = refs[:4], refs[4:8], refs[8:]
    proj_ref, out_ref, bias_ref, gain_ref, shift_ref, hidden_ref, last_ref = outs
    cross = functools.reduce(jnp.add, [r[...].astype(F32) for r in cross_refs])
    selfs = functools.reduce(jnp.add, [r[...].astype(F32) for r in self_refs])
    for i in range(3):
        proj_ref[i] = selfs[i * own : (i + 1) * own]
    for ref, index, at in ((proj_ref, 4, 0), (proj_ref, 5, 1), (out_ref, 1, 2), (out_ref, 0, 3), (proj_ref, 3, 4)):
        ref[index] = cross[at * own : (at + 1) * own]
    sums = selfs[3 * own : 3 * own + 16, :128]
    bias_ref[...] = sums[0:6, :own]
    for ref, lines in ((gain_ref, (6, 11, 8)), (shift_ref, (7, 12, 9))):
        for i, line in enumerate(lines):
            ref[i : i + 1] = sums[line : line + 1, :own]
    hidden_ref[...] = sums[15:16, : hidden_ref.shape[1]]
    last_ref[...] = sums[10:11, :own]


def stage_call(kernel, me, args, outs, name):
    data = sum(a.size * a.dtype.itemsize for a in args)
    return pl.pallas_call(
        kernel,
        in_specs=[pl.BlockSpec(memory_space=pltpu.SMEM)] + [pl.BlockSpec(memory_space=pltpu.VMEM)] * len(args),
        out_specs=[pl.BlockSpec(memory_space=pltpu.VMEM)] * len(outs),
        out_shape=outs,
        compiler_params=pltpu.CompilerParams(vmem_limit_bytes=VMEM_LIMIT),
        cost_estimate=cost(data, 2 * data),
        name=name,
    )(me, *args)


def first_stage(me, keep, got):
    x, z, y, rows, d = keep.shape
    line = lambda *lead: pl.BlockSpec((*lead, rows, d // 2), lambda i: (i, 0, 0, 0))
    both = pl.BlockSpec((x, 1, y, rows, d), lambda i: (0, i, 0, 0, 0))
    side = pl.BlockSpec((x, 1, rows, d // 2), lambda i: (0, i, 0, 0))
    left, right = shape((z, y, rows, d // 2), BF), shape((x, z, rows, d // 2), BF)
    return pl.pallas_call(
        first_stage_kernel,
        grid=(z,),
        in_specs=[pl.BlockSpec(memory_space=pltpu.SMEM), both, both],
        out_specs=[line(1, y), line(1, y), side, side],
        out_shape=[left, left, right, right],
        compiler_params=params(("arbitrary",)),
        cost_estimate=cost(keep.size, 6 * keep.size),
        name="first_stage",
    )(me, keep, got)


def row_block(width):
    return pl.BlockSpec((SEQ_MAX, width), lambda b: (b, 0))


def col_block(height):
    return pl.BlockSpec((height, SEQ_MAX), lambda b: (0, b))


def lead_block(rows):
    return pl.BlockSpec((1, rows, SEQ_MAX), lambda b: (b, 0, 0))


def whole(array, **kw):
    zeros = (0,) * array.ndim
    return pl.BlockSpec(array.shape, lambda *_: zeros, pipeline_mode=pl.Buffered(1))


def planes(array, start, count):
    return pl.BlockSpec(
        (count, *array.shape[1:]), lambda *_: (start // count, 0, 0), pipeline_mode=pl.Buffered(1)
    )


def params(semantics):
    return pltpu.CompilerParams(vmem_limit_bytes=VMEM_LIMIT, dimension_semantics=semantics)


def cost(flops, data, exps=0):
    return pl.CostEstimate(flops=int(flops), bytes_accessed=int(data), transcendentals=int(exps))


def shape(dims, kind):
    return jax.ShapeDtypeStruct(dims, kind)


def self_forward(x, wqk, wv, bias, kmark, qmark):
    rows, d = x.shape
    blocks = rows // SEQ_MAX
    act = shape((rows, d), BF)
    return pl.pallas_call(
        self_forward_kernel,
        grid=(blocks,),
        in_specs=[row_block(d), whole(wqk), whole(wv), whole(bias), row_block(128), lead_block(HEAD_DIM)],
        out_specs=[row_block(d), row_block(d), row_block(d), col_block(d), lead_block(16)],
        out_shape=[act, act, act, shape((d, rows), BF), shape((blocks, 16, SEQ_MAX), F32)],
        scratch_shapes=[pltpu.VMEM((d, SEQ_MAX), BF)] * 2,
        compiler_params=params(("arbitrary",)),
        cost_estimate=cost(20e9, 12e6),
        name="self_forward",
    )(x, wqk, wv, bias, kmark, qmark)


def cross_forward(x, mem, sot, wo, wo_at, w, bias, gain, shift, kmark, qmark):
    rows, d = x.shape
    blocks = rows // SEQ_MAX
    act, wide = shape((rows, d), BF), shape((rows, d), F32)
    return pl.pallas_call(
        cross_forward_kernel,
        grid=(blocks,),
        in_specs=[
            row_block(d), row_block(d), col_block(d), planes(wo, wo_at, 2), planes(w, 0, 3), whole(bias), whole(gain),
            whole(shift),
            row_block(128), lead_block(HEAD_DIM),
        ],
        out_specs=[row_block(d)] * 5 + [col_block(d), lead_block(16), row_block(d)],
        out_shape=[wide, act, act, act, act, shape((d, rows), BF), shape((blocks, 16, SEQ_MAX), F32), wide],
        scratch_shapes=[pltpu.VMEM((d, SEQ_MAX), BF)] * 2,
        compiler_params=params(("arbitrary",)),
        cost_estimate=cost(24e9, 20e6),
        name="cross_forward",
    )(x, mem, sot, wo, w, bias, gain, shift, kmark, qmark)


def feed(second_sum, cot, win, bin_, wout, bout, gain, shift):
    rows, d = second_sum.shape
    width = win.shape[2]
    ff = bin_.shape[1]
    chunks = ff // width
    own = wout.shape[2] if wout.ndim == 4 else 0
    fixed = lambda p, j: (0, 0)
    parts = chunks if own else 1
    if own:
        wout_spec = pl.BlockSpec((parts, width // (parts * own), own, d), lambda p, j: (1, j, 0, 0))
    else:
        wout_spec = pl.BlockSpec((width, d), lambda p, j: (j, 0))
    return pl.pallas_call(
        functools.partial(feed_kernel, own),
        grid=(2, chunks),
        in_specs=[
            whole(second_sum), whole(cot),
            pl.BlockSpec((1, d, width), lambda p, j: (jnp.where(j == 0, 3, 9 + j) if own else j, 0, 0)),
            pl.BlockSpec((1, width), lambda p, j: (0, j)),
            wout_spec, whole(bout), whole(gain), whole(shift),
        ],
        out_specs=[
            pl.BlockSpec((rows, d), fixed),
            pl.BlockSpec((rows, d), fixed),
            pl.BlockSpec(memory_space=pl.ANY),
            pl.BlockSpec((1, width), lambda p, j: (0, j * p)),
            pl.BlockSpec((8, d), fixed),
        ],
        out_shape=[
            shape((rows, d), BF), shape((rows, d), F32), shape((d, 2 * ff), BF),
            shape((1, ff), F32), shape((8, d), F32),
        ],
        scratch_shapes=[
            pltpu.VMEM((rows, d), BF), pltpu.VMEM((d, rows), BF),
            pltpu.VMEM((chunks, rows, width), BF), pltpu.VMEM((chunks, rows, width), F32),
            pltpu.VMEM((rows, d), F32), pltpu.VMEM((rows, d), BF),
            pltpu.VMEM((2, d, width), BF), pltpu.VMEM((2, parts, width // parts, d), BF),
            pltpu.SemaphoreType.DMA((1 + parts, 2)),
        ],
        compiler_params=params(("arbitrary", "arbitrary")),
        cost_estimate=cost(40e9, 40e6),
        name="feed",
    )(second_sum, cot, win, bin_, wout, bout, gain, shift)


def back_scratch(d):
    return (
        [pltpu.VMEM((d, SEQ_MAX), BF)] * 2 + [pltpu.VMEM((SEQ_MAX, d), BF)] + [pltpu.VMEM((d, SEQ_MAX), BF)] * 2
    )


def at_row(block, width):
    return pl.BlockSpec((SEQ_MAX, width), lambda b: (block, 0))


def at_col(block, height):
    return pl.BlockSpec((height, SEQ_MAX), lambda b: (0, block))


def at_lead(block, rows):
    return pl.BlockSpec((1, rows, SEQ_MAX), lambda b: (block, 0, 0))


def one_back(kernel, block, before, args, specs, outs, name):
    d = outs[0].shape[1]
    kept = [pl.BlockSpec(memory_space=pl.ANY)] * len(before)
    return pl.pallas_call(
        kernel,
        grid=(1,),
        in_specs=specs + kept,
        out_specs=[at_row(block, d)] * len(outs) + [pl.BlockSpec((8, d), lambda b: (0, 0))],
        out_shape=outs + [shape((8, d), F32)],
        scratch_shapes=back_scratch(d),
        input_output_aliases={len(args) + i: i for i in range(len(before))},
        compiler_params=params(("arbitrary",)),
        cost_estimate=cost(25e9, 15e6),
        name=name,
    )(*args, *before)


def cross_back(block, before, wo_at, ssg, first_sum, q, k, v, ot, lse, wo, w, gain, kmark, qmark):
    rows, d = first_sum.shape
    act = shape((rows, d), BF)
    specs = [at_row(block, d)] * 5 + [
        at_col(block, d), at_lead(block, 16), planes(wo, wo_at + 1, 1), planes(w, 0, 1), whole(gain), at_row(block, 128), at_lead(block, HEAD_DIM),
    ]
    args = (ssg, first_sum, q, k, v, ot, lse, wo, w, gain, kmark, qmark)
    return one_back(
        cross_back_kernel, block, before, args, specs, [shape((rows, d), F32), act, act, act], f"cross_back_{block}"
    )


def self_back(block, before, wo_at, fsg, q, k, v, ot, lse, wo, kmark, qmark):
    rows, d = fsg.shape
    act = shape((rows, d), BF)
    specs = [at_row(block, d)] * 4 + [
        at_col(block, d), at_lead(block, 16), planes(wo, wo_at, 1), at_row(block, 128), at_lead(block, HEAD_DIM),
    ]
    args = (fsg, q, k, v, ot, lse, wo, kmark, qmark)
    return one_back(self_back_kernel, block, before, args, specs, [act, act, act], f"self_back_{block}")


def weight_outs(staged, count, extra, devices, d):
    if not staged:
        return [shape((count, d, d), BF), shape((1,), jnp.int32)], pltpu.VMEM((count, d, d), BF)
    rows = count * d // devices + extra
    half = shape((2, 4, 2, rows, d), BF)
    return [half, half], pltpu.VMEM((2, 2, 4, 2, rows, d), BF)


def cross_weight(staged, me, devices, dq, dk, dv, low, mem, ot, ssg, sot, fsg):
    rows, d = dq.shape
    args = (mem, dk, dv, ot, ssg, sot, fsg, low, dq)
    anywhere = pl.BlockSpec(memory_space=pl.ANY)
    outs, scratch = weight_outs(staged, 5, 0, devices, d)
    last = anywhere if staged else pl.BlockSpec(memory_space=pltpu.SMEM)
    return pl.pallas_call(
        functools.partial(cross_weight_kernel, staged),
        in_specs=[pl.BlockSpec(memory_space=pltpu.SMEM)] + [anywhere] * 9,
        out_specs=[anywhere, last],
        out_shape=outs,
        scratch_shapes=[pltpu.VMEM(a.shape, a.dtype) for a in args] + [
            scratch, pltpu.SemaphoreType.DMA((9,)), pltpu.SemaphoreType.DMA((4,)),
        ],
        compiler_params=pltpu.CompilerParams(vmem_limit_bytes=VMEM_LIMIT),
        cost_estimate=cost(9e9, 20e6),
        name="cross_weight",
    )(me, *args)


def self_last(staged, me, devices, block, before, wo_at, fsg, q, k, v, ot, lse, wo, kmark, qmark, sums, dbin, x):
    rows, d = x.shape
    anywhere, here = pl.BlockSpec(memory_space=pl.ANY), pl.BlockSpec(memory_space=pltpu.VMEM)
    outs, scratch = weight_outs(staged, 3, 16, devices, d)
    act = shape((rows, d), BF)
    args = (me, fsg, q, k, v, ot, lse, wo, kmark, qmark, sums, dbin, x)
    if not before:
        before = [jnp.zeros((rows, d), BF)] * 3
    fixed = lambda array: pl.BlockSpec(array.shape, lambda b: (0,) * array.ndim)
    if not staged:
        outs[1] = shape((16, d), F32)
    return pl.pallas_call(
        functools.partial(self_last_kernel, staged),
        grid=(1,),
        in_specs=[pl.BlockSpec(memory_space=pltpu.SMEM)] + [at_row(block, d)] * 4 + [
            at_col(block, d), at_lead(block, 16), planes(wo, wo_at, 1), at_row(block, 128), at_lead(block, HEAD_DIM),
            fixed(sums), fixed(dbin), anywhere,
        ] + [anywhere] * 3,
        out_specs=[anywhere, anywhere if staged else fixed(outs[1])] + [anywhere] * 3,
        out_shape=outs + [act] * 3,
        scratch_shapes=back_scratch(d) + [pltpu.VMEM((rows, d), BF)] * 4 + [
            scratch, pltpu.SemaphoreType.DMA((7,)), pltpu.SemaphoreType.DMA((4,)),
        ],
        input_output_aliases={len(args) + i: 2 + i for i in range(3)},
        compiler_params=params(("arbitrary",)),
        cost_estimate=cost(25e9, 20e6),
        name="self_last",
    )(*args, *before)


def memory_input(dk, dv, w):
    rows, d = dk.shape
    return pl.pallas_call(
        memory_input_kernel,
        grid=(rows // SEQ_MAX,),
        in_specs=[row_block(d)] * 2 + [planes(w, 1, 1), planes(w, 2, 1)],
        out_specs=row_block(d),
        out_shape=shape((rows, d), F32),
        compiler_params=params(("arbitrary",)),
        cost_estimate=cost(3e9, 9e6),
        name="memory_input",
    )(dk, dv, w, w)


def self_input(fsg, dq, dk, dv, wqk, wv):
    rows, d = fsg.shape
    return pl.pallas_call(
        self_input_kernel,
        grid=(rows // SEQ_MAX,),
        in_specs=[row_block(d)] * 4 + [whole(wqk), whole(wv)],
        out_specs=row_block(d),
        out_shape=shape((rows, d), F32),
        compiler_params=params(("arbitrary",)),
        cost_estimate=cost(4e9, 14e6),
        name="self_input",
    )(fsg, dq, dk, dv, wqk, wv)


def key_marks(seg):
    odd = (seg & 1)[:, None]
    lane = lax.broadcasted_iota(jnp.int32, (seg.shape[0], 128), 1) % HEAD_DIM
    return jnp.where(lane == 0, 1 - odd, jnp.where(lane == 1, odd, 0)).astype(BF)


def query_marks(seg):
    odd = (seg & 1).reshape(-1, 1, SEQ_MAX)
    row = lax.broadcasted_iota(jnp.int32, (odd.shape[0], HEAD_DIM, SEQ_MAX), 1)
    return jnp.where(row == 0, odd, jnp.where(row == 1, 1 - odd, 0)).astype(BF) * (-MASKED)


def swap(value, name):
    return lax.ppermute(value, name, [(0, 1), (1, 0)])


class Halving:
    def __init__(self, me, keep, send):
        self.me, self.keep, self.out = me, [keep], [send]

    def core(self):
        got = swap(self.out[0], "c")
        sl, kl, sr, kr = first_stage(self.me, self.keep[0], got)
        self.keep, self.out = [kl, kr], [sl, sr]

    def first(self):
        (kl, kr), (sl, sr) = self.keep, self.out
        gl, gr = swap(sl, "x"), swap(sr, "y")
        z, _, rows, half = kl.shape
        piece = shape((z, rows, half), BF)
        sl, ml, sr, mr = stage_call(second_stage_kernel, self.me, (kl, gl, kr, gr), [piece] * 4, "second_stage")
        self.keep, self.out = [ml, mr], [sl, sr]

    def second(self):
        (kl, kr), (sl, sr) = self.keep, self.out
        gl, gr = swap(sl, "y"), swap(sr, "x")
        _, rows, half = kl.shape
        piece = (rows, 2 * half)
        outs = [shape(piece, F32)] + [shape(piece, BF)] * 3
        own, *self.out = stage_call(third_stage_kernel, self.me, (kl, gl, kr, gr), outs, "third_stage")
        self.keep = [own]

    def last(self):
        steps = zip(range(1, 4), self.out)
        return self.keep + [lax.ppermute(out, "z", [(i, (i + step) % 4) for i in range(4)]) for step, out in steps]

    @staticmethod
    def finish(cross, selfs, small, dbin, own, devices):
        d = cross[0].shape[1]
        wide = dbin.shape[1] // devices
        outs = [
            shape(dims, F32)
            for dims in ((6, own, d), (2, own, d), (6, own), (3, own), (3, own), (1, wide), (1, own))
        ]
        args = cross + selfs
        proj, out, bias, gain, shift, hidden, last = pl.pallas_call(
            functools.partial(final_stage_kernel, own),
            in_specs=[pl.BlockSpec(memory_space=pltpu.VMEM)] * 8,
            out_specs=[pl.BlockSpec(memory_space=pltpu.VMEM)] * 7,
            out_shape=outs,
            compiler_params=pltpu.CompilerParams(vmem_limit_bytes=VMEM_LIMIT),
            cost_estimate=cost(2e6, 3e6),
            name="final_stage",
        )(*args)
        return proj, out, bias, gain, shift, hidden.reshape(-1), last.reshape(-1)

    @staticmethod
    def feed(grads, own):
        sums = lax.psum_scatter(grads, ("x", "c", "z", "y"), scatter_dimension=0, tiled=True).astype(F32)
        half = sums.shape[1] // 2
        d = grads.shape[0]
        return sums[:, :half], sums[:, half:].reshape(own, -1, d).swapaxes(0, 1).reshape(-1, d)


class Whole:
    def __init__(self, me, grads, _):
        self.grads, self.out, self.keep = grads, (), ()

    def core(self):
        pass

    first = second = core

    def last(self):
        sums = lax.psum_scatter(self.grads, ("dp", "fsdp"), scatter_dimension=1, tiled=True).astype(F32)
        return sums.reshape(-1, sums.shape[2])

    @staticmethod
    def finish(cross, selfs, small, dbin, own, devices):
        sum_up = functools.partial(lax.psum_scatter, axis_name=("dp", "fsdp"), scatter_dimension=1, tiled=True)
        small, dbin = sum_up(small), sum_up(dbin)[0]
        cross, selfs = cross.reshape(5, own, -1), selfs.reshape(3, own, -1)
        proj = jnp.concatenate([selfs, cross[4:], cross[:2]])
        gain, shift = jnp.stack([small[6], small[11], small[8]]), jnp.stack([small[7], small[12], small[9]])
        return proj, cross[3:1:-1], small[0:6], gain, shift, dbin, small[10]

    @staticmethod
    def feed(grads, own):
        sum_up = functools.partial(lax.psum_scatter, axis_name=("dp", "fsdp"), scatter_dimension=0, tiled=True)
        half, d = grads.shape[1] // 2, grads.shape[0]
        dwin = sum_up(grads[:, :half]).astype(F32)
        return dwin, sum_up(grads[:, half:].reshape(d, -1, d).swapaxes(0, 1).reshape(-1, d)).astype(F32)


def after(value, *sums):
    value, outs = lax.optimization_barrier((value, [s.out for s in sums]))
    for s, s.out in zip(sums, outs):
        pass
    return value


def hold(sums, value):
    sums.keep = lax.optimization_barrier((sums.keep, value))[0]


def take_turns(value):
    me = lax.axis_index("z")
    parts = [value]
    for step in range(3, 0, -1):
        parts.append(lax.ppermute(value, "z", [(i, (i + step) % 4) for i in range(4)]))
    return jnp.stack([lax.select_n((j - me) % 4, *parts) for j in range(4)], axis=1)


def take_pair(value, name, axis):
    me = lax.axis_index(name)
    got = lax.ppermute(value, name, [(0, 1), (1, 0)])
    return jnp.stack([jnp.where(me == 0, value, got), jnp.where(me == 0, got, value)], axis=axis)


class Doubling:
    def __init__(self, left, right):
        self.cut, self.rows = left.shape[0], left.shape[1]
        self.flat = left.shape[1:] != right.shape[1:]
        if self.flat:
            left, right = (a.reshape(1, -1, a.shape[2]) for a in (left, right))
            self.out = [jnp.concatenate([left, right], axis=1)]
            self.split = left.shape[1]
        else:
            self.out = [jnp.concatenate([left, right])]

    def line(self):
        both = take_turns(self.out[0])
        if self.flat:
            d = both.shape[3]
            left = both[0, :, : self.split].reshape(4, self.cut, self.rows, d).swapaxes(0, 1)
            self.out = [left, both[:, :, self.split :]]
        else:
            self.out = [both[: self.cut], both[self.cut :]]

    def first(self):
        self.out = [take_pair(self.out[0], "y", 2), take_pair(self.out[1], "x", 1)]

    def second(self):
        self.out = [take_pair(self.out[0], "x", 1), take_pair(self.out[1], "y", 3)]

    def core(self):
        self.out = [take_pair(self.out[0], "c", 2), take_pair(self.out[1], "c", 2)]
        return self.out


def local_small(bias, gain, shift, bin_, bout):
    return jnp.concatenate([a.reshape(-1) for a in (bias, gain, shift, bout, bin_)])


def spread_small(parts, own):
    parts = parts.astype(F32)
    devices = parts.shape[0]
    rows = parts[:, : 13 * own].reshape(devices, 13, own).swapaxes(0, 1).reshape(13, -1)
    bin_ = parts[:, 13 * own :].reshape(1, -1)
    return {"bias": rows[0:6], "gain": rows[6:9], "shift": rows[9:12], "bout": rows[12:13], "bin": bin_}


class Stages:
    out_at = 8

    def __init__(self, proj, out, small, win, wout):
        _, own, d = proj.shape
        panels = win.reshape(own, -1, d).swapaxes(0, 1)
        rest = jnp.concatenate([proj[3:6], panels[:1], wout.reshape(-1, own, d), out, panels[1:]])
        self.rest = lax.all_gather(rest, ("x", "c", "z", "y"), axis=1)
        extra = jnp.pad(small[None, None], ((0, 0), (0, 7), (0, d - small.shape[0])))
        self.one = Doubling(proj[:2], jnp.concatenate([proj[2:3], extra], axis=1))
        self.own, self.cut, self.d = own, small.shape[0], d

    def begin(self):
        one, own, d = self.one, self.own, self.d
        one.line()
        one.first()
        one.second()
        left, right = one.core()
        full = {"qk": left.reshape(2, -1, d), "v": right[..., :own, :].reshape(1, -1, d)}
        full.update(spread_small(right[..., own, : self.cut].reshape(-1, self.cut), own))
        return full

    def finish(self):
        planes = self.rest.reshape(self.rest.shape[0], -1, self.d)
        return {"cross_proj": planes, "out": planes, "win": planes, "wout": self.rest}


class Plain:
    out_at = 0

    def __init__(self, proj, out, small, win, wout):
        take = functools.partial(lax.all_gather, axis_name=("dp", "fsdp"), tiled=True)
        _, own, d = proj.shape
        proj = take(proj, axis=1)
        self.full = {"qk": proj[:2], "v": proj[2:3]}
        self.full.update(spread_small(take(small[None], axis=0), own))
        win = take(win, axis=0).reshape(d, -1, d).swapaxes(0, 1)
        self.rest = {"cross_proj": proj[3:], "out": take(out, axis=1), "win": win, "wout": take(wout, axis=0)}

    def begin(self):
        return self.full

    def finish(self):
        return self.rest


def body(
    gather, scatter, devices, query, memory, query_seg, memory_seg, attn_proj, attn_out, attn_bias, norm_gain, norm_bias,
    ffn_in, ffn_in_bias, ffn_out, ffn_out_bias, cotangent,
):
    blocks = range(query.shape[0] // SEQ_MAX)
    own = attn_proj.shape[1]
    d = query.shape[1]
    staged = scatter is Halving
    me, pair = jnp.zeros((3,), jnp.int32), jnp.zeros((1,), jnp.int32)
    if staged:
        me = jnp.stack([lax.axis_index(name) for name in ("x", "y", "z")])
        pair = lax.axis_index("c").reshape(1)
    small = local_small(attn_bias, norm_gain, norm_bias, ffn_in_bias, ffn_out_bias)
    weights = gather(attn_proj, attn_out, small, ffn_in, ffn_out)
    full = weights.begin()
    bias, gain, shift = full["bias"], full["gain"], full["shift"]
    qmark = query_marks(query_seg)
    smark, cmark = key_marks(query_seg), key_marks(memory_seg)
    sq, sk, sv, sot, slse = self_forward(query, full["qk"], full["v"], bias, smark, qmark)
    rest, out_at = weights.finish(), weights.out_at
    out, cross_proj = rest["out"], rest["cross_proj"]
    first_sum, low, cq, ck, cv, cot_, clse, second_sum = cross_forward(
        query, memory, sot, out, out_at, cross_proj, bias, gain, shift, cmark, qmark
    )
    mixed, ssg, fdw, dbin, small3 = feed(
        second_sum, cotangent, rest["win"], full["bin"], rest["wout"], full["bout"], gain, shift
    )
    dwin, dwout = scatter.feed(fdw, own)
    grads, small2 = [], 0
    for block in blocks:
        *grads, part = cross_back(
            block, grads, out_at, ssg, first_sum, cq, ck, cv, cot_, clse, out, cross_proj, gain, cmark, qmark
        )
        small2 = small2 + part
    fsg, dq, dk, dv = grads
    keep, send = cross_weight(staged, pair, devices, dq, dk, dv, low, memory, cot_, ssg, sot, fsg)
    cross_sum = scatter(me, keep, send)
    dk = after(dk, cross_sum)
    memory_grad = memory_input(dk, dv, cross_proj)
    cross_sum.core()
    upstream, memory_grad = after((fsg, memory_grad), cross_sum)
    grads = []
    small1 = jnp.zeros((8, d), F32)
    for block in blocks[:-1]:
        *grads, part = self_back(block, grads, out_at, upstream, sq, sk, sv, sot, slse, out, smark, qmark)
        small1 = small1 + part
    cross_sum.first()
    upstream = after(upstream, cross_sum)
    sums = jnp.concatenate([small1[:3], small2[:5], small3[:5], jnp.zeros((3, d), F32)])
    keep, send, dq, dk, dv = self_last(
        staged, pair, devices, blocks[-1], grads, out_at, upstream, sq, sk, sv, sot, slse, out, smark, qmark, sums, dbin,
        query,
    )
    self_sum = scatter(me, keep, send)
    cross_sum.second()
    self_sum.out = after(self_sum.out, cross_sum)
    self_sum.core()
    upstream = after(fsg, self_sum, cross_sum)
    query_grad = self_input(upstream, dq, dk, dv, full["qk"], full["v"])
    cross = cross_sum.last()
    hold(self_sum, (query_grad, cross))
    self_sum.first()
    self_sum.second()
    proj_g, out_g, bias_g, gain_g, shift_g, dbin_g, dbout_g = scatter.finish(cross, self_sum.last(), send, dbin, own, devices)
    return (
        mixed, query_grad, memory_grad, proj_g, out_g, bias_g, gain_g, shift_g, dwin, dbin_g, dwout, dbout_g,
    )


def solution(mesh):
    devices = mesh.size
    if dict(mesh.shape) == {"dp": 4, "fsdp": 8}:
        axes = ("x", "c", "z", "y")
        mesh = Mesh(mesh.devices.reshape(2, 2, 4, 2), axes)
        gather, scatter = Stages, Halving
    else:
        axes = ("dp", "fsdp")
        gather, scatter = Plain, Whole
    rows, mid, flat, row1 = P(axes, None), P(None, axes, None), P(None, axes), P(axes)
    return jax.shard_map(
        functools.partial(body, gather, scatter, devices),
        mesh=mesh,
        in_specs=(rows, rows, row1, row1, mid, mid, flat, flat, flat, rows, row1, rows, row1, rows),
        out_specs=(rows, rows, rows, mid, mid, flat, flat, flat, rows, row1, rows, row1),
        check_vma=False,
    )
```

```python
import functools

import jax
import jax.numpy as jnp
from jax import lax
from jax.experimental import pallas as pl
from jax.experimental.pallas import tpu as pltpu
from jax.sharding import Mesh
from jax.sharding import PartitionSpec as P

HEADS = 12
HEAD_DIM = 64
SEQ_MAX = 512
PAIRS = HEADS // 2
FINE = 256
EPSILON = 1e-05
MASKED = 1e30
SCALE = HEAD_DIM ** (-0.5)
BF = jnp.bfloat16
F32 = jnp.float32
VMEM_LIMIT = 60 * 1024 * 1024


def dot(left, right):
    return jnp.dot(left, right, preferred_element_type=F32)


def dot_nt(left, right):
    return lax.dot_general(left, right, (((1,), (1,)), ((), ())), preferred_element_type=F32)


def norm_parts(resid):
    center = resid - jnp.mean(resid, axis=-1, keepdims=True)
    rstd = lax.rsqrt(jnp.mean(center * center, axis=-1, keepdims=True) + EPSILON)
    return center * rstd, rstd


def norm_back(unit, rstd, gain, upstream):
    scaled = upstream * gain
    mean_s = jnp.mean(scaled, axis=-1, keepdims=True)
    mean_su = jnp.mean(scaled * unit, axis=-1, keepdims=True)
    grad = rstd * (scaled - mean_s - unit * mean_su)
    return grad, col_sum(upstream * unit), col_sum(upstream)


def col_sum(rows):
    return jnp.sum(rows, axis=0, keepdims=True)


def place_rows(rows, count):
    parts = list(rows)
    parts.append(jnp.zeros((count - len(parts), parts[0].shape[1]), F32))
    return jnp.concatenate(parts, axis=0)


def gelu_parts(value):
    size = jnp.abs(value) * (0.5**0.5)
    bell = jnp.exp(-0.5 * value * value)
    t = 1.0 / (1.0 + 0.3275911 * size)
    poly = t * (0.254829592 + t * (-0.284496736 + t * (1.421413741 + t * (-1.453152027 + t * 1.061405429))))
    tail = 0.5 * poly * bell
    phi = jnp.where(value >= 0, 1.0 - tail, tail)
    return value * phi, phi + value * (bell * (1.0 / (2.0 * 3.141592653589793) ** 0.5))


def left_half(shape):
    return lax.broadcasted_iota(jnp.int32, shape, 1) < HEAD_DIM


def head_pair(side, pair):
    return pl.ds(pl.multiple_of(pair * 128 + side * HEAD_DIM, HEAD_DIM), HEAD_DIM)


def key_tile(tile, marks, side):
    left = left_half(tile.shape)
    return jnp.where(left, tile, marks) if side == 0 else jnp.where(left, marks, tile)


def query_tile(rows, marks, side):
    return jnp.concatenate([rows, marks] if side == 0 else [marks, rows], axis=0)


def attend_block(k_ref, qt_ref, vt_ref, kmark_ref, qmark_ref, ot_ref, lse_ref):
    kmark = kmark_ref[...]
    qmark = qmark_ref[0]
    ones = jnp.ones((16, SEQ_MAX), BF)

    def score(head):
        pair, side = head // 2, head % 2
        rows = slice(head * HEAD_DIM, (head + 1) * HEAD_DIM)
        tile = k_ref[:, pair * 128 : (pair + 1) * 128]
        return dot(key_tile(tile, kmark, side), query_tile(qt_ref[rows, :], qmark, side))

    def finish(head, peak, weights):
        rows = slice(head * HEAD_DIM, (head + 1) * HEAD_DIM)
        result = dot(jnp.concatenate([vt_ref[rows, :], ones], axis=0), weights)
        total = result[HEAD_DIM : HEAD_DIM + 1]
        ot_ref[rows, :] = (result[:HEAD_DIM] * (1.0 / total)).astype(BF)
        lse_ref[0, head : head + 1, :] = peak + jnp.log(total)

    for start in range(0, HEADS, 6):
        heads = range(start, start + 6)
        scores = [score(head) for head in heads]
        peaks = [jnp.max(s, axis=0, keepdims=True) for s in scores]
        weights = [jnp.exp(s - peak).astype(BF) for s, peak in zip(scores, peaks)]
        for head, peak, weight in zip(heads, peaks, weights):
            finish(head, peak, weight)


def attend_back_block(
    q_ref, k_ref, v_ref, qt_ref, kt_ref, ot_ref, do_ref, dot_ref, kmark_ref, qmark_ref, lse_ref, dqt_ref, dk_ref, dv_ref
):
    kmark = kmark_ref[...]
    qmark = qmark_ref[0]
    left = left_half((SEQ_MAX, 128))
    blank = jnp.zeros((HEAD_DIM, SEQ_MAX), BF)

    def begin(head):
        pair, side = head // 2, head % 2
        rows = slice(head * HEAD_DIM, (head + 1) * HEAD_DIM)
        cols = slice(pair * 128, (pair + 1) * 128)
        scores = dot(key_tile(k_ref[:, cols], kmark, side), query_tile(qt_ref[rows, :], qmark, side))
        up = dot_ref[rows, :]
        probs_grad = dot(v_ref[:, cols], query_tile(up, blank, side))
        return scores, probs_grad, col_sum(up.astype(F32) * ot_ref[rows, :].astype(F32))

    def middle(head, scores, probs_grad, center):
        probs = jnp.exp(scores - lse_ref[0, head : head + 1, :])
        return probs.astype(BF), (probs * (probs_grad - center)).astype(BF)

    def finish(head, probs, score_grad):
        rows = slice(head * HEAD_DIM, (head + 1) * HEAD_DIM)
        cols = slice(head // 2 * 128, (head // 2 + 1) * 128)
        dqt_ref[rows, :] = (dot(kt_ref[rows, :], score_grad) * SCALE).astype(BF)
        return dot(probs, do_ref[:, cols]), dot(score_grad, q_ref[:, cols])

    for start in range(0, HEADS, 4):
        heads = range(start, start + 4)
        begun = [begin(head) for head in heads]
        mid = [middle(head, *b) for head, b in zip(heads, begun)]
        done = [finish(head, *m) for head, m in zip(heads, mid)]
        for i in range(0, 4, 2):
            cols = slice((start + i) // 2 * 128, ((start + i) // 2 + 1) * 128)
            dv_ref[:, cols] = jnp.where(left, done[i][0], done[i + 1][0]).astype(BF)
            dk_ref[:, cols] = jnp.where(left, done[i][1], done[i + 1][1]).astype(BF)


def self_forward_kernel(
    x_ref, wqk_ref, wv_ref, bias_ref, kmark_ref, qmark_ref, q_ref, k_ref, v_ref, ot_ref, lse_ref, qt_s, vt_s
):
    x = x_ref[...]
    queries = ((dot(x, wqk_ref[0]) + bias_ref[0:1]).astype(BF)) * SCALE
    q_ref[...] = queries
    qt_s[...] = queries.T
    k_ref[...] = dot(x, wqk_ref[1]).astype(BF)
    values = (dot(x, wv_ref[0]) + bias_ref[1:2]).astype(BF)
    v_ref[...] = values
    vt_s[...] = values.T
    attend_block(k_ref, qt_s, vt_s, kmark_ref, qmark_ref, ot_ref, lse_ref)


def cross_forward_kernel(
    x_ref, mem_ref, sot_ref, wo_ref, w_ref, bias_ref, gain_ref, shift_ref, kmark_ref, qmark_ref,
    first_sum_ref, low_ref, q_ref, k_ref, v_ref, ot_ref, lse_ref, second_sum_ref, qt_s, vt_s,
):
    mem = mem_ref[...]
    k_ref[...] = dot(mem, w_ref[1]).astype(BF)
    values = (dot(mem, w_ref[2]) + bias_ref[4:5]).astype(BF)
    v_ref[...] = values
    vt_s[...] = values.T
    first_sum = x_ref[...].astype(F32) + (dot(sot_ref[...].T, wo_ref[0]) + bias_ref[2:3])
    first_sum_ref[...] = first_sum
    unit, _ = norm_parts(first_sum)
    first = unit * gain_ref[0:1] + shift_ref[0:1]
    low = first.astype(BF)
    low_ref[...] = low
    queries = ((dot(low, w_ref[0]) + bias_ref[3:4]).astype(BF)) * SCALE
    q_ref[...] = queries
    qt_s[...] = queries.T
    attend_block(k_ref, qt_s, vt_s, kmark_ref, qmark_ref, ot_ref, lse_ref)
    second_sum_ref[...] = first + (dot(ot_ref[...].T, wo_ref[1]) + bias_ref[5:6])


def feed_kernel(
    own, ss_ref, cot_ref, win_ref, bin_ref, wout_ref, bout_ref, gain_ref, shift_ref,
    mixed_ref, ssg_ref, dw_ref, dbin_ref, small_ref,
    low_s, lowt_s, hid_s, slope_s, acc_s, z_s, din_s, dout_s, sems,
):
    phase, chunk = pl.program_id(0), pl.program_id(1)
    chunks = pl.num_programs(1)
    last = chunks - 1
    slot = chunk % 2
    width, d = dout_s.shape[1] * dout_s.shape[2], dout_s.shape[3]
    parts = dout_s.shape[1]

    def wout():
        if not own:
            return wout_ref[...]
        groups = wout_ref[...].astype(F32)
        return jnp.concatenate([groups[:, i] for i in range(groups.shape[1])], axis=0).reshape(width, d).astype(BF)

    def sends(slot, chunk):
        if own:
            group = width // parts
            rows = pl.ds(pl.multiple_of(chunk * group, group), group)
            outs = [
                pltpu.make_async_copy(
                    dout_s.at[slot, part], dw_ref.at[rows, pl.ds((chunks + part) * width, width)], sems.at[1 + part, slot]
                )
                for part in range(parts)
            ]
        else:
            cols = pl.ds(pl.multiple_of((chunks + chunk) * width, width), width)
            outs = [pltpu.make_async_copy(dout_s.at[slot, 0], dw_ref.at[:, cols], sems.at[1, slot])]
        cols = pl.ds(pl.multiple_of(chunk * width, width), width)
        return [pltpu.make_async_copy(din_s.at[slot], dw_ref.at[:, cols], sems.at[0, slot])] + outs

    @pl.when((phase == 0) & (chunk == 0))
    def _():
        unit, _ = norm_parts(ss_ref[...])
        second = unit * gain_ref[1:2] + shift_ref[1:2]
        low = second.astype(BF)
        low_s[...] = low
        lowt_s[...] = low.T
        acc_s[...] = second + bout_ref[...]

    @pl.when(phase == 0)
    def _():
        weights_in, weights_out, count = win_ref[0], wout(), low_s.shape[0] // 4
        blocks = [slice(i * count, (i + 1) * count) for i in range(4)]
        pres = [dot(low_s[block, :], weights_in) + bin_ref[...] for block in blocks]
        both = [gelu_parts(pre) for pre in pres]
        for block, (hidden, slope) in zip(blocks, both):
            hidden = hidden.astype(BF)
            hid_s[chunk, block] = hidden
            slope_s[chunk, block] = slope
            acc_s[block, :] += dot(hidden, weights_out)

    @pl.when((phase == 1) & (chunk == 0))
    def _():
        unit, rstd = norm_parts(acc_s[...])
        mixed_ref[...] = (unit * gain_ref[2:3] + shift_ref[2:3]).astype(BF)
        third, dgain, dshift = norm_back(unit, rstd, gain_ref[2:3], cot_ref[...].astype(F32))
        z = third.astype(BF)
        z_s[...] = z
        acc_s[...] = third
        small_ref[...] = place_rows([dgain, dshift, col_sum(z.astype(F32))], 8)

    @pl.when((phase == 1) & (chunk >= 2))
    def _():
        for copy in sends(slot, chunk - 2):
            copy.wait()

    @pl.when(phase == 1)
    def _():
        z = z_s[...]
        pre_grad = (dot_nt(z, wout()) * slope_s[chunk]).astype(BF)
        dbin_ref[...] = col_sum(pre_grad.astype(F32))
        dout = dot(hid_s[chunk].T, z)
        if own:
            groups = dout.reshape(width // (parts * own), parts, own, d)
            for part in range(parts):
                dout_s[slot, part] = groups[:, part].reshape(width // parts, d).astype(BF)
        else:
            dout_s[slot] = dout.reshape(dout_s.shape[1:]).astype(BF)
        din_s[slot] = dot(lowt_s[...], pre_grad).astype(BF)
        for copy in sends(slot, chunk):
            copy.start()
        acc_s[...] += dot_nt(pre_grad, win_ref[0])

    @pl.when((phase == 1) & (chunk == last))
    def _():
        unit, rstd = norm_parts(ss_ref[...])
        grad, dgain, dshift = norm_back(unit, rstd, gain_ref[1:2], acc_s[...])
        ssg_ref[...] = grad
        small_ref[3:5] = jnp.concatenate([dgain, dshift], axis=0)
        for copy in sends(1 - slot, chunk - 1) + sends(slot, chunk):
            copy.wait()


def cross_back_kernel(
    ssg_ref, fs_ref, q_ref, k_ref, v_ref, ot_ref, lse_ref, wo_ref, w_ref, gain_ref, kmark_ref, qmark_ref, *refs
):
    fsg_ref, dq_ref, dk_ref, dv_ref, small_ref, qt_s, kt_s, do_s, dot_s, dqt_s = refs[-10:]
    upstream = ssg_ref[...]
    branch = upstream.astype(BF)
    mixed_grad = dot_nt(branch, wo_ref[0]).astype(BF)
    do_s[...] = mixed_grad
    dot_s[...] = mixed_grad.T
    qt_s[...] = q_ref[...].T
    kt_s[...] = k_ref[...].T
    attend_back_block(
        q_ref, k_ref, v_ref, qt_s, kt_s, ot_ref, do_s, dot_s, kmark_ref, qmark_ref, lse_ref, dqt_s, dk_ref, dv_ref
    )
    dq = dqt_s[...].T
    dq_ref[...] = dq
    first_grad = upstream + dot_nt(dq, w_ref[0])
    unit, rstd = norm_parts(fs_ref[...])
    grad, dgain, dshift = norm_back(unit, rstd, gain_ref[0:1], first_grad)
    fsg_ref[...] = grad
    sums = [col_sum(dq.astype(F32)), col_sum(dv_ref[...].astype(F32)), col_sum(branch.astype(F32)), dgain, dshift]
    small_ref[...] = place_rows(sums, 8)


def self_back_kernel(fsg_ref, q_ref, k_ref, v_ref, ot_ref, lse_ref, wo_ref, kmark_ref, qmark_ref, *refs):
    dq_ref, dk_ref, dv_ref, small_ref, qt_s, kt_s, do_s, dot_s, dqt_s = refs[-9:]
    branch = fsg_ref[...].astype(BF)
    mixed_grad = dot_nt(branch, wo_ref[0]).astype(BF)
    do_s[...] = mixed_grad
    dot_s[...] = mixed_grad.T
    qt_s[...] = q_ref[...].T
    kt_s[...] = k_ref[...].T
    attend_back_block(
        q_ref, k_ref, v_ref, qt_s, kt_s, ot_ref, do_s, dot_s, kmark_ref, qmark_ref, lse_ref, dqt_s, dk_ref, dv_ref
    )
    dq = dqt_s[...].T
    dq_ref[...] = dq
    sums = [col_sum(dq.astype(F32)), col_sum(dv_ref[...].astype(F32)), col_sum(branch.astype(F32))]
    small_ref[...] = place_rows(sums, 8)


def bring(sources, slots, sems):
    copies = [pltpu.make_async_copy(s, v, sems.at[i]) for i, (s, v) in enumerate(zip(sources, slots))]
    for copy in copies:
        copy.start()

    def get(i):
        copies[i].wait()
        return slots[i][...]

    return get


def lay_out(out_s, at, grads, more=None):
    places = out_s.shape[2] * out_s.shape[3]
    d = out_s.shape[5]
    own = d // (4 * places)
    for quarter in range(4):
        first = quarter * places
        parts = [g[first * own : (first + places) * own].reshape(places, own, d) for g in grads]
        if more is not None:
            parts.append(jnp.stack([more(first + i) for i in range(places)]))
        rows = jnp.concatenate(parts, axis=1).astype(BF)
        count = rows.shape[1]
        out_s[quarter // 2, quarter % 2, :, :, at : at + count] = rows.reshape(*out_s.shape[2:4], count, d)


def hand_out(out_s, me, keep_ref, send_ref, sems):
    moves = []
    for x in range(2):
        moves.append(pltpu.make_async_copy(out_s.at[x, me], keep_ref.at[x], sems.at[2 * x]))
        moves.append(pltpu.make_async_copy(out_s.at[x, 1 - me], send_ref.at[x], sems.at[2 * x + 1]))
    for move in moves:
        move.start()
    return moves


def cross_weight_kernel(staged, me_ref, *refs):
    sources, (keep_ref, send_ref), slots = refs[:9], refs[9:11], refs[11:20]
    out_s, sems, out_sems = refs[20:]
    get = bring(sources, slots, sems)
    memt = get(0).T
    dk = get(1)
    keys = dot(memt, dk)
    dv = get(2)
    values = dot(memt, dv)
    if staged:
        lay_out(out_s, 0, [keys, values])
    else:
        out_s[0], out_s[1] = keys.astype(BF), values.astype(BF)
    outs = [dot(get(3), get(4).astype(BF)), dot(get(5), get(6).astype(BF))]
    if staged:
        lay_out(out_s, 2 * outs[0].shape[0] // 32, outs)
    else:
        out_s[2], out_s[3] = outs[0].astype(BF), outs[1].astype(BF)
    queries = dot(get(7).T, get(8))
    if staged:
        lay_out(out_s, 4 * outs[0].shape[0] // 32, [queries])
        moves = hand_out(out_s, me_ref[0], keep_ref, send_ref, out_sems)
    else:
        out_s[4] = queries.astype(BF)
        send_ref[0] = 0
        moves = [pltpu.make_async_copy(out_s, keep_ref, out_sems.at[0])]
        moves[0].start()
    for move in moves:
        move.wait()


def self_last_kernel(
    staged, me_ref, fsg_ref, q_ref, k_ref, v_ref, ot_ref, lse_ref, wo_ref, kmark_ref, qmark_ref, sums_ref, dbin_ref, x_ref,
    *refs,
):
    (keep_ref, send_ref), outs = refs[3:5], refs[5:8]
    qt_s, kt_s, do_s, dot_s, dqt_s, dq_s, dk_s, dv_s, x_s, out_s, sems, out_sems = refs[8:]
    grads = (dq_s, dk_s, dv_s)
    before = x_s.shape[0] - SEQ_MAX
    mine = pl.ds(before, SEQ_MAX)
    loads = [pltpu.make_async_copy(x_ref, x_s, sems.at[0])]
    if before:
        early = pl.ds(0, before)
        loads += [
            pltpu.make_async_copy(o.at[early], g.at[early], sems.at[1 + i]) for i, (o, g) in enumerate(zip(outs, grads))
        ]
    for load in loads:
        load.start()
    branch = fsg_ref[...].astype(BF)
    mixed_grad = dot_nt(branch, wo_ref[0]).astype(BF)
    do_s[...] = mixed_grad
    dot_s[...] = mixed_grad.T
    qt_s[...] = q_ref[...].T
    kt_s[...] = k_ref[...].T
    attend_back_block(
        q_ref, k_ref, v_ref, qt_s, kt_s, ot_ref, do_s, dot_s, kmark_ref, qmark_ref, lse_ref, dqt_s,
        dk_s.at[mine], dv_s.at[mine],
    )
    dq_s[mine] = dqt_s[...].T
    moves = [
        pltpu.make_async_copy(g.at[mine], o.at[mine], sems.at[4 + i]) for i, (g, o) in enumerate(zip(grads, outs))
    ]
    for load in loads:
        load.wait()
    for move in moves:
        move.start()
    last = [col_sum(dq_s[mine].astype(F32)), col_sum(dv_s[mine].astype(F32)), col_sum(branch.astype(F32))]
    sums = sums_ref[...] + place_rows(last, 16)
    xt = x_s[...].T
    if not staged:
        for i in range(3):
            out_s[i] = dot(xt, grads[i][...]).astype(BF)
        send_ref[...] = sums
        moves.append(pltpu.make_async_copy(out_s, keep_ref, out_sems.at[0]))
        moves[-1].start()
    else:
        d, wide = sums_ref.shape[1], dbin_ref.shape[1]
        lines = jnp.broadcast_to(dbin_ref[...], (8, wide))
        last_row = lax.broadcasted_iota(jnp.int32, (16, d), 0) == 15

        def small(device):
            rows, line = sums, lines
            if device:
                rows = pltpu.roll(rows, d - d // 32 * device, 1)
                line = pltpu.roll(lines, wide - wide // 32 * device, 1)
            line = line[:, :d]
            return jnp.where(last_row, jnp.concatenate([line, line], axis=0), rows)

        lay_out(out_s, 0, [dot(xt, dq_s[...]), dot(xt, dk_s[...])])
        lay_out(out_s, 2 * d // 32, [dot(xt, dv_s[...])], small)
        moves += hand_out(out_s, me_ref[0], keep_ref, send_ref, out_sems)
    for move in moves:
        move.wait()


def memory_input_kernel(dk_ref, dv_ref, wk_ref, wv_ref, mg_ref):
    mg_ref[...] = dot_nt(dk_ref[...], wk_ref[0]) + dot_nt(dv_ref[...], wv_ref[0])


def self_input_kernel(fsg_ref, dq_ref, dk_ref, dv_ref, wqk_ref, wv_ref, qg_ref):
    qg_ref[...] = (
        fsg_ref[...]
        + dot_nt(dq_ref[...], wqk_ref[0]) + dot_nt(dk_ref[...], wqk_ref[1]) + dot_nt(dv_ref[...], wv_ref[0])
    )


def pick(first, second, other):
    return jnp.where(other == 0, first, second)


def first_stage_kernel(me_ref, keep_ref, got_ref, sl_ref, kl_ref, sr_ref, kr_ref):
    total = keep_ref[...].astype(F32) + got_ref[...].astype(F32)
    half = total.shape[4] // 2
    left, right = total[..., :half], total[..., half:]
    sl_ref[...] = pick(left[1], left[0], me_ref[0]).astype(BF)
    kl_ref[...] = pick(left[0], left[1], me_ref[0]).astype(BF)
    sr_ref[...] = pick(right[:, :, 1], right[:, :, 0], me_ref[1]).astype(BF)
    kr_ref[...] = pick(right[:, :, 0], right[:, :, 1], me_ref[1]).astype(BF)


def second_stage_kernel(me_ref, kl_ref, gl_ref, kr_ref, gr_ref, sl_ref, ml_ref, sr_ref, mr_ref):
    left = kl_ref[...].astype(F32) + gl_ref[...].astype(F32)
    right = kr_ref[...].astype(F32) + gr_ref[...].astype(F32)
    sl_ref[...] = pick(left[:, 1], left[:, 0], me_ref[1]).astype(BF)
    ml_ref[...] = pick(left[:, 0], left[:, 1], me_ref[1]).astype(BF)
    sr_ref[...] = pick(right[1], right[0], me_ref[0]).astype(BF)
    mr_ref[...] = pick(right[0], right[1], me_ref[0]).astype(BF)


def third_stage_kernel(me_ref, kl_ref, gl_ref, kr_ref, gr_ref, own_ref, *outs):
    total = jnp.concatenate(
        [kl_ref[...].astype(F32) + gl_ref[...].astype(F32), kr_ref[...].astype(F32) + gr_ref[...].astype(F32)], axis=2
    )
    me = me_ref[2]
    for step, ref in enumerate((own_ref, *outs)):
        index = (me + step) % 4
        value = jnp.where(
            index < 2, jnp.where(index == 0, total[0], total[1]), jnp.where(index == 2, total[2], total[3])
        )
        ref[...] = value.astype(ref.dtype)


def final_stage_kernel(own, *refs):
    cross_refs, self_refs, outs = refs[:4], refs[4:8], refs[8:]
    proj_ref, out_ref, bias_ref, gain_ref, shift_ref, hidden_ref, last_ref = outs
    cross = functools.reduce(jnp.add, [r[...].astype(F32) for r in cross_refs])
    selfs = functools.reduce(jnp.add, [r[...].astype(F32) for r in self_refs])
    for i in range(3):
        proj_ref[i] = selfs[i * own : (i + 1) * own]
    for ref, index, at in ((proj_ref, 4, 0), (proj_ref, 5, 1), (out_ref, 1, 2), (out_ref, 0, 3), (proj_ref, 3, 4)):
        ref[index] = cross[at * own : (at + 1) * own]
    sums = selfs[3 * own : 3 * own + 16, :128]
    bias_ref[...] = sums[0:6, :own]
    for ref, lines in ((gain_ref, (6, 11, 8)), (shift_ref, (7, 12, 9))):
        for i, line in enumerate(lines):
            ref[i : i + 1] = sums[line : line + 1, :own]
    hidden_ref[...] = sums[15:16, : hidden_ref.shape[1]]
    last_ref[...] = sums[10:11, :own]


def stage_call(kernel, me, args, outs, name):
    data = sum(a.size * a.dtype.itemsize for a in args)
    return pl.pallas_call(
        kernel,
        in_specs=[pl.BlockSpec(memory_space=pltpu.SMEM)] + [pl.BlockSpec(memory_space=pltpu.VMEM)] * len(args),
        out_specs=[pl.BlockSpec(memory_space=pltpu.VMEM)] * len(outs),
        out_shape=outs,
        compiler_params=pltpu.CompilerParams(vmem_limit_bytes=VMEM_LIMIT),
        cost_estimate=cost(data, 2 * data),
        name=name,
    )(me, *args)


def first_stage(me, keep, got):
    x, z, y, rows, d = keep.shape
    line = lambda *lead: pl.BlockSpec((*lead, rows, d // 2), lambda i: (i, 0, 0, 0))
    both = pl.BlockSpec((x, 1, y, rows, d), lambda i: (0, i, 0, 0, 0))
    side = pl.BlockSpec((x, 1, rows, d // 2), lambda i: (0, i, 0, 0))
    left, right = shape((z, y, rows, d // 2), BF), shape((x, z, rows, d // 2), BF)
    return pl.pallas_call(
        first_stage_kernel,
        grid=(z,),
        in_specs=[pl.BlockSpec(memory_space=pltpu.SMEM), both, both],
        out_specs=[line(1, y), line(1, y), side, side],
        out_shape=[left, left, right, right],
        compiler_params=params(("arbitrary",)),
        cost_estimate=cost(keep.size, 6 * keep.size),
        name="first_stage",
    )(me, keep, got)


def row_block(width):
    return pl.BlockSpec((SEQ_MAX, width), lambda b: (b, 0))


def fine_block(width):
    return pl.BlockSpec((FINE, width), lambda b: (b, 0))


def col_block(height):
    return pl.BlockSpec((height, SEQ_MAX), lambda b: (0, b))


def lead_block(rows):
    return pl.BlockSpec((1, rows, SEQ_MAX), lambda b: (b, 0, 0))


def whole(array, **kw):
    zeros = (0,) * array.ndim
    return pl.BlockSpec(array.shape, lambda *_: zeros, pipeline_mode=pl.Buffered(1))


def planes(array, start, count):
    return pl.BlockSpec(
        (count, *array.shape[1:]), lambda *_: (start // count, 0, 0), pipeline_mode=pl.Buffered(1)
    )


def params(semantics):
    return pltpu.CompilerParams(vmem_limit_bytes=VMEM_LIMIT, dimension_semantics=semantics)


def cost(flops, data, exps=0):
    return pl.CostEstimate(flops=int(flops), bytes_accessed=int(data), transcendentals=int(exps))


def shape(dims, kind):
    return jax.ShapeDtypeStruct(dims, kind)


def self_forward(x, wqk, wv, bias, kmark, qmark):
    rows, d = x.shape
    blocks = rows // SEQ_MAX
    act = shape((rows, d), BF)
    return pl.pallas_call(
        self_forward_kernel,
        grid=(blocks,),
        in_specs=[row_block(d), whole(wqk), whole(wv), whole(bias), row_block(128), lead_block(HEAD_DIM)],
        out_specs=[row_block(d), row_block(d), row_block(d), col_block(d), lead_block(16)],
        out_shape=[act, act, act, shape((d, rows), BF), shape((blocks, 16, SEQ_MAX), F32)],
        scratch_shapes=[pltpu.VMEM((d, SEQ_MAX), BF)] * 2,
        compiler_params=params(("arbitrary",)),
        cost_estimate=cost(20e9, 12e6),
        name="self_forward",
    )(x, wqk, wv, bias, kmark, qmark)


def cross_forward(x, mem, sot, wo, wo_at, w, bias, gain, shift, kmark, qmark):
    rows, d = x.shape
    blocks = rows // SEQ_MAX
    act, wide = shape((rows, d), BF), shape((rows, d), F32)
    return pl.pallas_call(
        cross_forward_kernel,
        grid=(blocks,),
        in_specs=[
            row_block(d), row_block(d), col_block(d), planes(wo, wo_at, 2), planes(w, 0, 3), whole(bias), whole(gain),
            whole(shift),
            row_block(128), lead_block(HEAD_DIM),
        ],
        out_specs=[row_block(d)] * 5 + [col_block(d), lead_block(16), row_block(d)],
        out_shape=[wide, act, act, act, act, shape((d, rows), BF), shape((blocks, 16, SEQ_MAX), F32), wide],
        scratch_shapes=[pltpu.VMEM((d, SEQ_MAX), BF)] * 2,
        compiler_params=params(("arbitrary",)),
        cost_estimate=cost(24e9, 20e6),
        name="cross_forward",
    )(x, mem, sot, wo, w, bias, gain, shift, kmark, qmark)


def feed(second_sum, cot, win, bin_, wout, bout, gain, shift):
    rows, d = second_sum.shape
    width = win.shape[2]
    ff = bin_.shape[1]
    chunks = ff // width
    own = wout.shape[2] if wout.ndim == 4 else 0
    fixed = lambda p, j: (0, 0)
    parts = chunks if own else 1
    if own:
        wout_spec = pl.BlockSpec((parts, width // (parts * own), own, d), lambda p, j: (1, j, 0, 0))
    else:
        wout_spec = pl.BlockSpec((width, d), lambda p, j: (j, 0))
    return pl.pallas_call(
        functools.partial(feed_kernel, own),
        grid=(2, chunks),
        in_specs=[
            whole(second_sum), whole(cot),
            pl.BlockSpec((1, d, width), lambda p, j: (jnp.where(j == 0, 3, 7 + j) if own else j, 0, 0)),
            pl.BlockSpec((1, width), lambda p, j: (0, j)),
            wout_spec, whole(bout), whole(gain), whole(shift),
        ],
        out_specs=[
            pl.BlockSpec((rows, d), fixed),
            pl.BlockSpec((rows, d), fixed),
            pl.BlockSpec(memory_space=pl.ANY),
            pl.BlockSpec((1, width), lambda p, j: (0, j * p)),
            pl.BlockSpec((8, d), fixed),
        ],
        out_shape=[
            shape((rows, d), BF), shape((rows, d), F32), shape((d, 2 * ff), BF),
            shape((1, ff), F32), shape((8, d), F32),
        ],
        scratch_shapes=[
            pltpu.VMEM((rows, d), BF), pltpu.VMEM((d, rows), BF),
            pltpu.VMEM((chunks, rows, width), BF), pltpu.VMEM((chunks, rows, width), F32),
            pltpu.VMEM((rows, d), F32), pltpu.VMEM((rows, d), BF),
            pltpu.VMEM((2, d, width), BF), pltpu.VMEM((2, parts, width // parts, d), BF),
            pltpu.SemaphoreType.DMA((1 + parts, 2)),
        ],
        compiler_params=params(("arbitrary", "arbitrary")),
        cost_estimate=cost(40e9, 40e6),
        name="feed",
    )(second_sum, cot, win, bin_, wout, bout, gain, shift)


def back_scratch(d):
    return (
        [pltpu.VMEM((d, SEQ_MAX), BF)] * 2 + [pltpu.VMEM((SEQ_MAX, d), BF)] + [pltpu.VMEM((d, SEQ_MAX), BF)] * 2
    )


def at_row(block, width):
    return pl.BlockSpec((SEQ_MAX, width), lambda b: (block, 0))


def at_col(block, height):
    return pl.BlockSpec((height, SEQ_MAX), lambda b: (0, block))


def at_lead(block, rows):
    return pl.BlockSpec((1, rows, SEQ_MAX), lambda b: (block, 0, 0))


def one_back(kernel, block, before, args, specs, outs, name):
    d = outs[0].shape[1]
    kept = [pl.BlockSpec(memory_space=pl.ANY)] * len(before)
    return pl.pallas_call(
        kernel,
        grid=(1,),
        in_specs=specs + kept,
        out_specs=[at_row(block, d)] * len(outs) + [pl.BlockSpec((8, d), lambda b: (0, 0))],
        out_shape=outs + [shape((8, d), F32)],
        scratch_shapes=back_scratch(d),
        input_output_aliases={len(args) + i: i for i in range(len(before))},
        compiler_params=params(("arbitrary",)),
        cost_estimate=cost(25e9, 15e6),
        name=name,
    )(*args, *before)


def cross_back(block, before, wo_at, ssg, first_sum, q, k, v, ot, lse, wo, w, gain, kmark, qmark):
    rows, d = first_sum.shape
    act = shape((rows, d), BF)
    specs = [at_row(block, d)] * 5 + [
        at_col(block, d), at_lead(block, 16), planes(wo, wo_at + 1, 1), planes(w, 0, 1), whole(gain), at_row(block, 128), at_lead(block, HEAD_DIM),
    ]
    args = (ssg, first_sum, q, k, v, ot, lse, wo, w, gain, kmark, qmark)
    return one_back(
        cross_back_kernel, block, before, args, specs, [shape((rows, d), F32), act, act, act], f"cross_back_{block}"
    )


def self_back(block, before, wo_at, fsg, q, k, v, ot, lse, wo, kmark, qmark):
    rows, d = fsg.shape
    act = shape((rows, d), BF)
    specs = [at_row(block, d)] * 4 + [
        at_col(block, d), at_lead(block, 16), planes(wo, wo_at, 1), at_row(block, 128), at_lead(block, HEAD_DIM),
    ]
    args = (fsg, q, k, v, ot, lse, wo, kmark, qmark)
    return one_back(self_back_kernel, block, before, args, specs, [act, act, act], f"self_back_{block}")


def weight_outs(staged, count, extra, devices, d):
    if not staged:
        return [shape((count, d, d), BF), shape((1,), jnp.int32)], pltpu.VMEM((count, d, d), BF)
    rows = count * d // devices + extra
    half = shape((2, 4, 2, rows, d), BF)
    return [half, half], pltpu.VMEM((2, 2, 4, 2, rows, d), BF)


def cross_weight(staged, me, devices, dq, dk, dv, low, mem, ot, ssg, sot, fsg):
    rows, d = dq.shape
    args = (mem, dk, dv, ot, ssg, sot, fsg, low, dq)
    anywhere = pl.BlockSpec(memory_space=pl.ANY)
    outs, scratch = weight_outs(staged, 5, 0, devices, d)
    last = anywhere if staged else pl.BlockSpec(memory_space=pltpu.SMEM)
    return pl.pallas_call(
        functools.partial(cross_weight_kernel, staged),
        in_specs=[pl.BlockSpec(memory_space=pltpu.SMEM)] + [anywhere] * 9,
        out_specs=[anywhere, last],
        out_shape=outs,
        scratch_shapes=[pltpu.VMEM(a.shape, a.dtype) for a in args] + [
            scratch, pltpu.SemaphoreType.DMA((9,)), pltpu.SemaphoreType.DMA((4,)),
        ],
        compiler_params=pltpu.CompilerParams(vmem_limit_bytes=VMEM_LIMIT),
        cost_estimate=cost(9e9, 20e6),
        name="cross_weight",
    )(me, *args)


def self_last(staged, me, devices, block, before, wo_at, fsg, q, k, v, ot, lse, wo, kmark, qmark, sums, dbin, x):
    rows, d = x.shape
    anywhere, here = pl.BlockSpec(memory_space=pl.ANY), pl.BlockSpec(memory_space=pltpu.VMEM)
    outs, scratch = weight_outs(staged, 3, 16, devices, d)
    act = shape((rows, d), BF)
    args = (me, fsg, q, k, v, ot, lse, wo, kmark, qmark, sums, dbin, x)
    if not before:
        before = [jnp.zeros((rows, d), BF)] * 3
    fixed = lambda array: pl.BlockSpec(array.shape, lambda b: (0,) * array.ndim)
    if not staged:
        outs[1] = shape((16, d), F32)
    return pl.pallas_call(
        functools.partial(self_last_kernel, staged),
        grid=(1,),
        in_specs=[pl.BlockSpec(memory_space=pltpu.SMEM)] + [at_row(block, d)] * 4 + [
            at_col(block, d), at_lead(block, 16), planes(wo, wo_at, 1), at_row(block, 128), at_lead(block, HEAD_DIM),
            fixed(sums), fixed(dbin), anywhere,
        ] + [anywhere] * 3,
        out_specs=[anywhere, anywhere if staged else fixed(outs[1])] + [anywhere] * 3,
        out_shape=outs + [act] * 3,
        scratch_shapes=back_scratch(d) + [pltpu.VMEM((rows, d), BF)] * 4 + [
            scratch, pltpu.SemaphoreType.DMA((7,)), pltpu.SemaphoreType.DMA((4,)),
        ],
        input_output_aliases={len(args) + i: 2 + i for i in range(3)},
        compiler_params=params(("arbitrary",)),
        cost_estimate=cost(25e9, 20e6),
        name="self_last",
    )(*args, *before)


def memory_input(dk, dv, w):
    rows, d = dk.shape
    return pl.pallas_call(
        memory_input_kernel,
        grid=(rows // FINE,),
        in_specs=[fine_block(d)] * 2 + [planes(w, 1, 1), planes(w, 2, 1)],
        out_specs=fine_block(d),
        out_shape=shape((rows, d), F32),
        compiler_params=params(("arbitrary",)),
        cost_estimate=cost(3e9, 9e6),
        name="memory_input",
    )(dk, dv, w, w)


def self_input(fsg, dq, dk, dv, wqk, wv):
    rows, d = fsg.shape
    return pl.pallas_call(
        self_input_kernel,
        grid=(rows // FINE,),
        in_specs=[fine_block(d)] * 4 + [whole(wqk), whole(wv)],
        out_specs=fine_block(d),
        out_shape=shape((rows, d), F32),
        compiler_params=params(("arbitrary",)),
        cost_estimate=cost(4e9, 14e6),
        name="self_input",
    )(fsg, dq, dk, dv, wqk, wv)


def key_marks(seg):
    odd = (seg & 1)[:, None]
    lane = lax.broadcasted_iota(jnp.int32, (seg.shape[0], 128), 1) % HEAD_DIM
    return jnp.where(lane == 0, 1 - odd, jnp.where(lane == 1, odd, 0)).astype(BF)


def query_marks(seg):
    odd = (seg & 1).reshape(-1, 1, SEQ_MAX)
    row = lax.broadcasted_iota(jnp.int32, (odd.shape[0], HEAD_DIM, SEQ_MAX), 1)
    return jnp.where(row == 0, odd, jnp.where(row == 1, 1 - odd, 0)).astype(BF) * (-MASKED)


def swap(value, name):
    return lax.ppermute(value, name, [(0, 1), (1, 0)])


class Halving:
    def __init__(self, me, keep, send):
        self.me, self.keep, self.out = me, [keep], [send]

    def core(self):
        got = swap(self.out[0], "c")
        sl, kl, sr, kr = first_stage(self.me, self.keep[0], got)
        self.keep, self.out = [kl, kr], [sl, sr]

    def first(self):
        (kl, kr), (sl, sr) = self.keep, self.out
        gl, gr = swap(sl, "x"), swap(sr, "y")
        z, _, rows, half = kl.shape
        piece = shape((z, rows, half), BF)
        sl, ml, sr, mr = stage_call(second_stage_kernel, self.me, (kl, gl, kr, gr), [piece] * 4, "second_stage")
        self.keep, self.out = [ml, mr], [sl, sr]

    def second(self):
        (kl, kr), (sl, sr) = self.keep, self.out
        gl, gr = swap(sl, "y"), swap(sr, "x")
        _, rows, half = kl.shape
        piece = (rows, 2 * half)
        outs = [shape(piece, F32)] + [shape(piece, BF)] * 3
        own, *self.out = stage_call(third_stage_kernel, self.me, (kl, gl, kr, gr), outs, "third_stage")
        self.keep = [own]

    def last(self):
        steps = zip(range(1, 4), self.out)
        return self.keep + [lax.ppermute(out, "z", [(i, (i + step) % 4) for i in range(4)]) for step, out in steps]

    @staticmethod
    def finish(cross, selfs, small, dbin, own, devices):
        d = cross[0].shape[1]
        wide = dbin.shape[1] // devices
        outs = [
            shape(dims, F32)
            for dims in ((6, own, d), (2, own, d), (6, own), (3, own), (3, own), (1, wide), (1, own))
        ]
        args = cross + selfs
        proj, out, bias, gain, shift, hidden, last = pl.pallas_call(
            functools.partial(final_stage_kernel, own),
            in_specs=[pl.BlockSpec(memory_space=pltpu.VMEM)] * 8,
            out_specs=[pl.BlockSpec(memory_space=pltpu.VMEM)] * 7,
            out_shape=outs,
            compiler_params=pltpu.CompilerParams(vmem_limit_bytes=VMEM_LIMIT),
            cost_estimate=cost(2e6, 3e6),
            name="final_stage",
        )(*args)
        return proj, out, bias, gain, shift, hidden.reshape(-1), last.reshape(-1)

    @staticmethod
    def feed(grads, own):
        sums = lax.psum_scatter(grads, ("x", "c", "z", "y"), scatter_dimension=0, tiled=True).astype(F32)
        half = sums.shape[1] // 2
        d = grads.shape[0]
        return sums[:, :half], sums[:, half:].reshape(own, -1, d).swapaxes(0, 1).reshape(-1, d)


class Whole:
    def __init__(self, me, grads, _):
        self.grads, self.out, self.keep = grads, (), ()

    def core(self):
        pass

    first = second = core

    def last(self):
        sums = lax.psum_scatter(self.grads, ("dp", "fsdp"), scatter_dimension=1, tiled=True).astype(F32)
        return sums.reshape(-1, sums.shape[2])

    @staticmethod
    def finish(cross, selfs, small, dbin, own, devices):
        sum_up = functools.partial(lax.psum_scatter, axis_name=("dp", "fsdp"), scatter_dimension=1, tiled=True)
        small, dbin = sum_up(small), sum_up(dbin)[0]
        cross, selfs = cross.reshape(5, own, -1), selfs.reshape(3, own, -1)
        proj = jnp.concatenate([selfs, cross[4:], cross[:2]])
        gain, shift = jnp.stack([small[6], small[11], small[8]]), jnp.stack([small[7], small[12], small[9]])
        return proj, cross[3:1:-1], small[0:6], gain, shift, dbin, small[10]

    @staticmethod
    def feed(grads, own):
        sum_up = functools.partial(lax.psum_scatter, axis_name=("dp", "fsdp"), scatter_dimension=0, tiled=True)
        half, d = grads.shape[1] // 2, grads.shape[0]
        dwin = sum_up(grads[:, :half]).astype(F32)
        return dwin, sum_up(grads[:, half:].reshape(d, -1, d).swapaxes(0, 1).reshape(-1, d)).astype(F32)


def after(value, *sums):
    value, outs = lax.optimization_barrier((value, [s.out for s in sums]))
    for s, s.out in zip(sums, outs):
        pass
    return value


def hold(sums, value):
    sums.keep = lax.optimization_barrier((sums.keep, value))[0]


def take_turns(value):
    me = lax.axis_index("z")
    parts = [value]
    for step in range(3, 0, -1):
        parts.append(lax.ppermute(value, "z", [(i, (i + step) % 4) for i in range(4)]))
    return jnp.stack([lax.select_n((j - me) % 4, *parts) for j in range(4)], axis=1)


def take_pair(value, name, axis):
    me = lax.axis_index(name)
    got = lax.ppermute(value, name, [(0, 1), (1, 0)])
    return jnp.stack([jnp.where(me == 0, value, got), jnp.where(me == 0, got, value)], axis=axis)


class Doubling:
    def __init__(self, left, right):
        self.cut, self.rows = left.shape[0], left.shape[1]
        self.flat = left.shape[1:] != right.shape[1:]
        if self.flat:
            left, right = (a.reshape(1, -1, a.shape[2]) for a in (left, right))
            self.out = [jnp.concatenate([left, right], axis=1)]
            self.split = left.shape[1]
        else:
            self.out = [jnp.concatenate([left, right])]

    def line(self):
        both = take_turns(self.out[0])
        if self.flat:
            d = both.shape[3]
            left = both[0, :, : self.split].reshape(4, self.cut, self.rows, d).swapaxes(0, 1)
            self.out = [left, both[:, :, self.split :]]
        else:
            self.out = [both[: self.cut], both[self.cut :]]

    def first(self):
        self.out = [take_pair(self.out[0], "y", 2), take_pair(self.out[1], "x", 1)]

    def second(self):
        self.out = [take_pair(self.out[0], "x", 1), take_pair(self.out[1], "y", 3)]

    def core(self):
        self.out = [take_pair(self.out[0], "c", 2), take_pair(self.out[1], "c", 2)]
        return self.out


def local_small(bias, gain, shift, bin_, bout):
    return jnp.concatenate([a.reshape(-1) for a in (bias, gain, shift, bout, bin_)])


def spread_small(parts, own):
    parts = parts.astype(F32)
    devices = parts.shape[0]
    rows = parts[:, : 13 * own].reshape(devices, 13, own).swapaxes(0, 1).reshape(13, -1)
    bin_ = parts[:, 13 * own :].reshape(1, -1)
    return {"bias": rows[0:6], "gain": rows[6:9], "shift": rows[9:12], "bout": rows[12:13], "bin": bin_}


class Stages:
    out_at = 0

    def __init__(self, proj, out, small, win, wout):
        _, own, d = proj.shape
        panels = win.reshape(own, -1, d).swapaxes(0, 1)
        rest = jnp.concatenate([proj[3:6], panels[:1], wout.reshape(-1, own, d), panels[1:]])
        self.rest = lax.all_gather(rest, ("x", "c", "z", "y"), axis=1)
        extra = jnp.pad(small[None, None], ((0, 0), (0, 7), (0, d - small.shape[0])))
        self.one = Doubling(proj[:2], jnp.concatenate([proj[2:3], extra], axis=1))
        self.two = Doubling(out[:1], out[1:])
        self.own, self.cut, self.d = own, small.shape[0], d

    def begin(self):
        one, own, d = self.one, self.own, self.d
        one.line()
        one.first()
        one.second()
        self.two.out = after(self.two.out, one)
        left, right = one.core()
        full = {"qk": left.reshape(2, -1, d), "v": right[..., :own, :].reshape(1, -1, d)}
        full.update(spread_small(right[..., own, : self.cut].reshape(-1, self.cut), own))
        return full

    def finish(self, value):
        planes = self.rest.reshape(self.rest.shape[0], -1, self.d)
        two = self.two
        two.line()
        two.out, value = lax.optimization_barrier((two.out, value))
        two.first()
        two.second()
        out = jnp.concatenate(two.core()).reshape(2, -1, self.d)
        return {"cross_proj": planes, "out": out, "win": planes, "wout": self.rest}, value


class Plain:
    out_at = 0

    def __init__(self, proj, out, small, win, wout):
        take = functools.partial(lax.all_gather, axis_name=("dp", "fsdp"), tiled=True)
        _, own, d = proj.shape
        proj = take(proj, axis=1)
        self.full = {"qk": proj[:2], "v": proj[2:3]}
        self.full.update(spread_small(take(small[None], axis=0), own))
        win = take(win, axis=0).reshape(d, -1, d).swapaxes(0, 1)
        self.rest = {"cross_proj": proj[3:], "out": take(out, axis=1), "win": win, "wout": take(wout, axis=0)}

    def begin(self):
        return self.full

    def finish(self, value):
        return self.rest, value


def body(
    gather, scatter, devices, query, memory, query_seg, memory_seg, attn_proj, attn_out, attn_bias, norm_gain, norm_bias,
    ffn_in, ffn_in_bias, ffn_out, ffn_out_bias, cotangent,
):
    blocks = range(query.shape[0] // SEQ_MAX)
    own = attn_proj.shape[1]
    d = query.shape[1]
    staged = scatter is Halving
    me, pair = jnp.zeros((3,), jnp.int32), jnp.zeros((1,), jnp.int32)
    if staged:
        me = jnp.stack([lax.axis_index(name) for name in ("x", "y", "z")])
        pair = lax.axis_index("c").reshape(1)
    small = local_small(attn_bias, norm_gain, norm_bias, ffn_in_bias, ffn_out_bias)
    weights = gather(attn_proj, attn_out, small, ffn_in, ffn_out)
    full = weights.begin()
    bias, gain, shift = full["bias"], full["gain"], full["shift"]
    qmark = query_marks(query_seg)
    smark, cmark = key_marks(query_seg), key_marks(memory_seg)
    sq, sk, sv, sot, slse = self_forward(query, full["qk"], full["v"], bias, smark, qmark)
    (rest, sot), out_at = weights.finish(sot), weights.out_at
    out, cross_proj = rest["out"], rest["cross_proj"]
    first_sum, low, cq, ck, cv, cot_, clse, second_sum = cross_forward(
        query, memory, sot, out, out_at, cross_proj, bias, gain, shift, cmark, qmark
    )
    mixed, ssg, fdw, dbin, small3 = feed(
        second_sum, cotangent, rest["win"], full["bin"], rest["wout"], full["bout"], gain, shift
    )
    dwin, dwout = scatter.feed(fdw, own)
    grads, small2 = [], 0
    for block in blocks:
        *grads, part = cross_back(
            block, grads, out_at, ssg, first_sum, cq, ck, cv, cot_, clse, out, cross_proj, gain, cmark, qmark
        )
        small2 = small2 + part
    fsg, dq, dk, dv = grads
    keep, send = cross_weight(staged, pair, devices, dq, dk, dv, low, memory, cot_, ssg, sot, fsg)
    cross_sum = scatter(me, keep, send)
    dk = after(dk, cross_sum)
    memory_grad = memory_input(dk, dv, cross_proj)
    cross_sum.core()
    upstream, memory_grad = after((fsg, memory_grad), cross_sum)
    grads = []
    small1 = jnp.zeros((8, d), F32)
    for block in blocks[:-1]:
        *grads, part = self_back(block, grads, out_at, upstream, sq, sk, sv, sot, slse, out, smark, qmark)
        small1 = small1 + part
    cross_sum.first()
    upstream = after(upstream, cross_sum)
    sums = jnp.concatenate([small1[:3], small2[:5], small3[:5], jnp.zeros((3, d), F32)])
    keep, send, dq, dk, dv = self_last(
        staged, pair, devices, blocks[-1], grads, out_at, upstream, sq, sk, sv, sot, slse, out, smark, qmark, sums, dbin,
        query,
    )
    self_sum = scatter(me, keep, send)
    cross_sum.second()
    self_sum.out = after(self_sum.out, cross_sum)
    self_sum.core()
    upstream = after(fsg, self_sum, cross_sum)
    query_grad = self_input(upstream, dq, dk, dv, full["qk"], full["v"])
    cross = cross_sum.last()
    hold(self_sum, (query_grad, cross))
    self_sum.first()
    self_sum.second()
    proj_g, out_g, bias_g, gain_g, shift_g, dbin_g, dbout_g = scatter.finish(cross, self_sum.last(), send, dbin, own, devices)
    return (
        mixed, query_grad, memory_grad, proj_g, out_g, bias_g, gain_g, shift_g, dwin, dbin_g, dwout, dbout_g,
    )


def solution(mesh):
    devices = mesh.size
    if dict(mesh.shape) == {"dp": 4, "fsdp": 8}:
        axes = ("x", "c", "z", "y")
        mesh = Mesh(mesh.devices.reshape(2, 2, 4, 2), axes)
        gather, scatter = Stages, Halving
    else:
        axes = ("dp", "fsdp")
        gather, scatter = Plain, Whole
    rows, mid, flat, row1 = P(axes, None), P(None, axes, None), P(None, axes), P(axes)
    return jax.shard_map(
        functools.partial(body, gather, scatter, devices),
        mesh=mesh,
        in_specs=(rows, rows, row1, row1, mid, mid, flat, flat, flat, rows, row1, rows, row1, rows),
        out_specs=(rows, rows, rows, mid, mid, flat, flat, flat, rows, row1, rows, row1),
        check_vma=False,
    )
```

```python
import functools

import jax
import jax.numpy as jnp
from jax import lax
from jax.experimental import pallas as pl
from jax.experimental.pallas import tpu as pltpu
from jax.sharding import Mesh
from jax.sharding import PartitionSpec as P

HEADS = 12
HEAD_DIM = 64
SEQ_MAX = 512
PAIRS = HEADS // 2
FINE = 512
EPSILON = 1e-05
MASKED = 1e30
SCALE = HEAD_DIM ** (-0.5)
BF = jnp.bfloat16
F32 = jnp.float32
VMEM_LIMIT = 60 * 1024 * 1024


def dot(left, right):
    return jnp.dot(left, right, preferred_element_type=F32)


def dot_nt(left, right):
    return lax.dot_general(left, right, (((1,), (1,)), ((), ())), preferred_element_type=F32)


def norm_parts(resid):
    center = resid - jnp.mean(resid, axis=-1, keepdims=True)
    rstd = lax.rsqrt(jnp.mean(center * center, axis=-1, keepdims=True) + EPSILON)
    return center * rstd, rstd


def norm_back(unit, rstd, gain, upstream):
    scaled = upstream * gain
    mean_s = jnp.mean(scaled, axis=-1, keepdims=True)
    mean_su = jnp.mean(scaled * unit, axis=-1, keepdims=True)
    grad = rstd * (scaled - mean_s - unit * mean_su)
    return grad, col_sum(upstream * unit), col_sum(upstream)


def col_sum(rows):
    return jnp.sum(rows, axis=0, keepdims=True)


def place_rows(rows, count):
    parts = list(rows)
    parts.append(jnp.zeros((count - len(parts), parts[0].shape[1]), F32))
    return jnp.concatenate(parts, axis=0)


def gelu_parts(value):
    size = jnp.abs(value) * (0.5**0.5)
    bell = jnp.exp(-0.5 * value * value)
    t = 1.0 / (1.0 + 0.3275911 * size)
    poly = t * (0.254829592 + t * (-0.284496736 + t * (1.421413741 + t * (-1.453152027 + t * 1.061405429))))
    tail = 0.5 * poly * bell
    phi = jnp.where(value >= 0, 1.0 - tail, tail)
    return value * phi, phi + value * (bell * (1.0 / (2.0 * 3.141592653589793) ** 0.5))


def left_half(shape):
    return lax.broadcasted_iota(jnp.int32, shape, 1) < HEAD_DIM


def head_pair(side, pair):
    return pl.ds(pl.multiple_of(pair * 128 + side * HEAD_DIM, HEAD_DIM), HEAD_DIM)


def key_tile(tile, marks, side):
    left = left_half(tile.shape)
    return jnp.where(left, tile, marks) if side == 0 else jnp.where(left, marks, tile)


def query_tile(rows, marks, side):
    return jnp.concatenate([rows, marks] if side == 0 else [marks, rows], axis=0)


def attend_block(k_ref, qt_ref, vt_ref, kmark_ref, qmark_ref, ot_ref, lse_ref):
    kmark = kmark_ref[...]
    qmark = qmark_ref[0]
    ones = jnp.ones((16, SEQ_MAX), BF)

    def score(head):
        pair, side = head // 2, head % 2
        rows = slice(head * HEAD_DIM, (head + 1) * HEAD_DIM)
        tile = k_ref[:, pair * 128 : (pair + 1) * 128]
        return dot(key_tile(tile, kmark, side), query_tile(qt_ref[rows, :], qmark, side))

    def finish(head, peak, weights):
        rows = slice(head * HEAD_DIM, (head + 1) * HEAD_DIM)
        result = dot(jnp.concatenate([vt_ref[rows, :], ones], axis=0), weights)
        total = result[HEAD_DIM : HEAD_DIM + 1]
        ot_ref[rows, :] = (result[:HEAD_DIM] * (1.0 / total)).astype(BF)
        lse_ref[0, head : head + 1, :] = peak + jnp.log(total)

    for start in range(0, HEADS, 6):
        heads = range(start, start + 6)
        scores = [score(head) for head in heads]
        peaks = [jnp.max(s, axis=0, keepdims=True) for s in scores]
        weights = [jnp.exp(s - peak).astype(BF) for s, peak in zip(scores, peaks)]
        for head, peak, weight in zip(heads, peaks, weights):
            finish(head, peak, weight)


def attend_back_block(
    q_ref, k_ref, v_ref, qt_ref, kt_ref, ot_ref, do_ref, dot_ref, kmark_ref, qmark_ref, lse_ref, dqt_ref, dk_ref, dv_ref
):
    kmark = kmark_ref[...]
    qmark = qmark_ref[0]
    left = left_half((SEQ_MAX, 128))
    blank = jnp.zeros((HEAD_DIM, SEQ_MAX), BF)

    def begin(head):
        pair, side = head // 2, head % 2
        rows = slice(head * HEAD_DIM, (head + 1) * HEAD_DIM)
        cols = slice(pair * 128, (pair + 1) * 128)
        scores = dot(key_tile(k_ref[:, cols], kmark, side), query_tile(qt_ref[rows, :], qmark, side))
        up = dot_ref[rows, :]
        probs_grad = dot(v_ref[:, cols], query_tile(up, blank, side))
        return scores, probs_grad, col_sum(up.astype(F32) * ot_ref[rows, :].astype(F32))

    def middle(head, scores, probs_grad, center):
        probs = jnp.exp(scores - lse_ref[0, head : head + 1, :])
        return probs.astype(BF), (probs * (probs_grad - center)).astype(BF)

    def finish(head, probs, score_grad):
        rows = slice(head * HEAD_DIM, (head + 1) * HEAD_DIM)
        cols = slice(head // 2 * 128, (head // 2 + 1) * 128)
        dqt_ref[rows, :] = (dot(kt_ref[rows, :], score_grad) * SCALE).astype(BF)
        return dot(probs, do_ref[:, cols]), dot(score_grad, q_ref[:, cols])

    for start in range(0, HEADS, 4):
        heads = range(start, start + 4)
        begun = [begin(head) for head in heads]
        mid = [middle(head, *b) for head, b in zip(heads, begun)]
        done = [finish(head, *m) for head, m in zip(heads, mid)]
        for i in range(0, 4, 2):
            cols = slice((start + i) // 2 * 128, ((start + i) // 2 + 1) * 128)
            dv_ref[:, cols] = jnp.where(left, done[i][0], done[i + 1][0]).astype(BF)
            dk_ref[:, cols] = jnp.where(left, done[i][1], done[i + 1][1]).astype(BF)


def self_forward_kernel(
    x_ref, wqk_ref, wv_ref, bias_ref, kmark_ref, qmark_ref, q_ref, k_ref, v_ref, ot_ref, lse_ref, qt_s, vt_s
):
    x = x_ref[...]
    queries = ((dot(x, wqk_ref[0]) + bias_ref[0:1]).astype(BF)) * SCALE
    q_ref[...] = queries
    qt_s[...] = queries.T
    k_ref[...] = dot(x, wqk_ref[1]).astype(BF)
    values = (dot(x, wv_ref[0]) + bias_ref[1:2]).astype(BF)
    v_ref[...] = values
    vt_s[...] = values.T
    attend_block(k_ref, qt_s, vt_s, kmark_ref, qmark_ref, ot_ref, lse_ref)


def cross_forward_kernel(
    x_ref, mem_ref, sot_ref, wo_ref, w_ref, bias_ref, gain_ref, shift_ref, kmark_ref, qmark_ref,
    first_sum_ref, low_ref, q_ref, k_ref, v_ref, ot_ref, lse_ref, second_sum_ref, qt_s, vt_s,
):
    mem = mem_ref[...]
    k_ref[...] = dot(mem, w_ref[1]).astype(BF)
    values = (dot(mem, w_ref[2]) + bias_ref[4:5]).astype(BF)
    v_ref[...] = values
    vt_s[...] = values.T
    first_sum = x_ref[...].astype(F32) + (dot(sot_ref[...].T, wo_ref[0]) + bias_ref[2:3])
    first_sum_ref[...] = first_sum
    unit, _ = norm_parts(first_sum)
    first = unit * gain_ref[0:1] + shift_ref[0:1]
    low = first.astype(BF)
    low_ref[...] = low
    queries = ((dot(low, w_ref[0]) + bias_ref[3:4]).astype(BF)) * SCALE
    q_ref[...] = queries
    qt_s[...] = queries.T
    attend_block(k_ref, qt_s, vt_s, kmark_ref, qmark_ref, ot_ref, lse_ref)
    second_sum_ref[...] = first + (dot(ot_ref[...].T, wo_ref[1]) + bias_ref[5:6])


def feed_kernel(
    own, ss_ref, cot_ref, win_ref, bin_ref, wout_ref, bout_ref, gain_ref, shift_ref,
    mixed_ref, ssg_ref, dw_ref, dbin_ref, small_ref,
    low_s, lowt_s, hid_s, slope_s, acc_s, z_s, din_s, dout_s, sems,
):
    phase, chunk = pl.program_id(0), pl.program_id(1)
    chunks = pl.num_programs(1)
    last = chunks - 1
    slot = chunk % 2
    width, d = dout_s.shape[1] * dout_s.shape[2], dout_s.shape[3]
    parts = dout_s.shape[1]

    def wout():
        if not own:
            return wout_ref[...]
        groups = wout_ref[...].astype(F32)
        return jnp.concatenate([groups[:, i] for i in range(groups.shape[1])], axis=0).reshape(width, d).astype(BF)

    def sends(slot, chunk):
        if own:
            group = width // parts
            rows = pl.ds(pl.multiple_of(chunk * group, group), group)
            outs = [
                pltpu.make_async_copy(
                    dout_s.at[slot, part], dw_ref.at[rows, pl.ds((chunks + part) * width, width)], sems.at[1 + part, slot]
                )
                for part in range(parts)
            ]
        else:
            cols = pl.ds(pl.multiple_of((chunks + chunk) * width, width), width)
            outs = [pltpu.make_async_copy(dout_s.at[slot, 0], dw_ref.at[:, cols], sems.at[1, slot])]
        cols = pl.ds(pl.multiple_of(chunk * width, width), width)
        return [pltpu.make_async_copy(din_s.at[slot], dw_ref.at[:, cols], sems.at[0, slot])] + outs

    @pl.when((phase == 0) & (chunk == 0))
    def _():
        unit, _ = norm_parts(ss_ref[...])
        second = unit * gain_ref[1:2] + shift_ref[1:2]
        low = second.astype(BF)
        low_s[...] = low
        lowt_s[...] = low.T
        acc_s[...] = second + bout_ref[...]

    @pl.when(phase == 0)
    def _():
        weights_in, weights_out, count = win_ref[0], wout(), low_s.shape[0] // 4
        blocks = [slice(i * count, (i + 1) * count) for i in range(4)]
        pres = [dot(low_s[block, :], weights_in) + bin_ref[...] for block in blocks]
        both = [gelu_parts(pre) for pre in pres]
        for block, (hidden, slope) in zip(blocks, both):
            hidden = hidden.astype(BF)
            hid_s[chunk, block] = hidden
            slope_s[chunk, block] = slope
            acc_s[block, :] += dot(hidden, weights_out)

    @pl.when((phase == 1) & (chunk == 0))
    def _():
        unit, rstd = norm_parts(acc_s[...])
        mixed_ref[...] = (unit * gain_ref[2:3] + shift_ref[2:3]).astype(BF)
        third, dgain, dshift = norm_back(unit, rstd, gain_ref[2:3], cot_ref[...].astype(F32))
        z = third.astype(BF)
        z_s[...] = z
        acc_s[...] = third
        small_ref[...] = place_rows([dgain, dshift, col_sum(z.astype(F32))], 8)

    @pl.when((phase == 1) & (chunk >= 2))
    def _():
        for copy in sends(slot, chunk - 2):
            copy.wait()

    @pl.when(phase == 1)
    def _():
        z = z_s[...]
        pre_grad = (dot_nt(z, wout()) * slope_s[chunk]).astype(BF)
        dbin_ref[...] = col_sum(pre_grad.astype(F32))
        dout = dot(hid_s[chunk].T, z)
        if own:
            groups = dout.reshape(width // (parts * own), parts, own, d)
            for part in range(parts):
                dout_s[slot, part] = groups[:, part].reshape(width // parts, d).astype(BF)
        else:
            dout_s[slot] = dout.reshape(dout_s.shape[1:]).astype(BF)
        din_s[slot] = dot(lowt_s[...], pre_grad).astype(BF)
        for copy in sends(slot, chunk):
            copy.start()
        acc_s[...] += dot_nt(pre_grad, win_ref[0])

    @pl.when((phase == 1) & (chunk == last))
    def _():
        unit, rstd = norm_parts(ss_ref[...])
        grad, dgain, dshift = norm_back(unit, rstd, gain_ref[1:2], acc_s[...])
        ssg_ref[...] = grad
        small_ref[3:5] = jnp.concatenate([dgain, dshift], axis=0)
        for copy in sends(1 - slot, chunk - 1) + sends(slot, chunk):
            copy.wait()


def cross_back_kernel(
    ssg_ref, fs_ref, q_ref, k_ref, v_ref, ot_ref, lse_ref, wo_ref, w_ref, gain_ref, kmark_ref, qmark_ref, *refs
):
    fsg_ref, dq_ref, dk_ref, dv_ref, small_ref, qt_s, kt_s, do_s, dot_s, dqt_s = refs[-10:]
    upstream = ssg_ref[...]
    branch = upstream.astype(BF)
    mixed_grad = dot_nt(branch, wo_ref[0]).astype(BF)
    do_s[...] = mixed_grad
    dot_s[...] = mixed_grad.T
    qt_s[...] = q_ref[...].T
    kt_s[...] = k_ref[...].T
    attend_back_block(
        q_ref, k_ref, v_ref, qt_s, kt_s, ot_ref, do_s, dot_s, kmark_ref, qmark_ref, lse_ref, dqt_s, dk_ref, dv_ref
    )
    dq = dqt_s[...].T
    dq_ref[...] = dq
    first_grad = upstream + dot_nt(dq, w_ref[0])
    unit, rstd = norm_parts(fs_ref[...])
    grad, dgain, dshift = norm_back(unit, rstd, gain_ref[0:1], first_grad)
    fsg_ref[...] = grad
    sums = [col_sum(dq.astype(F32)), col_sum(dv_ref[...].astype(F32)), col_sum(branch.astype(F32)), dgain, dshift]
    small_ref[...] = place_rows(sums, 8)


def self_back_kernel(fsg_ref, q_ref, k_ref, v_ref, ot_ref, lse_ref, wo_ref, kmark_ref, qmark_ref, *refs):
    dq_ref, dk_ref, dv_ref, small_ref, qt_s, kt_s, do_s, dot_s, dqt_s = refs[-9:]
    branch = fsg_ref[...].astype(BF)
    mixed_grad = dot_nt(branch, wo_ref[0]).astype(BF)
    do_s[...] = mixed_grad
    dot_s[...] = mixed_grad.T
    qt_s[...] = q_ref[...].T
    kt_s[...] = k_ref[...].T
    attend_back_block(
        q_ref, k_ref, v_ref, qt_s, kt_s, ot_ref, do_s, dot_s, kmark_ref, qmark_ref, lse_ref, dqt_s, dk_ref, dv_ref
    )
    dq = dqt_s[...].T
    dq_ref[...] = dq
    sums = [col_sum(dq.astype(F32)), col_sum(dv_ref[...].astype(F32)), col_sum(branch.astype(F32))]
    small_ref[...] = place_rows(sums, 8)


def bring(sources, slots, sems):
    copies = [pltpu.make_async_copy(s, v, sems.at[i]) for i, (s, v) in enumerate(zip(sources, slots))]
    for copy in copies:
        copy.start()

    def get(i):
        copies[i].wait()
        return slots[i][...]

    return get


def lay_out(out_s, at, grads, more=None):
    places = out_s.shape[2] * out_s.shape[3]
    d = out_s.shape[5]
    own = d // (4 * places)
    for quarter in range(4):
        first = quarter * places
        parts = [g[first * own : (first + places) * own].reshape(places, own, d) for g in grads]
        if more is not None:
            parts.append(jnp.stack([more(first + i) for i in range(places)]))
        rows = jnp.concatenate(parts, axis=1).astype(BF)
        count = rows.shape[1]
        out_s[quarter // 2, quarter % 2, :, :, at : at + count] = rows.reshape(*out_s.shape[2:4], count, d)


def hand_out(out_s, me, keep_ref, send_ref, sems):
    moves = []
    for x in range(2):
        moves.append(pltpu.make_async_copy(out_s.at[x, me], keep_ref.at[x], sems.at[2 * x]))
        moves.append(pltpu.make_async_copy(out_s.at[x, 1 - me], send_ref.at[x], sems.at[2 * x + 1]))
    for move in moves:
        move.start()
    return moves


def cross_weight_kernel(staged, me_ref, *refs):
    sources, (keep_ref, send_ref), slots = refs[:9], refs[9:11], refs[11:20]
    out_s, sems, out_sems = refs[20:]
    get = bring(sources, slots, sems)
    memt = get(0).T
    dk = get(1)
    keys = dot(memt, dk)
    dv = get(2)
    values = dot(memt, dv)
    if staged:
        lay_out(out_s, 0, [keys, values])
    else:
        out_s[0], out_s[1] = keys.astype(BF), values.astype(BF)
    outs = [dot(get(3), get(4).astype(BF)), dot(get(5), get(6).astype(BF))]
    if staged:
        lay_out(out_s, 2 * outs[0].shape[0] // 32, outs)
    else:
        out_s[2], out_s[3] = outs[0].astype(BF), outs[1].astype(BF)
    queries = dot(get(7).T, get(8))
    if staged:
        lay_out(out_s, 4 * outs[0].shape[0] // 32, [queries])
        moves = hand_out(out_s, me_ref[0], keep_ref, send_ref, out_sems)
    else:
        out_s[4] = queries.astype(BF)
        send_ref[0] = 0
        moves = [pltpu.make_async_copy(out_s, keep_ref, out_sems.at[0])]
        moves[0].start()
    for move in moves:
        move.wait()


def self_last_kernel(
    staged, me_ref, fsg_ref, q_ref, k_ref, v_ref, ot_ref, lse_ref, wo_ref, kmark_ref, qmark_ref, sums_ref, dbin_ref, x_ref,
    *refs,
):
    (keep_ref, send_ref), outs = refs[3:5], refs[5:8]
    qt_s, kt_s, do_s, dot_s, dqt_s, dq_s, dk_s, dv_s, x_s, out_s, sems, out_sems = refs[8:]
    grads = (dq_s, dk_s, dv_s)
    before = x_s.shape[0] - SEQ_MAX
    mine = pl.ds(before, SEQ_MAX)
    loads = [pltpu.make_async_copy(x_ref, x_s, sems.at[0])]
    if before:
        early = pl.ds(0, before)
        loads += [
            pltpu.make_async_copy(o.at[early], g.at[early], sems.at[1 + i]) for i, (o, g) in enumerate(zip(outs, grads))
        ]
    for load in loads:
        load.start()
    branch = fsg_ref[...].astype(BF)
    mixed_grad = dot_nt(branch, wo_ref[0]).astype(BF)
    do_s[...] = mixed_grad
    dot_s[...] = mixed_grad.T
    qt_s[...] = q_ref[...].T
    kt_s[...] = k_ref[...].T
    attend_back_block(
        q_ref, k_ref, v_ref, qt_s, kt_s, ot_ref, do_s, dot_s, kmark_ref, qmark_ref, lse_ref, dqt_s,
        dk_s.at[mine], dv_s.at[mine],
    )
    dq_s[mine] = dqt_s[...].T
    moves = [
        pltpu.make_async_copy(g.at[mine], o.at[mine], sems.at[4 + i]) for i, (g, o) in enumerate(zip(grads, outs))
    ]
    for load in loads:
        load.wait()
    for move in moves:
        move.start()
    last = [col_sum(dq_s[mine].astype(F32)), col_sum(dv_s[mine].astype(F32)), col_sum(branch.astype(F32))]
    sums = sums_ref[...] + place_rows(last, 16)
    xt = x_s[...].T
    if not staged:
        for i in range(3):
            out_s[i] = dot(xt, grads[i][...]).astype(BF)
        send_ref[...] = sums
        moves.append(pltpu.make_async_copy(out_s, keep_ref, out_sems.at[0]))
        moves[-1].start()
    else:
        d, wide = sums_ref.shape[1], dbin_ref.shape[1]
        lines = jnp.broadcast_to(dbin_ref[...], (8, wide))
        last_row = lax.broadcasted_iota(jnp.int32, (16, d), 0) == 15

        def small(device):
            rows, line = sums, lines
            if device:
                rows = pltpu.roll(rows, d - d // 32 * device, 1)
                line = pltpu.roll(lines, wide - wide // 32 * device, 1)
            line = line[:, :d]
            return jnp.where(last_row, jnp.concatenate([line, line], axis=0), rows)

        lay_out(out_s, 0, [dot(xt, dq_s[...]), dot(xt, dk_s[...])])
        lay_out(out_s, 2 * d // 32, [dot(xt, dv_s[...])], small)
        moves += hand_out(out_s, me_ref[0], keep_ref, send_ref, out_sems)
    for move in moves:
        move.wait()


def memory_input_kernel(dk_ref, dv_ref, wk_ref, wv_ref, mg_ref):
    mg_ref[...] = dot_nt(dk_ref[...], wk_ref[0]) + dot_nt(dv_ref[...], wv_ref[0])


def self_input_kernel(fsg_ref, dq_ref, dk_ref, dv_ref, wqk_ref, wv_ref, qg_ref):
    qg_ref[...] = (
        fsg_ref[...]
        + dot_nt(dq_ref[...], wqk_ref[0]) + dot_nt(dk_ref[...], wqk_ref[1]) + dot_nt(dv_ref[...], wv_ref[0])
    )


def pick(first, second, other):
    return jnp.where(other == 0, first, second)


def first_stage_kernel(me_ref, keep_ref, got_ref, sl_ref, kl_ref, sr_ref, kr_ref):
    total = keep_ref[...].astype(F32) + got_ref[...].astype(F32)
    half = total.shape[4] // 2
    left, right = total[..., :half], total[..., half:]
    sl_ref[...] = pick(left[1], left[0], me_ref[0]).astype(BF)
    kl_ref[...] = pick(left[0], left[1], me_ref[0]).astype(BF)
    sr_ref[...] = pick(right[:, :, 1], right[:, :, 0], me_ref[1]).astype(BF)
    kr_ref[...] = pick(right[:, :, 0], right[:, :, 1], me_ref[1]).astype(BF)


def second_stage_kernel(me_ref, kl_ref, gl_ref, kr_ref, gr_ref, sl_ref, ml_ref, sr_ref, mr_ref):
    left = kl_ref[...].astype(F32) + gl_ref[...].astype(F32)
    right = kr_ref[...].astype(F32) + gr_ref[...].astype(F32)
    sl_ref[...] = pick(left[:, 1], left[:, 0], me_ref[1]).astype(BF)
    ml_ref[...] = pick(left[:, 0], left[:, 1], me_ref[1]).astype(BF)
    sr_ref[...] = pick(right[1], right[0], me_ref[0]).astype(BF)
    mr_ref[...] = pick(right[0], right[1], me_ref[0]).astype(BF)


def third_stage_kernel(me_ref, kl_ref, gl_ref, kr_ref, gr_ref, own_ref, *outs):
    total = jnp.concatenate(
        [kl_ref[...].astype(F32) + gl_ref[...].astype(F32), kr_ref[...].astype(F32) + gr_ref[...].astype(F32)], axis=2
    )
    me = me_ref[2]
    for step, ref in enumerate((own_ref, *outs)):
        index = (me + step) % 4
        value = jnp.where(
            index < 2, jnp.where(index == 0, total[0], total[1]), jnp.where(index == 2, total[2], total[3])
        )
        ref[...] = value.astype(ref.dtype)


def final_stage_kernel(own, *refs):
    cross_refs, self_refs, outs = refs[:4], refs[4:8], refs[8:]
    proj_ref, out_ref, bias_ref, gain_ref, shift_ref, hidden_ref, last_ref = outs
    cross = functools.reduce(jnp.add, [r[...].astype(F32) for r in cross_refs])
    selfs = functools.reduce(jnp.add, [r[...].astype(F32) for r in self_refs])
    for i in range(3):
        proj_ref[i] = selfs[i * own : (i + 1) * own]
    for ref, index, at in ((proj_ref, 4, 0), (proj_ref, 5, 1), (out_ref, 1, 2), (out_ref, 0, 3), (proj_ref, 3, 4)):
        ref[index] = cross[at * own : (at + 1) * own]
    sums = selfs[3 * own : 3 * own + 16, :128]
    bias_ref[...] = sums[0:6, :own]
    for ref, lines in ((gain_ref, (6, 11, 8)), (shift_ref, (7, 12, 9))):
        for i, line in enumerate(lines):
            ref[i : i + 1] = sums[line : line + 1, :own]
    hidden_ref[...] = sums[15:16, : hidden_ref.shape[1]]
    last_ref[...] = sums[10:11, :own]


def stage_call(kernel, me, args, outs, name):
    data = sum(a.size * a.dtype.itemsize for a in args)
    return pl.pallas_call(
        kernel,
        in_specs=[pl.BlockSpec(memory_space=pltpu.SMEM)] + [pl.BlockSpec(memory_space=pltpu.VMEM)] * len(args),
        out_specs=[pl.BlockSpec(memory_space=pltpu.VMEM)] * len(outs),
        out_shape=outs,
        compiler_params=pltpu.CompilerParams(vmem_limit_bytes=VMEM_LIMIT),
        cost_estimate=cost(data, 2 * data),
        name=name,
    )(me, *args)


def first_stage(me, keep, got):
    x, z, y, rows, d = keep.shape
    line = lambda *lead: pl.BlockSpec((*lead, rows, d // 2), lambda i: (i, 0, 0, 0))
    both = pl.BlockSpec((x, 1, y, rows, d), lambda i: (0, i, 0, 0, 0))
    side = pl.BlockSpec((x, 1, rows, d // 2), lambda i: (0, i, 0, 0))
    left, right = shape((z, y, rows, d // 2), BF), shape((x, z, rows, d // 2), BF)
    return pl.pallas_call(
        first_stage_kernel,
        grid=(z,),
        in_specs=[pl.BlockSpec(memory_space=pltpu.SMEM), both, both],
        out_specs=[line(1, y), line(1, y), side, side],
        out_shape=[left, left, right, right],
        compiler_params=params(("arbitrary",)),
        cost_estimate=cost(keep.size, 6 * keep.size),
        name="first_stage",
    )(me, keep, got)


def row_block(width):
    return pl.BlockSpec((SEQ_MAX, width), lambda b: (b, 0))


def fine_block(width):
    return pl.BlockSpec((FINE, width), lambda b: (b, 0))


def col_block(height):
    return pl.BlockSpec((height, SEQ_MAX), lambda b: (0, b))


def lead_block(rows):
    return pl.BlockSpec((1, rows, SEQ_MAX), lambda b: (b, 0, 0))


def whole(array, **kw):
    zeros = (0,) * array.ndim
    return pl.BlockSpec(array.shape, lambda *_: zeros, pipeline_mode=pl.Buffered(1))


def planes(array, start, count):
    return pl.BlockSpec(
        (count, *array.shape[1:]), lambda *_: (start // count, 0, 0), pipeline_mode=pl.Buffered(1)
    )


def params(semantics):
    return pltpu.CompilerParams(vmem_limit_bytes=VMEM_LIMIT, dimension_semantics=semantics)


def cost(flops, data, exps=0):
    return pl.CostEstimate(flops=int(flops), bytes_accessed=int(data), transcendentals=int(exps))


def shape(dims, kind):
    return jax.ShapeDtypeStruct(dims, kind)


def self_forward(x, wqk, wv, bias, kmark, qmark):
    rows, d = x.shape
    blocks = rows // SEQ_MAX
    act = shape((rows, d), BF)
    return pl.pallas_call(
        self_forward_kernel,
        grid=(blocks,),
        in_specs=[row_block(d), whole(wqk), whole(wv), whole(bias), row_block(128), lead_block(HEAD_DIM)],
        out_specs=[row_block(d), row_block(d), row_block(d), col_block(d), lead_block(16)],
        out_shape=[act, act, act, shape((d, rows), BF), shape((blocks, 16, SEQ_MAX), F32)],
        scratch_shapes=[pltpu.VMEM((d, SEQ_MAX), BF)] * 2,
        compiler_params=params(("arbitrary",)),
        cost_estimate=cost(20e9, 12e6),
        name="self_forward",
    )(x, wqk, wv, bias, kmark, qmark)


def cross_forward(x, mem, sot, wo, wo_at, w, bias, gain, shift, kmark, qmark):
    rows, d = x.shape
    blocks = rows // SEQ_MAX
    act, wide = shape((rows, d), BF), shape((rows, d), F32)
    return pl.pallas_call(
        cross_forward_kernel,
        grid=(blocks,),
        in_specs=[
            row_block(d), row_block(d), col_block(d), planes(wo, wo_at, 2), planes(w, 0, 3), whole(bias), whole(gain),
            whole(shift),
            row_block(128), lead_block(HEAD_DIM),
        ],
        out_specs=[row_block(d)] * 5 + [col_block(d), lead_block(16), row_block(d)],
        out_shape=[wide, act, act, act, act, shape((d, rows), BF), shape((blocks, 16, SEQ_MAX), F32), wide],
        scratch_shapes=[pltpu.VMEM((d, SEQ_MAX), BF)] * 2,
        compiler_params=params(("arbitrary",)),
        cost_estimate=cost(24e9, 20e6),
        name="cross_forward",
    )(x, mem, sot, wo, w, bias, gain, shift, kmark, qmark)


def feed(second_sum, cot, win, bin_, wout, bout, gain, shift):
    rows, d = second_sum.shape
    width = win.shape[2]
    ff = bin_.shape[1]
    chunks = ff // width
    own = wout.shape[2] if wout.ndim == 4 else 0
    fixed = lambda p, j: (0, 0)
    parts = chunks if own else 1
    if own:
        wout_spec = pl.BlockSpec((parts, width // (parts * own), own, d), lambda p, j: (1, j, 0, 0))
    else:
        wout_spec = pl.BlockSpec((width, d), lambda p, j: (j, 0))
    return pl.pallas_call(
        functools.partial(feed_kernel, own),
        grid=(2, chunks),
        in_specs=[
            whole(second_sum), whole(cot),
            pl.BlockSpec((1, d, width), lambda p, j: (jnp.where(j == 0, 3, 7 + j) if own else j, 0, 0)),
            pl.BlockSpec((1, width), lambda p, j: (0, j)),
            wout_spec, whole(bout), whole(gain), whole(shift),
        ],
        out_specs=[
            pl.BlockSpec((rows, d), fixed),
            pl.BlockSpec((rows, d), fixed),
            pl.BlockSpec(memory_space=pl.ANY),
            pl.BlockSpec((1, width), lambda p, j: (0, j * p)),
            pl.BlockSpec((8, d), fixed),
        ],
        out_shape=[
            shape((rows, d), BF), shape((rows, d), F32), shape((d, 2 * ff), BF),
            shape((1, ff), F32), shape((8, d), F32),
        ],
        scratch_shapes=[
            pltpu.VMEM((rows, d), BF), pltpu.VMEM((d, rows), BF),
            pltpu.VMEM((chunks, rows, width), BF), pltpu.VMEM((chunks, rows, width), F32),
            pltpu.VMEM((rows, d), F32), pltpu.VMEM((rows, d), BF),
            pltpu.VMEM((2, d, width), BF), pltpu.VMEM((2, parts, width // parts, d), BF),
            pltpu.SemaphoreType.DMA((1 + parts, 2)),
        ],
        compiler_params=params(("arbitrary", "arbitrary")),
        cost_estimate=cost(40e9, 40e6),
        name="feed",
    )(second_sum, cot, win, bin_, wout, bout, gain, shift)


def back_scratch(d):
    return (
        [pltpu.VMEM((d, SEQ_MAX), BF)] * 2 + [pltpu.VMEM((SEQ_MAX, d), BF)] + [pltpu.VMEM((d, SEQ_MAX), BF)] * 2
    )


def at_row(block, width):
    return pl.BlockSpec((SEQ_MAX, width), lambda b: (block, 0))


def at_col(block, height):
    return pl.BlockSpec((height, SEQ_MAX), lambda b: (0, block))


def at_lead(block, rows):
    return pl.BlockSpec((1, rows, SEQ_MAX), lambda b: (block, 0, 0))


def one_back(kernel, block, before, args, specs, outs, name):
    d = outs[0].shape[1]
    kept = [pl.BlockSpec(memory_space=pl.ANY)] * len(before)
    return pl.pallas_call(
        kernel,
        grid=(1,),
        in_specs=specs + kept,
        out_specs=[at_row(block, d)] * len(outs) + [pl.BlockSpec((8, d), lambda b: (0, 0))],
        out_shape=outs + [shape((8, d), F32)],
        scratch_shapes=back_scratch(d),
        input_output_aliases={len(args) + i: i for i in range(len(before))},
        compiler_params=params(("arbitrary",)),
        cost_estimate=cost(25e9, 15e6),
        name=name,
    )(*args, *before)


def cross_back(block, before, wo_at, ssg, first_sum, q, k, v, ot, lse, wo, w, gain, kmark, qmark):
    rows, d = first_sum.shape
    act = shape((rows, d), BF)
    specs = [at_row(block, d)] * 5 + [
        at_col(block, d), at_lead(block, 16), planes(wo, wo_at + 1, 1), planes(w, 0, 1), whole(gain), at_row(block, 128), at_lead(block, HEAD_DIM),
    ]
    args = (ssg, first_sum, q, k, v, ot, lse, wo, w, gain, kmark, qmark)
    return one_back(
        cross_back_kernel, block, before, args, specs, [shape((rows, d), F32), act, act, act], f"cross_back_{block}"
    )


def self_back(block, before, wo_at, fsg, q, k, v, ot, lse, wo, kmark, qmark):
    rows, d = fsg.shape
    act = shape((rows, d), BF)
    specs = [at_row(block, d)] * 4 + [
        at_col(block, d), at_lead(block, 16), planes(wo, wo_at, 1), at_row(block, 128), at_lead(block, HEAD_DIM),
    ]
    args = (fsg, q, k, v, ot, lse, wo, kmark, qmark)
    return one_back(self_back_kernel, block, before, args, specs, [act, act, act], f"self_back_{block}")


def weight_outs(staged, count, extra, devices, d):
    if not staged:
        return [shape((count, d, d), BF), shape((1,), jnp.int32)], pltpu.VMEM((count, d, d), BF)
    rows = count * d // devices + extra
    half = shape((2, 4, 2, rows, d), BF)
    return [half, half], pltpu.VMEM((2, 2, 4, 2, rows, d), BF)


def cross_weight(staged, me, devices, dq, dk, dv, low, mem, ot, ssg, sot, fsg):
    rows, d = dq.shape
    args = (mem, dk, dv, ot, ssg, sot, fsg, low, dq)
    anywhere = pl.BlockSpec(memory_space=pl.ANY)
    outs, scratch = weight_outs(staged, 5, 0, devices, d)
    last = anywhere if staged else pl.BlockSpec(memory_space=pltpu.SMEM)
    return pl.pallas_call(
        functools.partial(cross_weight_kernel, staged),
        in_specs=[pl.BlockSpec(memory_space=pltpu.SMEM)] + [anywhere] * 9,
        out_specs=[anywhere, last],
        out_shape=outs,
        scratch_shapes=[pltpu.VMEM(a.shape, a.dtype) for a in args] + [
            scratch, pltpu.SemaphoreType.DMA((9,)), pltpu.SemaphoreType.DMA((4,)),
        ],
        compiler_params=pltpu.CompilerParams(vmem_limit_bytes=VMEM_LIMIT),
        cost_estimate=cost(9e9, 20e6),
        name="cross_weight",
    )(me, *args)


def self_last(staged, me, devices, block, before, wo_at, fsg, q, k, v, ot, lse, wo, kmark, qmark, sums, dbin, x):
    rows, d = x.shape
    anywhere, here = pl.BlockSpec(memory_space=pl.ANY), pl.BlockSpec(memory_space=pltpu.VMEM)
    outs, scratch = weight_outs(staged, 3, 16, devices, d)
    act = shape((rows, d), BF)
    args = (me, fsg, q, k, v, ot, lse, wo, kmark, qmark, sums, dbin, x)
    if not before:
        before = [jnp.zeros((rows, d), BF)] * 3
    fixed = lambda array: pl.BlockSpec(array.shape, lambda b: (0,) * array.ndim)
    if not staged:
        outs[1] = shape((16, d), F32)
    return pl.pallas_call(
        functools.partial(self_last_kernel, staged),
        grid=(1,),
        in_specs=[pl.BlockSpec(memory_space=pltpu.SMEM)] + [at_row(block, d)] * 4 + [
            at_col(block, d), at_lead(block, 16), planes(wo, wo_at, 1), at_row(block, 128), at_lead(block, HEAD_DIM),
            fixed(sums), fixed(dbin), anywhere,
        ] + [anywhere] * 3,
        out_specs=[anywhere, anywhere if staged else fixed(outs[1])] + [anywhere] * 3,
        out_shape=outs + [act] * 3,
        scratch_shapes=back_scratch(d) + [pltpu.VMEM((rows, d), BF)] * 4 + [
            scratch, pltpu.SemaphoreType.DMA((7,)), pltpu.SemaphoreType.DMA((4,)),
        ],
        input_output_aliases={len(args) + i: 2 + i for i in range(3)},
        compiler_params=params(("arbitrary",)),
        cost_estimate=cost(25e9, 20e6),
        name="self_last",
    )(*args, *before)


def memory_input(dk, dv, w):
    rows, d = dk.shape
    return pl.pallas_call(
        memory_input_kernel,
        grid=(rows // FINE,),
        in_specs=[fine_block(d)] * 2 + [planes(w, 1, 1), planes(w, 2, 1)],
        out_specs=fine_block(d),
        out_shape=shape((rows, d), F32),
        compiler_params=params(("arbitrary",)),
        cost_estimate=cost(3e9, 9e6),
        name="memory_input",
    )(dk, dv, w, w)


def self_input(fsg, dq, dk, dv, wqk, wv):
    rows, d = fsg.shape
    return pl.pallas_call(
        self_input_kernel,
        grid=(rows // FINE,),
        in_specs=[fine_block(d)] * 4 + [whole(wqk), whole(wv)],
        out_specs=fine_block(d),
        out_shape=shape((rows, d), F32),
        compiler_params=params(("arbitrary",)),
        cost_estimate=cost(4e9, 14e6),
        name="self_input",
    )(fsg, dq, dk, dv, wqk, wv)


def key_marks(seg):
    odd = (seg & 1)[:, None]
    lane = lax.broadcasted_iota(jnp.int32, (seg.shape[0], 128), 1) % HEAD_DIM
    return jnp.where(lane == 0, 1 - odd, jnp.where(lane == 1, odd, 0)).astype(BF)


def query_marks(seg):
    odd = (seg & 1).reshape(-1, 1, SEQ_MAX)
    row = lax.broadcasted_iota(jnp.int32, (odd.shape[0], HEAD_DIM, SEQ_MAX), 1)
    return jnp.where(row == 0, odd, jnp.where(row == 1, 1 - odd, 0)).astype(BF) * (-MASKED)


def swap(value, name):
    return lax.ppermute(value, name, [(0, 1), (1, 0)])


class Halving:
    def __init__(self, me, keep, send):
        self.me, self.keep, self.out = me, [keep], [send]

    def core(self):
        got = swap(self.out[0], "c")
        sl, kl, sr, kr = first_stage(self.me, self.keep[0], got)
        self.keep, self.out = [kl, kr], [sl, sr]

    def first(self):
        (kl, kr), (sl, sr) = self.keep, self.out
        gl, gr = swap(sl, "x"), swap(sr, "y")
        z, _, rows, half = kl.shape
        piece = shape((z, rows, half), BF)
        sl, ml, sr, mr = stage_call(second_stage_kernel, self.me, (kl, gl, kr, gr), [piece] * 4, "second_stage")
        self.keep, self.out = [ml, mr], [sl, sr]

    def second(self):
        (kl, kr), (sl, sr) = self.keep, self.out
        gl, gr = swap(sl, "y"), swap(sr, "x")
        _, rows, half = kl.shape
        piece = (rows, 2 * half)
        outs = [shape(piece, F32)] + [shape(piece, BF)] * 3
        own, *self.out = stage_call(third_stage_kernel, self.me, (kl, gl, kr, gr), outs, "third_stage")
        self.keep = [own]

    def last(self):
        steps = zip(range(1, 4), self.out)
        return self.keep + [lax.ppermute(out, "z", [(i, (i + step) % 4) for i in range(4)]) for step, out in steps]

    @staticmethod
    def finish(cross, selfs, small, dbin, own, devices):
        d = cross[0].shape[1]
        wide = dbin.shape[1] // devices
        outs = [
            shape(dims, F32)
            for dims in ((6, own, d), (2, own, d), (6, own), (3, own), (3, own), (1, wide), (1, own))
        ]
        args = cross + selfs
        proj, out, bias, gain, shift, hidden, last = pl.pallas_call(
            functools.partial(final_stage_kernel, own),
            in_specs=[pl.BlockSpec(memory_space=pltpu.VMEM)] * 8,
            out_specs=[pl.BlockSpec(memory_space=pltpu.VMEM)] * 7,
            out_shape=outs,
            compiler_params=pltpu.CompilerParams(vmem_limit_bytes=VMEM_LIMIT),
            cost_estimate=cost(2e6, 3e6),
            name="final_stage",
        )(*args)
        return proj, out, bias, gain, shift, hidden.reshape(-1), last.reshape(-1)

    @staticmethod
    def feed(grads, own):
        sums = lax.psum_scatter(grads, ("x", "c", "z", "y"), scatter_dimension=0, tiled=True).astype(F32)
        half = sums.shape[1] // 2
        d = grads.shape[0]
        return sums[:, :half], sums[:, half:].reshape(own, -1, d).swapaxes(0, 1).reshape(-1, d)


class Whole:
    def __init__(self, me, grads, _):
        self.grads, self.out, self.keep = grads, (), ()

    def core(self):
        pass

    first = second = core

    def last(self):
        sums = lax.psum_scatter(self.grads, ("dp", "fsdp"), scatter_dimension=1, tiled=True).astype(F32)
        return sums.reshape(-1, sums.shape[2])

    @staticmethod
    def finish(cross, selfs, small, dbin, own, devices):
        sum_up = functools.partial(lax.psum_scatter, axis_name=("dp", "fsdp"), scatter_dimension=1, tiled=True)
        small, dbin = sum_up(small), sum_up(dbin)[0]
        cross, selfs = cross.reshape(5, own, -1), selfs.reshape(3, own, -1)
        proj = jnp.concatenate([selfs, cross[4:], cross[:2]])
        gain, shift = jnp.stack([small[6], small[11], small[8]]), jnp.stack([small[7], small[12], small[9]])
        return proj, cross[3:1:-1], small[0:6], gain, shift, dbin, small[10]

    @staticmethod
    def feed(grads, own):
        sum_up = functools.partial(lax.psum_scatter, axis_name=("dp", "fsdp"), scatter_dimension=0, tiled=True)
        half, d = grads.shape[1] // 2, grads.shape[0]
        dwin = sum_up(grads[:, :half]).astype(F32)
        return dwin, sum_up(grads[:, half:].reshape(d, -1, d).swapaxes(0, 1).reshape(-1, d)).astype(F32)


def after(value, *sums):
    value, outs = lax.optimization_barrier((value, [s.out for s in sums]))
    for s, s.out in zip(sums, outs):
        pass
    return value


def hold(sums, value):
    sums.keep = lax.optimization_barrier((sums.keep, value))[0]


def take_turns(value):
    me = lax.axis_index("z")
    parts = [value]
    for step in range(3, 0, -1):
        parts.append(lax.ppermute(value, "z", [(i, (i + step) % 4) for i in range(4)]))
    return jnp.stack([lax.select_n((j - me) % 4, *parts) for j in range(4)], axis=1)


def take_pair(value, name, axis):
    me = lax.axis_index(name)
    got = lax.ppermute(value, name, [(0, 1), (1, 0)])
    return jnp.stack([jnp.where(me == 0, value, got), jnp.where(me == 0, got, value)], axis=axis)


class Doubling:
    def __init__(self, left, right):
        self.cut, self.rows = left.shape[0], left.shape[1]
        self.flat = left.shape[1:] != right.shape[1:]
        if self.flat:
            left, right = (a.reshape(1, -1, a.shape[2]) for a in (left, right))
            self.out = [jnp.concatenate([left, right], axis=1)]
            self.split = left.shape[1]
        else:
            self.out = [jnp.concatenate([left, right])]

    def line(self):
        both = take_turns(self.out[0])
        if self.flat:
            d = both.shape[3]
            left = both[0, :, : self.split].reshape(4, self.cut, self.rows, d).swapaxes(0, 1)
            self.out = [left, both[:, :, self.split :]]
        else:
            self.out = [both[: self.cut], both[self.cut :]]

    def first(self):
        self.out = [take_pair(self.out[0], "y", 2), take_pair(self.out[1], "x", 1)]

    def second(self):
        self.out = [take_pair(self.out[0], "x", 1), take_pair(self.out[1], "y", 3)]

    def core(self):
        self.out = [take_pair(self.out[0], "c", 2), take_pair(self.out[1], "c", 2)]
        return self.out


def local_small(bias, gain, shift, bin_, bout):
    return jnp.concatenate([a.reshape(-1) for a in (bias, gain, shift, bout, bin_)])


def spread_small(parts, own):
    parts = parts.astype(F32)
    devices = parts.shape[0]
    rows = parts[:, : 13 * own].reshape(devices, 13, own).swapaxes(0, 1).reshape(13, -1)
    bin_ = parts[:, 13 * own :].reshape(1, -1)
    return {"bias": rows[0:6], "gain": rows[6:9], "shift": rows[9:12], "bout": rows[12:13], "bin": bin_}


class Stages:
    out_at = 0

    def __init__(self, proj, out, small, win, wout):
        _, own, d = proj.shape
        panels = win.reshape(own, -1, d).swapaxes(0, 1)
        rest = jnp.concatenate([proj[3:6], panels[:1], wout.reshape(-1, own, d), panels[1:]])
        self.rest = lax.all_gather(rest, ("x", "c", "z", "y"), axis=1)
        extra = jnp.pad(small[None, None], ((0, 0), (0, 7), (0, d - small.shape[0])))
        self.one = Doubling(proj[:2], jnp.concatenate([proj[2:3], extra], axis=1))
        self.two = Doubling(out[:1], out[1:])
        self.own, self.cut, self.d = own, small.shape[0], d

    def begin(self):
        one, own, d = self.one, self.own, self.d
        one.line()
        one.first()
        self.two.out = after(self.two.out, one)
        one.second()
        left, right = one.core()
        full = {"qk": left.reshape(2, -1, d), "v": right[..., :own, :].reshape(1, -1, d)}
        full.update(spread_small(right[..., own, : self.cut].reshape(-1, self.cut), own))
        return full

    def finish(self, value):
        planes = self.rest.reshape(self.rest.shape[0], -1, self.d)
        two = self.two
        two.line()
        two.out, value = lax.optimization_barrier((two.out, value))
        two.first()
        two.second()
        out = jnp.concatenate(two.core()).reshape(2, -1, self.d)
        return {"cross_proj": planes, "out": out, "win": planes, "wout": self.rest}, value


class Plain:
    out_at = 0

    def __init__(self, proj, out, small, win, wout):
        take = functools.partial(lax.all_gather, axis_name=("dp", "fsdp"), tiled=True)
        _, own, d = proj.shape
        proj = take(proj, axis=1)
        self.full = {"qk": proj[:2], "v": proj[2:3]}
        self.full.update(spread_small(take(small[None], axis=0), own))
        win = take(win, axis=0).reshape(d, -1, d).swapaxes(0, 1)
        self.rest = {"cross_proj": proj[3:], "out": take(out, axis=1), "win": win, "wout": take(wout, axis=0)}

    def begin(self):
        return self.full

    def finish(self, value):
        return self.rest, value


def body(
    gather, scatter, devices, query, memory, query_seg, memory_seg, attn_proj, attn_out, attn_bias, norm_gain, norm_bias,
    ffn_in, ffn_in_bias, ffn_out, ffn_out_bias, cotangent,
):
    blocks = range(query.shape[0] // SEQ_MAX)
    own = attn_proj.shape[1]
    d = query.shape[1]
    staged = scatter is Halving
    me, pair = jnp.zeros((3,), jnp.int32), jnp.zeros((1,), jnp.int32)
    if staged:
        me = jnp.stack([lax.axis_index(name) for name in ("x", "y", "z")])
        pair = lax.axis_index("c").reshape(1)
    small = local_small(attn_bias, norm_gain, norm_bias, ffn_in_bias, ffn_out_bias)
    weights = gather(attn_proj, attn_out, small, ffn_in, ffn_out)
    full = weights.begin()
    bias, gain, shift = full["bias"], full["gain"], full["shift"]
    qmark = query_marks(query_seg)
    smark, cmark = key_marks(query_seg), key_marks(memory_seg)
    sq, sk, sv, sot, slse = self_forward(query, full["qk"], full["v"], bias, smark, qmark)
    (rest, sot), out_at = weights.finish(sot), weights.out_at
    out, cross_proj = rest["out"], rest["cross_proj"]
    first_sum, low, cq, ck, cv, cot_, clse, second_sum = cross_forward(
        query, memory, sot, out, out_at, cross_proj, bias, gain, shift, cmark, qmark
    )
    mixed, ssg, fdw, dbin, small3 = feed(
        second_sum, cotangent, rest["win"], full["bin"], rest["wout"], full["bout"], gain, shift
    )
    dwin, dwout = scatter.feed(fdw, own)
    grads, small2 = [], 0
    for block in blocks:
        *grads, part = cross_back(
            block, grads, out_at, ssg, first_sum, cq, ck, cv, cot_, clse, out, cross_proj, gain, cmark, qmark
        )
        small2 = small2 + part
    fsg, dq, dk, dv = grads
    keep, send = cross_weight(staged, pair, devices, dq, dk, dv, low, memory, cot_, ssg, sot, fsg)
    cross_sum = scatter(me, keep, send)
    dk = after(dk, cross_sum)
    memory_grad = memory_input(dk, dv, cross_proj)
    cross_sum.core()
    upstream, memory_grad = after((fsg, memory_grad), cross_sum)
    grads = []
    small1 = jnp.zeros((8, d), F32)
    for block in blocks[:-1]:
        *grads, part = self_back(block, grads, out_at, upstream, sq, sk, sv, sot, slse, out, smark, qmark)
        small1 = small1 + part
    cross_sum.first()
    upstream = after(upstream, cross_sum)
    sums = jnp.concatenate([small1[:3], small2[:5], small3[:5], jnp.zeros((3, d), F32)])
    keep, send, dq, dk, dv = self_last(
        staged, pair, devices, blocks[-1], grads, out_at, upstream, sq, sk, sv, sot, slse, out, smark, qmark, sums, dbin,
        query,
    )
    self_sum = scatter(me, keep, send)
    cross_sum.second()
    self_sum.out = after(self_sum.out, cross_sum)
    self_sum.core()
    upstream = after(fsg, self_sum, cross_sum)
    query_grad = self_input(upstream, dq, dk, dv, full["qk"], full["v"])
    cross = cross_sum.last()
    hold(self_sum, (query_grad, cross))
    self_sum.first()
    self_sum.second()
    selfs, dwin, dwout = lax.optimization_barrier((self_sum.last(), dwin, dwout))
    proj_g, out_g, bias_g, gain_g, shift_g, dbin_g, dbout_g = scatter.finish(cross, selfs, send, dbin, own, devices)
    return (
        mixed, query_grad, memory_grad, proj_g, out_g, bias_g, gain_g, shift_g, dwin, dbin_g, dwout, dbout_g,
    )


def solution(mesh):
    devices = mesh.size
    if dict(mesh.shape) == {"dp": 4, "fsdp": 8}:
        axes = ("x", "c", "z", "y")
        mesh = Mesh(mesh.devices.reshape(2, 2, 4, 2), axes)
        gather, scatter = Stages, Halving
    else:
        axes = ("dp", "fsdp")
        gather, scatter = Plain, Whole
    rows, mid, flat, row1 = P(axes, None), P(None, axes, None), P(None, axes), P(axes)
    return jax.shard_map(
        functools.partial(body, gather, scatter, devices),
        mesh=mesh,
        in_specs=(rows, rows, row1, row1, mid, mid, flat, flat, flat, rows, row1, rows, row1, rows),
        out_specs=(rows, rows, rows, mid, mid, flat, flat, flat, rows, row1, rows, row1),
        check_vma=False,
    )
```

```python
import functools

import jax
import jax.numpy as jnp
from jax import lax
from jax.experimental import pallas as pl
from jax.experimental.pallas import tpu as pltpu
from jax.sharding import Mesh
from jax.sharding import PartitionSpec as P

HEADS = 12
HEAD_DIM = 64
SEQ_MAX = 512
PAIRS = HEADS // 2
FINE = 512
EPSILON = 1e-05
MASKED = 1e30
SCALE = HEAD_DIM ** (-0.5)
BF = jnp.bfloat16
F32 = jnp.float32
VMEM_LIMIT = 60 * 1024 * 1024


def dot(left, right):
    return jnp.dot(left, right, preferred_element_type=F32)


def dot_nt(left, right):
    return lax.dot_general(left, right, (((1,), (1,)), ((), ())), preferred_element_type=F32)


def norm_parts(resid):
    center = resid - jnp.mean(resid, axis=-1, keepdims=True)
    rstd = lax.rsqrt(jnp.mean(center * center, axis=-1, keepdims=True) + EPSILON)
    return center * rstd, rstd


def norm_back(unit, rstd, gain, upstream):
    scaled = upstream * gain
    mean_s = jnp.mean(scaled, axis=-1, keepdims=True)
    mean_su = jnp.mean(scaled * unit, axis=-1, keepdims=True)
    grad = rstd * (scaled - mean_s - unit * mean_su)
    return grad, col_sum(upstream * unit), col_sum(upstream)


def col_sum(rows):
    return jnp.sum(rows, axis=0, keepdims=True)


def place_rows(rows, count):
    parts = list(rows)
    parts.append(jnp.zeros((count - len(parts), parts[0].shape[1]), F32))
    return jnp.concatenate(parts, axis=0)


def gelu_parts(value):
    size = jnp.abs(value) * (0.5**0.5)
    bell = jnp.exp(-0.5 * value * value)
    t = 1.0 / (1.0 + 0.3275911 * size)
    poly = t * (0.254829592 + t * (-0.284496736 + t * (1.421413741 + t * (-1.453152027 + t * 1.061405429))))
    tail = 0.5 * poly * bell
    phi = jnp.where(value >= 0, 1.0 - tail, tail)
    return value * phi, phi + value * (bell * (1.0 / (2.0 * 3.141592653589793) ** 0.5))


def left_half(shape):
    return lax.broadcasted_iota(jnp.int32, shape, 1) < HEAD_DIM


def head_pair(side, pair):
    return pl.ds(pl.multiple_of(pair * 128 + side * HEAD_DIM, HEAD_DIM), HEAD_DIM)


def key_tile(tile, marks, side):
    left = left_half(tile.shape)
    return jnp.where(left, tile, marks) if side == 0 else jnp.where(left, marks, tile)


def query_tile(rows, marks, side):
    return jnp.concatenate([rows, marks] if side == 0 else [marks, rows], axis=0)


def attend_block(k_ref, qt_ref, vt_ref, kmark_ref, qmark_ref, ot_ref, lse_ref):
    kmark = kmark_ref[...]
    qmark = qmark_ref[0]
    ones = jnp.ones((16, SEQ_MAX), BF)

    def score(head):
        pair, side = head // 2, head % 2
        rows = slice(head * HEAD_DIM, (head + 1) * HEAD_DIM)
        tile = k_ref[:, pair * 128 : (pair + 1) * 128]
        return dot(key_tile(tile, kmark, side), query_tile(qt_ref[rows, :], qmark, side))

    def finish(head, peak, weights):
        rows = slice(head * HEAD_DIM, (head + 1) * HEAD_DIM)
        result = dot(jnp.concatenate([vt_ref[rows, :], ones], axis=0), weights)
        total = result[HEAD_DIM : HEAD_DIM + 1]
        ot_ref[rows, :] = (result[:HEAD_DIM] * (1.0 / total)).astype(BF)
        lse_ref[0, head : head + 1, :] = peak + jnp.log(total)

    for start in range(0, HEADS, 6):
        heads = range(start, start + 6)
        scores = [score(head) for head in heads]
        peaks = [jnp.max(s, axis=0, keepdims=True) for s in scores]
        weights = [jnp.exp(s - peak).astype(BF) for s, peak in zip(scores, peaks)]
        for head, peak, weight in zip(heads, peaks, weights):
            finish(head, peak, weight)


def attend_back_block(
    q_ref, k_ref, v_ref, qt_ref, kt_ref, ot_ref, do_ref, dot_ref, kmark_ref, qmark_ref, lse_ref, dqt_ref, dk_ref, dv_ref
):
    kmark = kmark_ref[...]
    qmark = qmark_ref[0]
    left = left_half((SEQ_MAX, 128))
    blank = jnp.zeros((HEAD_DIM, SEQ_MAX), BF)

    def begin(head):
        pair, side = head // 2, head % 2
        rows = slice(head * HEAD_DIM, (head + 1) * HEAD_DIM)
        cols = slice(pair * 128, (pair + 1) * 128)
        scores = dot(key_tile(k_ref[:, cols], kmark, side), query_tile(qt_ref[rows, :], qmark, side))
        up = dot_ref[rows, :]
        probs_grad = dot(v_ref[:, cols], query_tile(up, blank, side))
        return scores, probs_grad, col_sum(up.astype(F32) * ot_ref[rows, :].astype(F32))

    def middle(head, scores, probs_grad, center):
        probs = jnp.exp(scores - lse_ref[0, head : head + 1, :])
        return probs.astype(BF), (probs * (probs_grad - center)).astype(BF)

    def finish(head, probs, score_grad):
        rows = slice(head * HEAD_DIM, (head + 1) * HEAD_DIM)
        cols = slice(head // 2 * 128, (head // 2 + 1) * 128)
        dqt_ref[rows, :] = (dot(kt_ref[rows, :], score_grad) * SCALE).astype(BF)
        return dot(probs, do_ref[:, cols]), dot(score_grad, q_ref[:, cols])

    for start in range(0, HEADS, 4):
        heads = range(start, start + 4)
        begun = [begin(head) for head in heads]
        mid = [middle(head, *b) for head, b in zip(heads, begun)]
        done = [finish(head, *m) for head, m in zip(heads, mid)]
        for i in range(0, 4, 2):
            cols = slice((start + i) // 2 * 128, ((start + i) // 2 + 1) * 128)
            dv_ref[:, cols] = jnp.where(left, done[i][0], done[i + 1][0]).astype(BF)
            dk_ref[:, cols] = jnp.where(left, done[i][1], done[i + 1][1]).astype(BF)


def self_forward_kernel(
    x_ref, wqk_ref, wv_ref, bias_ref, kmark_ref, qmark_ref, q_ref, k_ref, v_ref, ot_ref, lse_ref, qt_s, vt_s
):
    x = x_ref[...]
    queries = ((dot(x, wqk_ref[0]) + bias_ref[0:1]).astype(BF)) * SCALE
    q_ref[...] = queries
    qt_s[...] = queries.T
    k_ref[...] = dot(x, wqk_ref[1]).astype(BF)
    values = (dot(x, wv_ref[0]) + bias_ref[1:2]).astype(BF)
    v_ref[...] = values
    vt_s[...] = values.T
    attend_block(k_ref, qt_s, vt_s, kmark_ref, qmark_ref, ot_ref, lse_ref)


def cross_forward_kernel(
    x_ref, mem_ref, sot_ref, wo_ref, w_ref, bias_ref, gain_ref, shift_ref, kmark_ref, qmark_ref,
    first_sum_ref, low_ref, q_ref, k_ref, v_ref, ot_ref, lse_ref, second_sum_ref, qt_s, vt_s,
):
    mem = mem_ref[...]
    k_ref[...] = dot(mem, w_ref[1]).astype(BF)
    values = (dot(mem, w_ref[2]) + bias_ref[4:5]).astype(BF)
    v_ref[...] = values
    vt_s[...] = values.T
    first_sum = x_ref[...].astype(F32) + (dot(sot_ref[...].T, wo_ref[0]) + bias_ref[2:3])
    first_sum_ref[...] = first_sum
    unit, _ = norm_parts(first_sum)
    first = unit * gain_ref[0:1] + shift_ref[0:1]
    low = first.astype(BF)
    low_ref[...] = low
    queries = ((dot(low, w_ref[0]) + bias_ref[3:4]).astype(BF)) * SCALE
    q_ref[...] = queries
    qt_s[...] = queries.T
    attend_block(k_ref, qt_s, vt_s, kmark_ref, qmark_ref, ot_ref, lse_ref)
    second_sum_ref[...] = first + (dot(ot_ref[...].T, wo_ref[1]) + bias_ref[5:6])


def feed_kernel(
    own, ss_ref, cot_ref, win_ref, bin_ref, wout_ref, bout_ref, gain_ref, shift_ref,
    mixed_ref, ssg_ref, dw_ref, dbin_ref, small_ref,
    low_s, lowt_s, hid_s, slope_s, acc_s, z_s, din_s, dout_s, sems,
):
    phase, chunk = pl.program_id(0), pl.program_id(1)
    chunks = pl.num_programs(1)
    last = chunks - 1
    slot = chunk % 2
    width, d = dout_s.shape[1] * dout_s.shape[2], dout_s.shape[3]
    parts = dout_s.shape[1]

    def wout():
        if not own:
            return wout_ref[...]
        groups = wout_ref[...].astype(F32)
        return jnp.concatenate([groups[:, i] for i in range(groups.shape[1])], axis=0).reshape(width, d).astype(BF)

    def sends(slot, chunk):
        if own:
            group = width // parts
            rows = pl.ds(pl.multiple_of(chunk * group, group), group)
            outs = [
                pltpu.make_async_copy(
                    dout_s.at[slot, part], dw_ref.at[rows, pl.ds((chunks + part) * width, width)], sems.at[1 + part, slot]
                )
                for part in range(parts)
            ]
        else:
            cols = pl.ds(pl.multiple_of((chunks + chunk) * width, width), width)
            outs = [pltpu.make_async_copy(dout_s.at[slot, 0], dw_ref.at[:, cols], sems.at[1, slot])]
        cols = pl.ds(pl.multiple_of(chunk * width, width), width)
        return [pltpu.make_async_copy(din_s.at[slot], dw_ref.at[:, cols], sems.at[0, slot])] + outs

    @pl.when((phase == 0) & (chunk == 0))
    def _():
        unit, _ = norm_parts(ss_ref[...])
        second = unit * gain_ref[1:2] + shift_ref[1:2]
        low = second.astype(BF)
        low_s[...] = low
        lowt_s[...] = low.T
        acc_s[...] = second + bout_ref[...]

    @pl.when(phase == 0)
    def _():
        weights_in, weights_out, count = win_ref[0], wout(), low_s.shape[0] // 4
        blocks = [slice(i * count, (i + 1) * count) for i in range(4)]
        pres = [dot(low_s[block, :], weights_in) + bin_ref[...] for block in blocks]
        both = [gelu_parts(pre) for pre in pres]
        for block, (hidden, slope) in zip(blocks, both):
            hidden = hidden.astype(BF)
            hid_s[chunk, block] = hidden
            slope_s[chunk, block] = slope
            acc_s[block, :] += dot(hidden, weights_out)

    @pl.when((phase == 1) & (chunk == 0))
    def _():
        unit, rstd = norm_parts(acc_s[...])
        mixed_ref[...] = (unit * gain_ref[2:3] + shift_ref[2:3]).astype(BF)
        third, dgain, dshift = norm_back(unit, rstd, gain_ref[2:3], cot_ref[...].astype(F32))
        z = third.astype(BF)
        z_s[...] = z
        acc_s[...] = third
        small_ref[...] = place_rows([dgain, dshift, col_sum(z.astype(F32))], 8)

    @pl.when((phase == 1) & (chunk >= 2))
    def _():
        for copy in sends(slot, chunk - 2):
            copy.wait()

    @pl.when(phase == 1)
    def _():
        z = z_s[...]
        pre_grad = (dot_nt(z, wout()) * slope_s[chunk]).astype(BF)
        dbin_ref[...] = col_sum(pre_grad.astype(F32))
        dout = dot(hid_s[chunk].T, z)
        if own:
            groups = dout.reshape(width // (parts * own), parts, own, d)
            for part in range(parts):
                dout_s[slot, part] = groups[:, part].reshape(width // parts, d).astype(BF)
        else:
            dout_s[slot] = dout.reshape(dout_s.shape[1:]).astype(BF)
        din_s[slot] = dot(lowt_s[...], pre_grad).astype(BF)
        for copy in sends(slot, chunk):
            copy.start()
        acc_s[...] += dot_nt(pre_grad, win_ref[0])

    @pl.when((phase == 1) & (chunk == last))
    def _():
        unit, rstd = norm_parts(ss_ref[...])
        grad, dgain, dshift = norm_back(unit, rstd, gain_ref[1:2], acc_s[...])
        ssg_ref[...] = grad
        small_ref[3:5] = jnp.concatenate([dgain, dshift], axis=0)
        for copy in sends(1 - slot, chunk - 1) + sends(slot, chunk):
            copy.wait()


def cross_back_kernel(
    ssg_ref, fs_ref, q_ref, k_ref, v_ref, ot_ref, lse_ref, wo_ref, w_ref, gain_ref, kmark_ref, qmark_ref, *refs
):
    fsg_ref, dq_ref, dk_ref, dv_ref, small_ref, qt_s, kt_s, do_s, dot_s, dqt_s = refs[-10:]
    upstream = ssg_ref[...]
    branch = upstream.astype(BF)
    mixed_grad = dot_nt(branch, wo_ref[0]).astype(BF)
    do_s[...] = mixed_grad
    dot_s[...] = mixed_grad.T
    qt_s[...] = q_ref[...].T
    kt_s[...] = k_ref[...].T
    attend_back_block(
        q_ref, k_ref, v_ref, qt_s, kt_s, ot_ref, do_s, dot_s, kmark_ref, qmark_ref, lse_ref, dqt_s, dk_ref, dv_ref
    )
    dq = dqt_s[...].T
    dq_ref[...] = dq
    first_grad = upstream + dot_nt(dq, w_ref[0])
    unit, rstd = norm_parts(fs_ref[...])
    grad, dgain, dshift = norm_back(unit, rstd, gain_ref[0:1], first_grad)
    fsg_ref[...] = grad
    sums = [col_sum(dq.astype(F32)), col_sum(dv_ref[...].astype(F32)), col_sum(branch.astype(F32)), dgain, dshift]
    small_ref[...] = place_rows(sums, 8)


def self_back_kernel(fsg_ref, q_ref, k_ref, v_ref, ot_ref, lse_ref, wo_ref, kmark_ref, qmark_ref, *refs):
    dq_ref, dk_ref, dv_ref, small_ref, qt_s, kt_s, do_s, dot_s, dqt_s = refs[-9:]
    branch = fsg_ref[...].astype(BF)
    mixed_grad = dot_nt(branch, wo_ref[0]).astype(BF)
    do_s[...] = mixed_grad
    dot_s[...] = mixed_grad.T
    qt_s[...] = q_ref[...].T
    kt_s[...] = k_ref[...].T
    attend_back_block(
        q_ref, k_ref, v_ref, qt_s, kt_s, ot_ref, do_s, dot_s, kmark_ref, qmark_ref, lse_ref, dqt_s, dk_ref, dv_ref
    )
    dq = dqt_s[...].T
    dq_ref[...] = dq
    sums = [col_sum(dq.astype(F32)), col_sum(dv_ref[...].astype(F32)), col_sum(branch.astype(F32))]
    small_ref[...] = place_rows(sums, 8)


def bring(sources, slots, sems):
    copies = [pltpu.make_async_copy(s, v, sems.at[i]) for i, (s, v) in enumerate(zip(sources, slots))]
    for copy in copies:
        copy.start()

    def get(i):
        copies[i].wait()
        return slots[i][...]

    return get


def lay_out(out_s, at, grads, more=None):
    places = out_s.shape[2] * out_s.shape[3]
    d = out_s.shape[5]
    own = d // (4 * places)
    for quarter in range(4):
        first = quarter * places
        parts = [g[first * own : (first + places) * own].reshape(places, own, d) for g in grads]
        if more is not None:
            parts.append(jnp.stack([more(first + i) for i in range(places)]))
        rows = jnp.concatenate(parts, axis=1).astype(BF)
        count = rows.shape[1]
        out_s[quarter // 2, quarter % 2, :, :, at : at + count] = rows.reshape(*out_s.shape[2:4], count, d)


def hand_out(out_s, me, keep_ref, send_ref, sems):
    moves = []
    for x in range(2):
        moves.append(pltpu.make_async_copy(out_s.at[x, me], keep_ref.at[x], sems.at[2 * x]))
        moves.append(pltpu.make_async_copy(out_s.at[x, 1 - me], send_ref.at[x], sems.at[2 * x + 1]))
    for move in moves:
        move.start()
    return moves


def cross_weight_kernel(staged, me_ref, *refs):
    sources, (keep_ref, send_ref), slots = refs[:9], refs[9:11], refs[11:20]
    out_s, sems, out_sems = refs[20:]
    get = bring(sources, slots, sems)
    memt = get(0).T
    dk = get(1)
    keys = dot(memt, dk)
    dv = get(2)
    values = dot(memt, dv)
    if staged:
        lay_out(out_s, 0, [keys, values])
    else:
        out_s[0], out_s[1] = keys.astype(BF), values.astype(BF)
    outs = [dot(get(3), get(4).astype(BF)), dot(get(5), get(6).astype(BF))]
    if staged:
        lay_out(out_s, 2 * outs[0].shape[0] // 32, outs)
    else:
        out_s[2], out_s[3] = outs[0].astype(BF), outs[1].astype(BF)
    queries = dot(get(7).T, get(8))
    if staged:
        lay_out(out_s, 4 * outs[0].shape[0] // 32, [queries])
        moves = hand_out(out_s, me_ref[0], keep_ref, send_ref, out_sems)
    else:
        out_s[4] = queries.astype(BF)
        send_ref[0] = 0
        moves = [pltpu.make_async_copy(out_s, keep_ref, out_sems.at[0])]
        moves[0].start()
    for move in moves:
        move.wait()


def self_last_kernel(
    staged, me_ref, fsg_ref, q_ref, k_ref, v_ref, ot_ref, lse_ref, wo_ref, kmark_ref, qmark_ref, sums_ref, dbin_ref, x_ref,
    *refs,
):
    (keep_ref, send_ref), outs = refs[3:5], refs[5:8]
    qt_s, kt_s, do_s, dot_s, dqt_s, dq_s, dk_s, dv_s, x_s, out_s, sems, out_sems = refs[8:]
    grads = (dq_s, dk_s, dv_s)
    before = x_s.shape[0] - SEQ_MAX
    mine = pl.ds(before, SEQ_MAX)
    loads = [pltpu.make_async_copy(x_ref, x_s, sems.at[0])]
    if before:
        early = pl.ds(0, before)
        loads += [
            pltpu.make_async_copy(o.at[early], g.at[early], sems.at[1 + i]) for i, (o, g) in enumerate(zip(outs, grads))
        ]
    for load in loads:
        load.start()
    branch = fsg_ref[...].astype(BF)
    mixed_grad = dot_nt(branch, wo_ref[0]).astype(BF)
    do_s[...] = mixed_grad
    dot_s[...] = mixed_grad.T
    qt_s[...] = q_ref[...].T
    kt_s[...] = k_ref[...].T
    attend_back_block(
        q_ref, k_ref, v_ref, qt_s, kt_s, ot_ref, do_s, dot_s, kmark_ref, qmark_ref, lse_ref, dqt_s,
        dk_s.at[mine], dv_s.at[mine],
    )
    dq_s[mine] = dqt_s[...].T
    moves = [
        pltpu.make_async_copy(g.at[mine], o.at[mine], sems.at[4 + i]) for i, (g, o) in enumerate(zip(grads, outs))
    ]
    for load in loads:
        load.wait()
    for move in moves:
        move.start()
    last = [col_sum(dq_s[mine].astype(F32)), col_sum(dv_s[mine].astype(F32)), col_sum(branch.astype(F32))]
    sums = sums_ref[...] + place_rows(last, 16)
    xt = x_s[...].T
    if not staged:
        for i in range(3):
            out_s[i] = dot(xt, grads[i][...]).astype(BF)
        send_ref[...] = sums
        moves.append(pltpu.make_async_copy(out_s, keep_ref, out_sems.at[0]))
        moves[-1].start()
    else:
        d, wide = sums_ref.shape[1], dbin_ref.shape[1]
        lines = jnp.broadcast_to(dbin_ref[...], (8, wide))
        last_row = lax.broadcasted_iota(jnp.int32, (16, d), 0) == 15

        def small(device):
            rows, line = sums, lines
            if device:
                rows = pltpu.roll(rows, d - d // 32 * device, 1)
                line = pltpu.roll(lines, wide - wide // 32 * device, 1)
            line = line[:, :d]
            return jnp.where(last_row, jnp.concatenate([line, line], axis=0), rows)

        lay_out(out_s, 0, [dot(xt, dq_s[...]), dot(xt, dk_s[...])])
        lay_out(out_s, 2 * d // 32, [dot(xt, dv_s[...])], small)
        moves += hand_out(out_s, me_ref[0], keep_ref, send_ref, out_sems)
    for move in moves:
        move.wait()


def memory_input_kernel(dk_ref, dv_ref, wk_ref, wv_ref, mg_ref):
    mg_ref[...] = dot_nt(dk_ref[...], wk_ref[0]) + dot_nt(dv_ref[...], wv_ref[0])


def self_input_kernel(fsg_ref, dq_ref, dk_ref, dv_ref, wqk_ref, wv_ref, qg_ref):
    qg_ref[...] = (
        fsg_ref[...]
        + dot_nt(dq_ref[...], wqk_ref[0]) + dot_nt(dk_ref[...], wqk_ref[1]) + dot_nt(dv_ref[...], wv_ref[0])
    )


def pick(first, second, other):
    return jnp.where(other == 0, first, second)


def first_stage_kernel(me_ref, keep_ref, got_ref, sl_ref, kl_ref, sr_ref, kr_ref):
    total = keep_ref[...].astype(F32) + got_ref[...].astype(F32)
    half = total.shape[4] // 2
    left, right = total[..., :half], total[..., half:]
    sl_ref[...] = pick(left[1], left[0], me_ref[0]).astype(BF)
    kl_ref[...] = pick(left[0], left[1], me_ref[0]).astype(BF)
    sr_ref[...] = pick(right[:, :, 1], right[:, :, 0], me_ref[1]).astype(BF)
    kr_ref[...] = pick(right[:, :, 0], right[:, :, 1], me_ref[1]).astype(BF)


def second_stage_kernel(me_ref, kl_ref, gl_ref, kr_ref, gr_ref, sl_ref, ml_ref, sr_ref, mr_ref):
    left = kl_ref[...].astype(F32) + gl_ref[...].astype(F32)
    right = kr_ref[...].astype(F32) + gr_ref[...].astype(F32)
    sl_ref[...] = pick(left[:, 1], left[:, 0], me_ref[1]).astype(BF)
    ml_ref[...] = pick(left[:, 0], left[:, 1], me_ref[1]).astype(BF)
    sr_ref[...] = pick(right[1], right[0], me_ref[0]).astype(BF)
    mr_ref[...] = pick(right[0], right[1], me_ref[0]).astype(BF)


def third_stage_kernel(me_ref, kl_ref, gl_ref, kr_ref, gr_ref, own_ref, *outs):
    total = jnp.concatenate(
        [kl_ref[...].astype(F32) + gl_ref[...].astype(F32), kr_ref[...].astype(F32) + gr_ref[...].astype(F32)], axis=2
    )
    me = me_ref[2]
    for step, ref in enumerate((own_ref, *outs)):
        index = (me + step) % 4
        value = jnp.where(
            index < 2, jnp.where(index == 0, total[0], total[1]), jnp.where(index == 2, total[2], total[3])
        )
        ref[...] = value.astype(ref.dtype)


def final_stage_kernel(own, *refs):
    cross_refs, self_refs, outs = refs[:4], refs[4:8], refs[8:]
    proj_ref, out_ref, bias_ref, gain_ref, shift_ref, hidden_ref, last_ref = outs
    cross = functools.reduce(jnp.add, [r[...].astype(F32) for r in cross_refs])
    selfs = functools.reduce(jnp.add, [r[...].astype(F32) for r in self_refs])
    for i in range(3):
        proj_ref[i] = selfs[i * own : (i + 1) * own]
    for ref, index, at in ((proj_ref, 4, 0), (proj_ref, 5, 1), (out_ref, 1, 2), (out_ref, 0, 3), (proj_ref, 3, 4)):
        ref[index] = cross[at * own : (at + 1) * own]
    sums = selfs[3 * own : 3 * own + 16, :128]
    bias_ref[...] = sums[0:6, :own]
    for ref, lines in ((gain_ref, (6, 11, 8)), (shift_ref, (7, 12, 9))):
        for i, line in enumerate(lines):
            ref[i : i + 1] = sums[line : line + 1, :own]
    hidden_ref[...] = sums[15:16, : hidden_ref.shape[1]]
    last_ref[...] = sums[10:11, :own]


def stage_call(kernel, me, args, outs, name):
    data = sum(a.size * a.dtype.itemsize for a in args)
    return pl.pallas_call(
        kernel,
        in_specs=[pl.BlockSpec(memory_space=pltpu.SMEM)] + [pl.BlockSpec(memory_space=pltpu.VMEM)] * len(args),
        out_specs=[pl.BlockSpec(memory_space=pltpu.VMEM)] * len(outs),
        out_shape=outs,
        compiler_params=pltpu.CompilerParams(vmem_limit_bytes=VMEM_LIMIT),
        cost_estimate=cost(data, 2 * data),
        name=name,
    )(me, *args)


def first_stage(me, keep, got):
    x, z, y, rows, d = keep.shape
    line = lambda *lead: pl.BlockSpec((*lead, rows, d // 2), lambda i: (i, 0, 0, 0))
    both = pl.BlockSpec((x, 1, y, rows, d), lambda i: (0, i, 0, 0, 0))
    side = pl.BlockSpec((x, 1, rows, d // 2), lambda i: (0, i, 0, 0))
    left, right = shape((z, y, rows, d // 2), BF), shape((x, z, rows, d // 2), BF)
    return pl.pallas_call(
        first_stage_kernel,
        grid=(z,),
        in_specs=[pl.BlockSpec(memory_space=pltpu.SMEM), both, both],
        out_specs=[line(1, y), line(1, y), side, side],
        out_shape=[left, left, right, right],
        compiler_params=params(("arbitrary",)),
        cost_estimate=cost(keep.size, 6 * keep.size),
        name="first_stage",
    )(me, keep, got)


def row_block(width):
    return pl.BlockSpec((SEQ_MAX, width), lambda b: (b, 0))


def fine_block(width):
    return pl.BlockSpec((FINE, width), lambda b: (b, 0))


def col_block(height):
    return pl.BlockSpec((height, SEQ_MAX), lambda b: (0, b))


def lead_block(rows):
    return pl.BlockSpec((1, rows, SEQ_MAX), lambda b: (b, 0, 0))


def whole(array, **kw):
    zeros = (0,) * array.ndim
    return pl.BlockSpec(array.shape, lambda *_: zeros, pipeline_mode=pl.Buffered(1))


def planes(array, start, count):
    return pl.BlockSpec(
        (count, *array.shape[1:]), lambda *_: (start // count, 0, 0), pipeline_mode=pl.Buffered(1)
    )


def params(semantics):
    return pltpu.CompilerParams(vmem_limit_bytes=VMEM_LIMIT, dimension_semantics=semantics)


def cost(flops, data, exps=0):
    return pl.CostEstimate(flops=int(flops), bytes_accessed=int(data), transcendentals=int(exps))


def shape(dims, kind):
    return jax.ShapeDtypeStruct(dims, kind)


def self_forward(x, wqk, wv, bias, kmark, qmark):
    rows, d = x.shape
    blocks = rows // SEQ_MAX
    act = shape((rows, d), BF)
    return pl.pallas_call(
        self_forward_kernel,
        grid=(blocks,),
        in_specs=[row_block(d), whole(wqk), whole(wv), whole(bias), row_block(128), lead_block(HEAD_DIM)],
        out_specs=[row_block(d), row_block(d), row_block(d), col_block(d), lead_block(16)],
        out_shape=[act, act, act, shape((d, rows), BF), shape((blocks, 16, SEQ_MAX), F32)],
        scratch_shapes=[pltpu.VMEM((d, SEQ_MAX), BF)] * 2,
        compiler_params=params(("arbitrary",)),
        cost_estimate=cost(20e9, 12e6),
        name="self_forward",
    )(x, wqk, wv, bias, kmark, qmark)


def cross_forward(x, mem, sot, wo, wo_at, w, bias, gain, shift, kmark, qmark):
    rows, d = x.shape
    blocks = rows // SEQ_MAX
    act, wide = shape((rows, d), BF), shape((rows, d), F32)
    return pl.pallas_call(
        cross_forward_kernel,
        grid=(blocks,),
        in_specs=[
            row_block(d), row_block(d), col_block(d), planes(wo, wo_at, 2), planes(w, 0, 3), whole(bias), whole(gain),
            whole(shift),
            row_block(128), lead_block(HEAD_DIM),
        ],
        out_specs=[row_block(d)] * 5 + [col_block(d), lead_block(16), row_block(d)],
        out_shape=[wide, act, act, act, act, shape((d, rows), BF), shape((blocks, 16, SEQ_MAX), F32), wide],
        scratch_shapes=[pltpu.VMEM((d, SEQ_MAX), BF)] * 2,
        compiler_params=params(("arbitrary",)),
        cost_estimate=cost(24e9, 20e6),
        name="cross_forward",
    )(x, mem, sot, wo, w, bias, gain, shift, kmark, qmark)


def feed(second_sum, cot, win, bin_, wout, bout, gain, shift):
    rows, d = second_sum.shape
    width = win.shape[2]
    ff = bin_.shape[1]
    chunks = ff // width
    own = wout.shape[2] if wout.ndim == 4 else 0
    fixed = lambda p, j: (0, 0)
    parts = chunks if own else 1
    if own:
        wout_spec = pl.BlockSpec((parts, width // (parts * own), own, d), lambda p, j: (1, j, 0, 0))
    else:
        wout_spec = pl.BlockSpec((width, d), lambda p, j: (j, 0))
    return pl.pallas_call(
        functools.partial(feed_kernel, own),
        grid=(2, chunks),
        in_specs=[
            whole(second_sum), whole(cot),
            pl.BlockSpec((1, d, width), lambda p, j: (jnp.where(j == 0, 3, 7 + j) if own else j, 0, 0)),
            pl.BlockSpec((1, width), lambda p, j: (0, j)),
            wout_spec, whole(bout), whole(gain), whole(shift),
        ],
        out_specs=[
            pl.BlockSpec((rows, d), fixed),
            pl.BlockSpec((rows, d), fixed),
            pl.BlockSpec(memory_space=pl.ANY),
            pl.BlockSpec((1, width), lambda p, j: (0, j * p)),
            pl.BlockSpec((8, d), fixed),
        ],
        out_shape=[
            shape((rows, d), BF), shape((rows, d), F32), shape((d, 2 * ff), BF),
            shape((1, ff), F32), shape((8, d), F32),
        ],
        scratch_shapes=[
            pltpu.VMEM((rows, d), BF), pltpu.VMEM((d, rows), BF),
            pltpu.VMEM((chunks, rows, width), BF), pltpu.VMEM((chunks, rows, width), F32),
            pltpu.VMEM((rows, d), F32), pltpu.VMEM((rows, d), BF),
            pltpu.VMEM((2, d, width), BF), pltpu.VMEM((2, parts, width // parts, d), BF),
            pltpu.SemaphoreType.DMA((1 + parts, 2)),
        ],
        compiler_params=params(("arbitrary", "arbitrary")),
        cost_estimate=cost(40e9, 40e6),
        name="feed",
    )(second_sum, cot, win, bin_, wout, bout, gain, shift)


def back_scratch(d):
    return (
        [pltpu.VMEM((d, SEQ_MAX), BF)] * 2 + [pltpu.VMEM((SEQ_MAX, d), BF)] + [pltpu.VMEM((d, SEQ_MAX), BF)] * 2
    )


def at_row(block, width):
    return pl.BlockSpec((SEQ_MAX, width), lambda b: (block, 0))


def at_col(block, height):
    return pl.BlockSpec((height, SEQ_MAX), lambda b: (0, block))


def at_lead(block, rows):
    return pl.BlockSpec((1, rows, SEQ_MAX), lambda b: (block, 0, 0))


def one_back(kernel, block, before, args, specs, outs, name):
    d = outs[0].shape[1]
    kept = [pl.BlockSpec(memory_space=pl.ANY)] * len(before)
    return pl.pallas_call(
        kernel,
        grid=(1,),
        in_specs=specs + kept,
        out_specs=[at_row(block, d)] * len(outs) + [pl.BlockSpec((8, d), lambda b: (0, 0))],
        out_shape=outs + [shape((8, d), F32)],
        scratch_shapes=back_scratch(d),
        input_output_aliases={len(args) + i: i for i in range(len(before))},
        compiler_params=params(("arbitrary",)),
        cost_estimate=cost(25e9, 15e6),
        name=name,
    )(*args, *before)


def cross_back(block, before, wo_at, ssg, first_sum, q, k, v, ot, lse, wo, w, gain, kmark, qmark):
    rows, d = first_sum.shape
    act = shape((rows, d), BF)
    specs = [at_row(block, d)] * 5 + [
        at_col(block, d), at_lead(block, 16), planes(wo, wo_at + 1, 1), planes(w, 0, 1), whole(gain), at_row(block, 128), at_lead(block, HEAD_DIM),
    ]
    args = (ssg, first_sum, q, k, v, ot, lse, wo, w, gain, kmark, qmark)
    return one_back(
        cross_back_kernel, block, before, args, specs, [shape((rows, d), F32), act, act, act], f"cross_back_{block}"
    )


def self_back(block, before, wo_at, fsg, q, k, v, ot, lse, wo, kmark, qmark):
    rows, d = fsg.shape
    act = shape((rows, d), BF)
    specs = [at_row(block, d)] * 4 + [
        at_col(block, d), at_lead(block, 16), planes(wo, wo_at, 1), at_row(block, 128), at_lead(block, HEAD_DIM),
    ]
    args = (fsg, q, k, v, ot, lse, wo, kmark, qmark)
    return one_back(self_back_kernel, block, before, args, specs, [act, act, act], f"self_back_{block}")


def weight_outs(staged, count, extra, devices, d):
    if not staged:
        return [shape((count, d, d), BF), shape((1,), jnp.int32)], pltpu.VMEM((count, d, d), BF)
    rows = count * d // devices + extra
    half = shape((2, 4, 2, rows, d), BF)
    return [half, half], pltpu.VMEM((2, 2, 4, 2, rows, d), BF)


def cross_weight(staged, me, devices, dq, dk, dv, low, mem, ot, ssg, sot, fsg):
    rows, d = dq.shape
    args = (mem, dk, dv, ot, ssg, sot, fsg, low, dq)
    anywhere = pl.BlockSpec(memory_space=pl.ANY)
    outs, scratch = weight_outs(staged, 5, 0, devices, d)
    last = anywhere if staged else pl.BlockSpec(memory_space=pltpu.SMEM)
    return pl.pallas_call(
        functools.partial(cross_weight_kernel, staged),
        in_specs=[pl.BlockSpec(memory_space=pltpu.SMEM)] + [anywhere] * 9,
        out_specs=[anywhere, last],
        out_shape=outs,
        scratch_shapes=[pltpu.VMEM(a.shape, a.dtype) for a in args] + [
            scratch, pltpu.SemaphoreType.DMA((9,)), pltpu.SemaphoreType.DMA((4,)),
        ],
        compiler_params=pltpu.CompilerParams(vmem_limit_bytes=VMEM_LIMIT),
        cost_estimate=cost(9e9, 20e6),
        name="cross_weight",
    )(me, *args)


def self_last(staged, me, devices, block, before, wo_at, fsg, q, k, v, ot, lse, wo, kmark, qmark, sums, dbin, x):
    rows, d = x.shape
    anywhere, here = pl.BlockSpec(memory_space=pl.ANY), pl.BlockSpec(memory_space=pltpu.VMEM)
    outs, scratch = weight_outs(staged, 3, 16, devices, d)
    act = shape((rows, d), BF)
    args = (me, fsg, q, k, v, ot, lse, wo, kmark, qmark, sums, dbin, x)
    if not before:
        before = [jnp.zeros((rows, d), BF)] * 3
    fixed = lambda array: pl.BlockSpec(array.shape, lambda b: (0,) * array.ndim)
    if not staged:
        outs[1] = shape((16, d), F32)
    return pl.pallas_call(
        functools.partial(self_last_kernel, staged),
        grid=(1,),
        in_specs=[pl.BlockSpec(memory_space=pltpu.SMEM)] + [at_row(block, d)] * 4 + [
            at_col(block, d), at_lead(block, 16), planes(wo, wo_at, 1), at_row(block, 128), at_lead(block, HEAD_DIM),
            fixed(sums), fixed(dbin), anywhere,
        ] + [anywhere] * 3,
        out_specs=[anywhere, anywhere if staged else fixed(outs[1])] + [anywhere] * 3,
        out_shape=outs + [act] * 3,
        scratch_shapes=back_scratch(d) + [pltpu.VMEM((rows, d), BF)] * 4 + [
            scratch, pltpu.SemaphoreType.DMA((7,)), pltpu.SemaphoreType.DMA((4,)),
        ],
        input_output_aliases={len(args) + i: 2 + i for i in range(3)},
        compiler_params=params(("arbitrary",)),
        cost_estimate=cost(25e9, 20e6),
        name="self_last",
    )(*args, *before)


def memory_input(dk, dv, w):
    rows, d = dk.shape
    return pl.pallas_call(
        memory_input_kernel,
        grid=(rows // FINE,),
        in_specs=[fine_block(d)] * 2 + [planes(w, 1, 1), planes(w, 2, 1)],
        out_specs=fine_block(d),
        out_shape=shape((rows, d), F32),
        compiler_params=params(("arbitrary",)),
        cost_estimate=cost(3e9, 9e6),
        name="memory_input",
    )(dk, dv, w, w)


def self_input(fsg, dq, dk, dv, wqk, wv):
    rows, d = fsg.shape
    return pl.pallas_call(
        self_input_kernel,
        grid=(rows // FINE,),
        in_specs=[fine_block(d)] * 4 + [whole(wqk), whole(wv)],
        out_specs=fine_block(d),
        out_shape=shape((rows, d), F32),
        compiler_params=params(("arbitrary",)),
        cost_estimate=cost(4e9, 14e6),
        name="self_input",
    )(fsg, dq, dk, dv, wqk, wv)


def key_marks(seg):
    odd = (seg & 1)[:, None]
    lane = lax.broadcasted_iota(jnp.int32, (seg.shape[0], 128), 1) % HEAD_DIM
    return jnp.where(lane == 0, 1 - odd, jnp.where(lane == 1, odd, 0)).astype(BF)


def query_marks(seg):
    odd = (seg & 1).reshape(-1, 1, SEQ_MAX)
    row = lax.broadcasted_iota(jnp.int32, (odd.shape[0], HEAD_DIM, SEQ_MAX), 1)
    return jnp.where(row == 0, odd, jnp.where(row == 1, 1 - odd, 0)).astype(BF) * (-MASKED)


def swap(value, name):
    return lax.ppermute(value, name, [(0, 1), (1, 0)])


class Halving:
    def __init__(self, me, keep, send):
        self.me, self.keep, self.out = me, [keep], [send]

    def core(self):
        got = swap(self.out[0], "c")
        sl, kl, sr, kr = first_stage(self.me, self.keep[0], got)
        self.keep, self.out = [kl, kr], [sl, sr]

    def first(self):
        (kl, kr), (sl, sr) = self.keep, self.out
        gl, gr = swap(sl, "x"), swap(sr, "y")
        z, _, rows, half = kl.shape
        piece = shape((z, rows, half), BF)
        sl, ml, sr, mr = stage_call(second_stage_kernel, self.me, (kl, gl, kr, gr), [piece] * 4, "second_stage")
        self.keep, self.out = [ml, mr], [sl, sr]

    def second(self):
        (kl, kr), (sl, sr) = self.keep, self.out
        gl, gr = swap(sl, "y"), swap(sr, "x")
        _, rows, half = kl.shape
        piece = (rows, 2 * half)
        outs = [shape(piece, F32)] + [shape(piece, BF)] * 3
        own, *self.out = stage_call(third_stage_kernel, self.me, (kl, gl, kr, gr), outs, "third_stage")
        self.keep = [own]

    def last(self):
        steps = zip(range(1, 4), self.out)
        return self.keep + [lax.ppermute(out, "z", [(i, (i + step) % 4) for i in range(4)]) for step, out in steps]

    @staticmethod
    def finish(cross, selfs, small, dbin, own, devices):
        d = cross[0].shape[1]
        wide = dbin.shape[1] // devices
        outs = [
            shape(dims, F32)
            for dims in ((6, own, d), (2, own, d), (6, own), (3, own), (3, own), (1, wide), (1, own))
        ]
        args = cross + selfs
        proj, out, bias, gain, shift, hidden, last = pl.pallas_call(
            functools.partial(final_stage_kernel, own),
            in_specs=[pl.BlockSpec(memory_space=pltpu.VMEM)] * 8,
            out_specs=[pl.BlockSpec(memory_space=pltpu.VMEM)] * 7,
            out_shape=outs,
            compiler_params=pltpu.CompilerParams(vmem_limit_bytes=VMEM_LIMIT),
            cost_estimate=cost(2e6, 3e6),
            name="final_stage",
        )(*args)
        return proj, out, bias, gain, shift, hidden.reshape(-1), last.reshape(-1)

    @staticmethod
    def feed(grads, own):
        sums = lax.psum_scatter(grads, ("x", "c", "z", "y"), scatter_dimension=0, tiled=True).astype(F32)
        half = sums.shape[1] // 2
        d = grads.shape[0]
        return sums[:, :half], sums[:, half:].reshape(own, -1, d).swapaxes(0, 1).reshape(-1, d)


class Whole:
    def __init__(self, me, grads, _):
        self.grads, self.out, self.keep = grads, (), ()

    def core(self):
        pass

    first = second = core

    def last(self):
        sums = lax.psum_scatter(self.grads, ("dp", "fsdp"), scatter_dimension=1, tiled=True).astype(F32)
        return sums.reshape(-1, sums.shape[2])

    @staticmethod
    def finish(cross, selfs, small, dbin, own, devices):
        sum_up = functools.partial(lax.psum_scatter, axis_name=("dp", "fsdp"), scatter_dimension=1, tiled=True)
        small, dbin = sum_up(small), sum_up(dbin)[0]
        cross, selfs = cross.reshape(5, own, -1), selfs.reshape(3, own, -1)
        proj = jnp.concatenate([selfs, cross[4:], cross[:2]])
        gain, shift = jnp.stack([small[6], small[11], small[8]]), jnp.stack([small[7], small[12], small[9]])
        return proj, cross[3:1:-1], small[0:6], gain, shift, dbin, small[10]

    @staticmethod
    def feed(grads, own):
        sum_up = functools.partial(lax.psum_scatter, axis_name=("dp", "fsdp"), scatter_dimension=0, tiled=True)
        half, d = grads.shape[1] // 2, grads.shape[0]
        dwin = sum_up(grads[:, :half]).astype(F32)
        return dwin, sum_up(grads[:, half:].reshape(d, -1, d).swapaxes(0, 1).reshape(-1, d)).astype(F32)


def after(value, *sums):
    value, outs = lax.optimization_barrier((value, [s.out for s in sums]))
    for s, s.out in zip(sums, outs):
        pass
    return value


def hold(sums, value):
    sums.keep = lax.optimization_barrier((sums.keep, value))[0]


def take_turns(value):
    me = lax.axis_index("z")
    parts = [value]
    for step in range(3, 0, -1):
        parts.append(lax.ppermute(value, "z", [(i, (i + step) % 4) for i in range(4)]))
    return jnp.stack([lax.select_n((j - me) % 4, *parts) for j in range(4)], axis=1)


def take_pair(value, name, axis):
    me = lax.axis_index(name)
    got = lax.ppermute(value, name, [(0, 1), (1, 0)])
    return jnp.stack([jnp.where(me == 0, value, got), jnp.where(me == 0, got, value)], axis=axis)


class Doubling:
    def __init__(self, left, right):
        self.cut, self.rows = left.shape[0], left.shape[1]
        self.flat = left.shape[1:] != right.shape[1:]
        if self.flat:
            left, right = (a.reshape(1, -1, a.shape[2]) for a in (left, right))
            self.out = [jnp.concatenate([left, right], axis=1)]
            self.split = left.shape[1]
        else:
            self.out = [jnp.concatenate([left, right])]

    def line(self):
        both = take_turns(self.out[0])
        if self.flat:
            d = both.shape[3]
            left = both[0, :, : self.split].reshape(4, self.cut, self.rows, d).swapaxes(0, 1)
            self.out = [left, both[:, :, self.split :]]
        else:
            self.out = [both[: self.cut], both[self.cut :]]

    def first(self):
        self.out = [take_pair(self.out[0], "y", 2), take_pair(self.out[1], "x", 1)]

    def second(self):
        self.out = [take_pair(self.out[0], "x", 1), take_pair(self.out[1], "y", 3)]

    def core(self):
        self.out = [take_pair(self.out[0], "c", 2), take_pair(self.out[1], "c", 2)]
        return self.out


def local_small(bias, gain, shift, bin_, bout):
    return jnp.concatenate([a.reshape(-1) for a in (bias, gain, shift, bout, bin_)])


def spread_small(parts, own):
    parts = parts.astype(F32)
    devices = parts.shape[0]
    rows = parts[:, : 13 * own].reshape(devices, 13, own).swapaxes(0, 1).reshape(13, -1)
    bin_ = parts[:, 13 * own :].reshape(1, -1)
    return {"bias": rows[0:6], "gain": rows[6:9], "shift": rows[9:12], "bout": rows[12:13], "bin": bin_}


class Stages:
    out_at = 0

    def __init__(self, proj, out, small, win, wout):
        _, own, d = proj.shape
        panels = win.reshape(own, -1, d).swapaxes(0, 1)
        rest = jnp.concatenate([proj[3:6], panels[:1], wout.reshape(-1, own, d), panels[1:]])
        self.rest = lax.all_gather(rest, ("x", "c", "z", "y"), axis=1)
        extra = jnp.pad(small[None, None], ((0, 0), (0, 7), (0, d - small.shape[0])))
        self.one = Doubling(proj[:2], jnp.concatenate([proj[2:3], extra], axis=1))
        self.two = Doubling(out[:1], out[1:])
        self.own, self.cut, self.d = own, small.shape[0], d

    def begin(self):
        one, own, d = self.one, self.own, self.d
        one.line()
        one.first()
        self.two.out = after(self.two.out, one)
        one.second()
        left, right = one.core()
        full = {"qk": left.reshape(2, -1, d), "v": right[..., :own, :].reshape(1, -1, d)}
        full.update(spread_small(right[..., own, : self.cut].reshape(-1, self.cut), own))
        return full

    def finish(self, value):
        planes = self.rest.reshape(self.rest.shape[0], -1, self.d)
        two = self.two
        two.line()
        two.out, value = lax.optimization_barrier((two.out, value))
        two.first()
        two.second()
        out = jnp.concatenate(two.core()).reshape(2, -1, self.d)
        return {"cross_proj": planes, "out": out, "win": planes, "wout": self.rest}, value


class Plain:
    out_at = 0

    def __init__(self, proj, out, small, win, wout):
        take = functools.partial(lax.all_gather, axis_name=("dp", "fsdp"), tiled=True)
        _, own, d = proj.shape
        proj = take(proj, axis=1)
        self.full = {"qk": proj[:2], "v": proj[2:3]}
        self.full.update(spread_small(take(small[None], axis=0), own))
        win = take(win, axis=0).reshape(d, -1, d).swapaxes(0, 1)
        self.rest = {"cross_proj": proj[3:], "out": take(out, axis=1), "win": win, "wout": take(wout, axis=0)}

    def begin(self):
        return self.full

    def finish(self, value):
        return self.rest, value


def body(
    gather, scatter, devices, query, memory, query_seg, memory_seg, attn_proj, attn_out, attn_bias, norm_gain, norm_bias,
    ffn_in, ffn_in_bias, ffn_out, ffn_out_bias, cotangent,
):
    blocks = range(query.shape[0] // SEQ_MAX)
    own = attn_proj.shape[1]
    d = query.shape[1]
    staged = scatter is Halving
    me, pair = jnp.zeros((3,), jnp.int32), jnp.zeros((1,), jnp.int32)
    if staged:
        me = jnp.stack([lax.axis_index(name) for name in ("x", "y", "z")])
        pair = lax.axis_index("c").reshape(1)
    small = local_small(attn_bias, norm_gain, norm_bias, ffn_in_bias, ffn_out_bias)
    weights = gather(attn_proj, attn_out, small, ffn_in, ffn_out)
    full = weights.begin()
    bias, gain, shift = full["bias"], full["gain"], full["shift"]
    qmark = query_marks(query_seg)
    smark, cmark = key_marks(query_seg), key_marks(memory_seg)
    sq, sk, sv, sot, slse = self_forward(query, full["qk"], full["v"], bias, smark, qmark)
    (rest, sot), out_at = weights.finish(sot), weights.out_at
    out, cross_proj = rest["out"], rest["cross_proj"]
    first_sum, low, cq, ck, cv, cot_, clse, second_sum = cross_forward(
        query, memory, sot, out, out_at, cross_proj, bias, gain, shift, cmark, qmark
    )
    mixed, ssg, fdw, dbin, small3 = feed(
        second_sum, cotangent, rest["win"], full["bin"], rest["wout"], full["bout"], gain, shift
    )
    dwin, dwout = scatter.feed(fdw, own)
    grads, small2 = [], 0
    for block in blocks:
        *grads, part = cross_back(
            block, grads, out_at, ssg, first_sum, cq, ck, cv, cot_, clse, out, cross_proj, gain, cmark, qmark
        )
        small2 = small2 + part
    fsg, dq, dk, dv = grads
    keep, send = cross_weight(staged, pair, devices, dq, dk, dv, low, memory, cot_, ssg, sot, fsg)
    cross_sum = scatter(me, keep, send)
    dk = after(dk, cross_sum)
    memory_grad = memory_input(dk, dv, cross_proj)
    cross_sum.core()
    upstream, memory_grad = after((fsg, memory_grad), cross_sum)
    grads = []
    small1 = jnp.zeros((8, d), F32)
    for block in blocks[:-1]:
        *grads, part = self_back(block, grads, out_at, upstream, sq, sk, sv, sot, slse, out, smark, qmark)
        small1 = small1 + part
    cross_sum.first()
    upstream = after(upstream, cross_sum)
    sums = jnp.concatenate([small1[:3], small2[:5], small3[:5], jnp.zeros((3, d), F32)])
    keep, send, dq, dk, dv = self_last(
        staged, pair, devices, blocks[-1], grads, out_at, upstream, sq, sk, sv, sot, slse, out, smark, qmark, sums, dbin,
        query,
    )
    self_sum = scatter(me, keep, send)
    cross_sum.second()
    self_sum.out = after(self_sum.out, cross_sum)
    self_sum.core()
    upstream = after(fsg, self_sum, cross_sum)
    query_grad = self_input(upstream, dq, dk, dv, full["qk"], full["v"])
    cross = cross_sum.last()
    hold(self_sum, query_grad)
    self_sum.first()
    hold(self_sum, cross)
    self_sum.second()
    selfs, dwin, dwout = lax.optimization_barrier((self_sum.last(), dwin, dwout))
    proj_g, out_g, bias_g, gain_g, shift_g, dbin_g, dbout_g = scatter.finish(cross, selfs, send, dbin, own, devices)
    return (
        mixed, query_grad, memory_grad, proj_g, out_g, bias_g, gain_g, shift_g, dwin, dbin_g, dwout, dbout_g,
    )


def solution(mesh):
    devices = mesh.size
    if dict(mesh.shape) == {"dp": 4, "fsdp": 8}:
        axes = ("x", "c", "z", "y")
        mesh = Mesh(mesh.devices.reshape(2, 2, 4, 2), axes)
        gather, scatter = Stages, Halving
    else:
        axes = ("dp", "fsdp")
        gather, scatter = Plain, Whole
    rows, mid, flat, row1 = P(axes, None), P(None, axes, None), P(None, axes), P(axes)
    return jax.shard_map(
        functools.partial(body, gather, scatter, devices),
        mesh=mesh,
        in_specs=(rows, rows, row1, row1, mid, mid, flat, flat, flat, rows, row1, rows, row1, rows),
        out_specs=(rows, rows, rows, mid, mid, flat, flat, flat, rows, row1, rows, row1),
        check_vma=False,
    )
```
